32 devices in a mesh: wide: 8 (over z, x), narrow: 4 (over y, core).
Axes of the slice: x: 2, y: 2, z: 4, core: 2. Of those that a mesh axis runs over, the one named last changes fastest.
Arguments:
- records: bfloat16 [8, 512, 12288], P(None, 'narrow', 'wide'), may hold values from -6 to 6
- taps: float32 [201], replicated, may hold values from -0.4375 to 0.4375
- pair_sources: int32 [8, 4], replicated, may hold values from 0 to 7, as said below
- pair_counts: int32 [8], P('wide'), may hold values from 1 to 4, as said below
Outputs:
- correlations: bfloat16 [8, 4, 512, 32, 256], P('wide', None, 'narrow')
The draws below stay inside these ranges and needn't reach their ends.
Inputs may be any that keep to these rules, and one draw needn't show every extreme that they name: `pair_sources`: each row lists 4 different blocks; only the first pair_counts[r] of row r are paired with r. `pair_counts`: some block has 4 pairs in every draw.
All inputs are finite; a program needn't handle non-finite values.
Results may differ from the reference program's by a relative error of at most 0.0096.
Values may be sent and summed in bfloat16 or wider, within the bound.
No kernel may reach another device: no remote copies, remote signals or barrier semaphores. Data moves between devices by JAX's collectives and lax.ppermute only.
A program may use at most 128 MiB of HBM per device.

```python
import math
import jax
import jax.numpy as jnp
from jax import lax

BLOCK_CHANNELS = 512
VIRTUAL_SOURCES = 32
TAPS = 201
WLEN = 512
FREQUENCY_BINS = 128
F_LO = 4
LAG_COUNT = 256
MAX_PAIRED_SRC = 4
BLOCKS = 8
NWIN = 24
TIME = 12288


def draw_pair_sources(key, part):
    key = jax.random.fold_in(key, 11)
    scores = jax.random.randint(key, (BLOCKS, BLOCKS), 0, 1 << 30, dtype=jnp.int32)
    order = jnp.argsort(scores, axis=1, stable=True).astype(jnp.int32)
    return order[:, :MAX_PAIRED_SRC]


def draw_pair_counts(key, part):
    key = jax.random.fold_in(key, 23)
    first, second = jax.random.split(key)
    counts = jax.random.randint(first, (BLOCKS,), 1, MAX_PAIRED_SRC + 1, dtype=jnp.int32)
    fullest = jax.random.randint(second, (), 0, BLOCKS, dtype=jnp.int32)
    return counts.at[fullest].set(MAX_PAIRED_SRC)


def level_of(rng, shape, shards, smallest, largest):
    def one(position, blocks):
        steps = jax.random.uniform(jax.random.fold_in(jax.random.fold_in(rng, 6), position), (blocks,), jnp.float32, smallest / len(shards), largest / len(shards))
        return jnp.repeat(jnp.exp(steps), shape[position] // blocks).reshape((-1,) + (1,) * (len(shape) - position - 1))

    factor_of = one(*shards[0])
    for cut in shards[1:]:
        factor_of = factor_of * one(*cut)
    return factor_of


def normal_values(own_key, extent, spread, bound, shards=(), held_as=jnp.bfloat16):
    result = jax.random.normal(own_key, extent, jnp.float32) * spread
    if len(shards) > 0:
        result = level_of(own_key, extent, shards, -0.22, 0.18) * result
    return jnp.clip(result, min=-bound, max=bound).astype(held_as)


def setup_inputs(seed: int = 0) -> dict:
    keys = jax.random.split(jax.random.key(seed), 5)
    return {
        "records": normal_values(keys[0], (BLOCKS, BLOCK_CHANNELS, TIME), 1.0, 6.0, ((1, 4), (2, 8))),
        "taps": normal_values(keys[1], (TAPS,), TAPS ** -0.5, 0.4375, (), jnp.float32),
        "pair_sources": draw_pair_sources(jax.random.fold_in(keys[4], 71), 0),
        "pair_counts": draw_pair_counts(jax.random.fold_in(keys[4], 71), 0),
    }


def taps_matrix(taps):
    kernel = taps.astype(jnp.bfloat16)
    span = WLEN + TAPS - 1
    padded = jnp.concatenate([kernel[::-1], jnp.zeros((WLEN,), kernel.dtype)])
    tiled = jnp.tile(padded, WLEN)[:WLEN * span].reshape(WLEN, span)
    return tiled.T

def dft_table():
    times = jnp.arange(WLEN, dtype=jnp.int32)[:, None]
    bins = (F_LO + jnp.arange(FREQUENCY_BINS, dtype=jnp.int32))[None, :]
    phase = jnp.mod(times * bins, WLEN)
    angle = phase.astype(jnp.float32) * (2.0 * math.pi / WLEN)
    scale = 1.0 / math.sqrt(WLEN)
    return jnp.concatenate([jnp.cos(angle) * scale, -jnp.sin(angle) * scale], 1).astype(jnp.bfloat16)

def lag_table():
    bins = (F_LO + jnp.arange(FREQUENCY_BINS, dtype=jnp.int32))[:, None]
    lags = (jnp.arange(LAG_COUNT, dtype=jnp.int32) - LAG_COUNT // 2)[None, :]
    phase = jnp.mod(bins * lags, WLEN)
    angle = phase.astype(jnp.float32) * (2.0 * math.pi / WLEN)
    scale = 1.0 / math.sqrt(FREQUENCY_BINS)
    return jnp.concatenate([jnp.cos(angle) * scale, -jnp.sin(angle) * scale], 0).astype(jnp.bfloat16)

def cross_spectra(recv, source_indices, count):
    rec_re = recv[:, :, 0]
    rec_im = recv[:, :, 1]
    src_re = source_indices[:, :, :, 0]
    src_im = source_indices[:, :, :, 1]
    form = 'iwf,kjwf->kijf'
    real = jnp.einsum(form, rec_re, src_re, preferred_element_type=jnp.float32) + jnp.einsum(form, rec_im, src_im, preferred_element_type=jnp.float32)
    imag = jnp.einsum(form, rec_im, src_re, preferred_element_type=jnp.float32) - jnp.einsum(form, rec_re, src_im, preferred_element_type=jnp.float32)
    scale = 1.0 / math.sqrt(recv.shape[1])
    live = (jnp.arange(MAX_PAIRED_SRC, dtype=jnp.int32) < count).astype(jnp.float32)[:, None, None, None]
    return jnp.stack([real * scale * live, imag * scale * live], 3).astype(jnp.bfloat16)

def reference(records, taps, pair_sources, pair_counts):
    toeplitz = taps_matrix(taps)
    forward = dft_table()
    backward = lag_table()

    def block_spectra(block):
        main = block.reshape(BLOCK_CHANNELS, NWIN, WLEN)
        tails = main[:, :, WLEN - (TAPS - 1):]
        previous = jnp.concatenate([jnp.zeros((BLOCK_CHANNELS, 1, TAPS - 1), block.dtype), tails[:, :NWIN - 1]], 1)
        windows = jnp.concatenate([previous, main], 2)
        whitened = jnp.dot(windows, toeplitz, preferred_element_type=jnp.float32).astype(jnp.bfloat16)
        block_spectrum = jnp.dot(whitened, forward, preferred_element_type=jnp.float32).astype(jnp.bfloat16)
        return block_spectrum.reshape(BLOCK_CHANNELS, NWIN, 2, FREQUENCY_BINS)
    block_spectrum = lax.map(block_spectra, records)
    virtual_channels = block_spectrum[:, ::BLOCK_CHANNELS // VIRTUAL_SOURCES]

    def receiver(index):
        recv = block_spectrum[index].astype(jnp.float32)
        source_indices = jnp.take(virtual_channels, pair_sources[index], axis=0).astype(jnp.float32)
        cross = cross_spectra(recv, source_indices, pair_counts[index])
        lag_domain = jnp.dot(cross.reshape(-1, 2 * FREQUENCY_BINS), backward, preferred_element_type=jnp.float32)
        return lag_domain.astype(jnp.bfloat16).reshape(MAX_PAIRED_SRC, BLOCK_CHANNELS, VIRTUAL_SOURCES, LAG_COUNT)
    return lax.map(receiver, jnp.arange(BLOCKS, dtype=jnp.int32))
```

```python
import math

import jax
import jax.numpy as jnp
import numpy as np
from jax import lax
from jax.experimental import pallas as pl
from jax.experimental.pallas import tpu as pltpu
from jax.sharding import PartitionSpec as P

BLOCK_CHANNELS = 512
VIRTUAL_SOURCES = 32
VSTEP = BLOCK_CHANNELS // VIRTUAL_SOURCES
TAPS = 201
WLEN = 512
HALF = 256
BINS = 128
F_LO = 4
LAG_COUNT = 256
SLOTS = 4
BF = jnp.bfloat16
F32 = jnp.float32
MIB = 1 << 20


def dft_table():
    times = np.arange(WLEN, dtype=np.int32)[:, None]
    bins = (F_LO + np.arange(BINS, dtype=np.int32))[None, :]
    angle = np.mod(times * bins, WLEN).astype(np.float32) * np.float32(2.0 * math.pi / WLEN)
    scale = np.float32(1.0 / math.sqrt(WLEN))
    return np.concatenate([np.cos(angle) * scale, -np.sin(angle) * scale], 1).astype(BF).astype(np.float32)


def lag_table():
    bins = (F_LO + np.arange(BINS, dtype=np.int32))[:, None]
    lags = (np.arange(LAG_COUNT, dtype=np.int32) - LAG_COUNT // 2)[None, :]
    angle = np.mod(bins * lags, WLEN).astype(np.float32) * np.float32(2.0 * math.pi / WLEN)
    scale = np.float32(1.0 / math.sqrt(BINS))
    return np.concatenate([np.cos(angle) * scale, -np.sin(angle) * scale], 0).astype(BF).astype(np.float32)


def dot(a, b):
    return lax.dot_general(a, b, (((1,), (0,)), ((), ())), preferred_element_type=F32)


def build_toeplitz(taps_ref, row, toeplitz):
    row[...] = jnp.zeros_like(row)
    row[:, 128 : 128 + TAPS] = jnp.broadcast_to(taps_ref[...].astype(BF).astype(F32), (8, TAPS))
    bands = jnp.broadcast_to(row[0:1, :], (128, 512))
    bands = pltpu.roll(bands, 0, 1, stride=1, stride_axis=0).astype(BF)
    zero = jnp.zeros((128, 128), BF)
    far, mid, near = [bands[:, at : at + 128] for at in (128, 256, 384)]
    toeplitz[:, :128] = jnp.concatenate([near, mid, far, zero], 0)
    toeplitz[:, 128:] = jnp.concatenate([zero, near, mid, far], 0)


def transform(blocks, wins, chans, toeplitz, table):
    rows = []
    for halo, rec in blocks:
        rows.append(jnp.concatenate([halo, rec[:, :HALF]], 1))
        rows += [rec[:, HALF * (m - 1) : HALF * (m + 1)] for m in range(1, 2 * wins)]
    white = dot(jnp.concatenate(rows, 0), toeplitz).astype(BF)
    pieces = [
        jnp.concatenate([white[2 * w * chans : (2 * w + 1) * chans], white[(2 * w + 1) * chans : (2 * w + 2) * chans]], 1)
        for w in range(len(blocks) * wins)
    ]
    return dot(jnp.concatenate(pieces, 0), table)


def select_kernel(nv, sizes, rec_ref, *refs):
    tails, virt_ref, near_ref = refs[: len(sizes)], refs[-2], refs[-1]
    time = rec_ref.shape[2]
    at = 0
    for tail, size in zip(tails, sizes):
        tail[...] = rec_ref[:, at : at + size, time - HALF :]
        at += size
    for b in range(rec_ref.shape[0]):
        rows = [rec_ref[b, r * VSTEP : (r + 1) * VSTEP, :].astype(F32)[0:1] for r in range(nv)]
        rows = jnp.concatenate(rows, 0)
        virt_ref[b * nv : (b + 1) * nv, :] = rows
        near_ref[b * nv : (b + 1) * nv, :] = rows[:, time - HALF :]


def select(records, sizes):
    nblk, chans, time = records.shape
    nv = chans // VSTEP
    per = 2 if nv % 8 == 0 else 4
    return pl.pallas_call(
        lambda *refs: select_kernel(nv, sizes, *refs),
        grid=(nblk // per,),
        in_specs=[pl.BlockSpec((per, chans, time), lambda b: (b, 0, 0))],
        out_specs=[pl.BlockSpec((per, size, HALF), lambda b: (b, 0, 0)) for size in sizes]
        + [pl.BlockSpec((per * nv, time), lambda b: (b, 0)), pl.BlockSpec((per * nv, HALF), lambda b: (b, 0))],
        out_shape=[jax.ShapeDtypeStruct((nblk, size, HALF), BF) for size in sizes]
        + [jax.ShapeDtypeStruct((nblk * nv, time), F32), jax.ShapeDtypeStruct((nblk * nv, HALF), F32)],
        compiler_params=pltpu.CompilerParams(vmem_limit_bytes=60 * MIB),
        cost_estimate=pl.CostEstimate(flops=0, bytes_accessed=records.size * 2, transcendentals=0),
        name="select",
    )(records)


def virtual_kernel(nblk, nv, wins, pairs_ref, virt_ref, halo_ref, taps_ref, table_ref, out_ref, toeplitz, row, held):
    build_toeplitz(taps_ref, row, toeplitz)
    count = nblk * nv
    block = (halo_ref[...].astype(BF), virt_ref[...].astype(BF))
    result = transform([block], wins, count, toeplitz[...], table_ref[...].astype(BF))
    for b in range(nblk):
        rows = [
            result[w * count + b * nv : w * count + (b + 1) * nv, p * BINS : (p + 1) * BINS]
            for w in range(wins)
            for p in range(2)
        ]
        held[b] = jnp.concatenate(rows, 0).astype(BF)
    for r in range(nblk):
        for k in range(SLOTS):
            out_ref[r, k] = held[pairs_ref[r, k]]


def virtual(virt, halo, taps, pairs, nblk):
    nv = virt.shape[0] // nblk
    wins = virt.shape[1] // WLEN
    rows = wins * 2 * nv
    shape = (nblk, SLOTS, rows, BINS)
    return pl.pallas_call(
        lambda *refs: virtual_kernel(nblk, nv, wins, *refs),
        grid_spec=pltpu.PrefetchScalarGridSpec(
            num_scalar_prefetch=1,
            grid=(1,),
            in_specs=[
                pl.BlockSpec(virt.shape, lambda t, s: (0, 0)),
                pl.BlockSpec(halo.shape, lambda t, s: (0, 0)),
                pl.BlockSpec((1, TAPS), lambda t, s: (0, 0)),
                pl.BlockSpec((WLEN, 2 * BINS), lambda t, s: (0, 0)),
            ],
            out_specs=pl.BlockSpec(shape, lambda t, s: (0, 0, 0, 0)),
            scratch_shapes=[
                pltpu.VMEM((WLEN, HALF), BF),
                pltpu.VMEM((8, 512), F32),
                pltpu.VMEM((nblk, rows, BINS), BF),
            ],
        ),
        out_shape=jax.ShapeDtypeStruct(shape, BF),
        compiler_params=pltpu.CompilerParams(vmem_limit_bytes=60 * MIB),
        cost_estimate=pl.CostEstimate(flops=10**8, bytes_accessed=virt.size * 8, transcendentals=0),
        name="virtual",
    )(pairs, virt, halo, taps, jnp.asarray(dft_table()))


def spectra_kernel(per, size, wins, rec_ref, halo_ref, taps_ref, table_ref, out_ref, toeplitz, table, row):
    @pl.when(pl.program_id(0) == 0)
    def _():
        table[...] = table_ref[...].astype(BF)
        build_toeplitz(taps_ref, row, toeplitz)

    blocks = [(halo_ref[b], rec_ref[b]) for b in range(per)]
    result = transform(blocks, wins, size, toeplitz[...], table[...]).astype(BF)
    for b in range(per):
        for w in range(wins):
            at = (b * wins + w) * size
            for p in range(2):
                out_ref[b, w, p] = result[at : at + size, p * BINS : (p + 1) * BINS]


def spectra(records, halo, taps, index):
    nblk, _, time = records.shape
    size = halo.shape[1]
    wins = time // WLEN
    per = 4
    return pl.pallas_call(
        lambda *refs: spectra_kernel(per, size, wins, *refs),
        grid=(nblk // per,),
        in_specs=[
            pl.BlockSpec((per, size, time), lambda b: (b, index, 0)),
            pl.BlockSpec((per, size, HALF), lambda b: (b, 0, 0)),
            pl.BlockSpec((1, TAPS), lambda b: (0, 0)),
            pl.BlockSpec((WLEN, 2 * BINS), lambda b: (0, 0)),
        ],
        out_specs=pl.BlockSpec((per, wins, 2, size, BINS), lambda b: (b, 0, 0, 0, 0)),
        out_shape=jax.ShapeDtypeStruct((nblk, wins, 2, size, BINS), BF),
        scratch_shapes=[pltpu.VMEM((WLEN, HALF), BF), pltpu.VMEM((WLEN, 2 * BINS), BF), pltpu.VMEM((8, 512), F32)],
        compiler_params=pltpu.CompilerParams(vmem_limit_bytes=60 * MIB),
        cost_estimate=pl.CostEstimate(
            flops=nblk * size * wins * 3 * 2 * 512 * 256, bytes_accessed=nblk * size * time * 3, transcendentals=0
        ),
        name="spectra",
    )(records, halo, taps, jnp.asarray(dft_table()))


def sources_kernel(nsrc, nnar, wins, nv, me_ref, *refs):
    virts, out_ref, held, turned = refs[:nnar], refs[-3], refs[-2], refs[-1]
    nw = nsrc * wins
    pitch = BINS + 8
    for n in range(nnar):
        held[me_ref[0] ^ n] = virts[n][...]

    def turn(src, carry):
        tiles = [[held[n, src, k].astype(F32) for n in range(nnar)] for k in range(SLOTS)]
        for w in range(wins):
            for p in range(2):
                at = (w * 2 + p) * nv
                tile = jnp.concatenate([tiles[k][n][at : at + nv] for k in range(SLOTS) for n in range(nnar)], 0)
                row = pl.multiple_of((p * nw + src * wins + w) * pitch, 8)
                turned[pl.ds(row, BINS), :] = tile.T
        return carry

    lax.fori_loop(0, nsrc, turn, 0, unroll=4)

    def one(j, carry):
        re = turned[pl.ds(j, nw, stride=pitch), :]
        im = turned[pl.ds(nw * pitch + j, nw, stride=pitch), :]
        top = jnp.concatenate([re, -im], 1)
        low = jnp.concatenate([im, re], 1)
        out_ref[j] = jnp.concatenate([top, low], 0).astype(BF)
        return carry

    lax.fori_loop(0, BINS, one, 0, unroll=8)


def sources(virts, me, wins, nv):
    nnar, nsrc = len(virts), virts[0].shape[0]
    nw = nsrc * wins
    width = SLOTS * nnar * nv
    return pl.pallas_call(
        lambda *refs: sources_kernel(nsrc, nnar, wins, nv, *refs),
        grid_spec=pltpu.PrefetchScalarGridSpec(
            num_scalar_prefetch=1,
            grid=(1,),
            in_specs=[pl.BlockSpec(v.shape, lambda t, e: (0,) * 4) for v in virts],
            out_specs=pl.BlockSpec((BINS, 2 * nw, 2 * width), lambda t, e: (0, 0, 0)),
            scratch_shapes=[
                pltpu.VMEM((nnar,) + virts[0].shape, BF),
                pltpu.VMEM((2 * nw * (BINS + 8), width), F32),
            ],
        ),
        out_shape=jax.ShapeDtypeStruct((BINS, 2 * nw, 2 * width), BF),
        compiler_params=pltpu.CompilerParams(vmem_limit_bytes=48 * MIB),
        cost_estimate=pl.CostEstimate(flops=10**8, bytes_accessed=8 * nnar * virts[0].size, transcendentals=0),
        name="sources",
    )(me, *virts)


def stack_kernel(nw, size, group, count_ref, *refs):
    recv, src_ref, lag_ref = refs[:3]
    out_ref, lag, wide, turned, cross = refs[-5:]
    step = pl.program_id(0)
    width = SLOTS * VIRTUAL_SOURCES
    depth = 2 * nw
    wins = recv.shape[1]
    pack = src_ref.shape[1] // depth
    full = pack * depth
    pitch, bpitch = size + 8, BINS + 8

    @pl.when(step == 0)
    def _():
        lag[...] = lag_ref[...].astype(BF)
        for src in range(recv.shape[0]):
            for w in range(wins):
                for p in range(2):
                    row = (p * nw + src * wins + w) * pitch
                    wide[row : row + size, :] = recv[src, w, p].astype(F32)

        def turn(i, carry):
            flat = wide[pl.ds(i, depth, stride=pitch), :]
            flat = jnp.concatenate([flat] * pack, 0).T
            if pack > 1:
                flat = jnp.where(own, flat, 0.0)
            for c in range(0, full, 128):
                part = flat[:, c : min(c + 128, full)]
                turned[c // 128, pl.ds(pl.multiple_of(i * bpitch, 8), BINS), 0 : part.shape[1]] = part
            return carry

        shape = (BINS, full)
        own = lax.broadcasted_iota(jnp.int32, shape, 0) % pack == lax.broadcasted_iota(jnp.int32, shape, 1) // depth
        lax.fori_loop(0, size, turn, 0, unroll=8)
        slot = lax.broadcasted_iota(jnp.int32, (1, 2 * width), 1) % width // VIRTUAL_SOURCES
        scale = jnp.where(slot < count_ref[0], 1.0 / math.sqrt(nw), 0.0).astype(F32)

        def one(j, carry):
            rows = []
            for u in range(pack):
                at = pl.ds(j * pack + u, size, stride=bpitch)
                rows.append(jnp.concatenate([turned[c, at, :] for c in range(turned.shape[0])], 1))
            left = jnp.concatenate(rows, 0)[:, :full].astype(BF)
            value = dot(left, src_ref[j]) * scale
            for u in range(pack):
                at = pl.ds(pl.multiple_of((j * pack + u) * pitch, 8), size)
                for p in range(2):
                    cross[p, at, :] = value[u * size : (u + 1) * size, p * width : (p + 1) * width]
            return carry

        lax.fori_loop(0, BINS // pack, one, 0, unroll=8 // pack)

    for q in range(0, group, 4):
        lefts = []
        for u in range(4):
            at = step * group + q + u
            tiles = [cross[p, pl.ds(at, BINS, stride=pitch), :].astype(BF).T for p in range(2)]
            lefts.append(jnp.concatenate(tiles, 1))
        value = dot(jnp.concatenate(lefts, 0), lag[...]).astype(BF)
        for u in range(4):
            for k in range(SLOTS):
                at = u * width + k * VIRTUAL_SOURCES
                out_ref[0, k, q + u] = value[at : at + VIRTUAL_SOURCES]


def stack(recv, table, count, lag, before, start, chans):
    nsrc, wins, _, size, _ = recv.shape
    nw = nsrc * wins
    group = 16
    pack = 2 if 4 * nw <= 128 else 1
    table = table.reshape(BINS // pack, pack * 2 * nw, table.shape[2])
    shape = (1, SLOTS, chans, VIRTUAL_SOURCES, LAG_COUNT)
    first = start // group
    operands = [count, recv, table, lag]
    in_specs = [
        pl.BlockSpec(recv.shape, lambda t, c: (0,) * 5),
        pl.BlockSpec(table.shape, lambda t, c: (0,) * 3),
        pl.BlockSpec(lag.shape, lambda t, c: (0, 0)),
    ]
    aliases = {}
    if before is not None:
        operands.append(before)
        in_specs.append(pl.BlockSpec(memory_space=pl.ANY))
        aliases = {4: 0}
    return pl.pallas_call(
        lambda *refs: stack_kernel(nw, size, group, *refs),
        grid_spec=pltpu.PrefetchScalarGridSpec(
            num_scalar_prefetch=1,
            grid=(size // group,),
            in_specs=in_specs,
            out_specs=pl.BlockSpec(
                (1, SLOTS, group, VIRTUAL_SOURCES, LAG_COUNT), lambda t, c: (0, 0, first + t, 0, 0)
            ),
            scratch_shapes=[
                pltpu.VMEM(lag.shape, BF),
                pltpu.VMEM((2 * nw * (size + 8), BINS), F32),
                pltpu.VMEM((-(-2 * nw * pack // 128), size * (BINS + 8), 128), F32),
                pltpu.VMEM((2, BINS * (size + 8), SLOTS * VIRTUAL_SOURCES), F32),
            ],
        ),
        out_shape=jax.ShapeDtypeStruct(shape, BF),
        input_output_aliases=aliases,
        compiler_params=pltpu.CompilerParams(vmem_limit_bytes=36 * MIB),
        cost_estimate=pl.CostEstimate(
            flops=size * 128 * 256 * 256 * 4, bytes_accessed=2 * (table.size + size * 32768), transcendentals=0
        ),
        name="stack",
    )(*operands)


def on_device(records, taps, pair_sources, pair_counts):
    nblk, chans, time = records.shape
    wins = time // WLEN
    nv = chans // VSTEP
    nwide, nnar = lax.axis_size("wide"), lax.axis_size("narrow")
    ahead = [(i, i + 1) for i in range(nwide - 1)]
    taps = taps[None]
    sizes = (chans // 2,) * 2
    *tails, rows, near = select(records, sizes)
    near = lax.ppermute(near, "wide", ahead)
    tails, near = lax.optimization_barrier((tails, near))
    halos = [lax.ppermute(tail, "wide", ahead) for tail in tails]
    picked = virtual(rows, near, taps, pair_sources, nblk)
    picked = lax.all_to_all(picked, "wide", split_axis=0, concat_axis=0, tiled=True)
    chunks = [spectra(records, halo, taps, i) for i, halo in enumerate(halos)]
    before, recvs = picked, []
    for chunk in chunks:
        chunk, _ = lax.optimization_barrier((chunk, before))
        before = lax.all_to_all(chunk, "wide", split_axis=0, concat_axis=0, tiled=True)
        recvs.append(before)
    virts = {0: picked}
    bit = nnar // 2
    while bit:
        for slot in sorted(virts):
            virts[slot ^ bit] = lax.ppermute(virts[slot], "narrow", [(i, i ^ bit) for i in range(nnar)])
        bit //= 2
    me = lax.axis_index("narrow").astype(jnp.int32)[None]
    table = sources([virts[slot] for slot in range(nnar)], me, wins, nv)
    lag = jnp.asarray(lag_table())
    out, start = None, 0
    for recv, size in zip(recvs, sizes):
        out = stack(recv, table, pair_counts, lag, out, start, chans)
        start += size
    return out


def solution(mesh):
    return jax.shard_map(
        on_device,
        mesh=mesh,
        in_specs=(P(None, "narrow", "wide"), P(), P(), P("wide")),
        out_specs=P("wide", None, "narrow", None, None),
        check_vma=False,
    )
```

```python
import math

import jax
import jax.numpy as jnp
import numpy as np
from jax import lax
from jax.experimental import pallas as pl
from jax.experimental.pallas import tpu as pltpu
from jax.sharding import PartitionSpec as P

BLOCK_CHANNELS = 512
VIRTUAL_SOURCES = 32
VSTEP = BLOCK_CHANNELS // VIRTUAL_SOURCES
TAPS = 201
WLEN = 512
HALF = 256
BINS = 128
F_LO = 4
LAG_COUNT = 256
SLOTS = 4
BF = jnp.bfloat16
F32 = jnp.float32
MIB = 1 << 20


def dft_table():
    times = np.arange(WLEN, dtype=np.int32)[:, None]
    bins = (F_LO + np.arange(BINS, dtype=np.int32))[None, :]
    angle = np.mod(times * bins, WLEN).astype(np.float32) * np.float32(2.0 * math.pi / WLEN)
    scale = np.float32(1.0 / math.sqrt(WLEN))
    return np.concatenate([np.cos(angle) * scale, -np.sin(angle) * scale], 1).astype(BF).astype(np.float32)


def lag_table():
    bins = (F_LO + np.arange(BINS, dtype=np.int32))[:, None]
    lags = (np.arange(LAG_COUNT, dtype=np.int32) - LAG_COUNT // 2)[None, :]
    angle = np.mod(bins * lags, WLEN).astype(np.float32) * np.float32(2.0 * math.pi / WLEN)
    scale = np.float32(1.0 / math.sqrt(BINS))
    return np.concatenate([np.cos(angle) * scale, -np.sin(angle) * scale], 0).astype(BF).astype(np.float32)


def dot(a, b):
    return lax.dot_general(a, b, (((1,), (0,)), ((), ())), preferred_element_type=F32)


def build_toeplitz(taps_ref, row, toeplitz):
    row[...] = jnp.zeros_like(row)
    row[:, 128 : 128 + TAPS] = jnp.broadcast_to(taps_ref[...].astype(BF).astype(F32), (8, TAPS))
    bands = jnp.broadcast_to(row[0:1, :], (128, 512))
    bands = pltpu.roll(bands, 0, 1, stride=1, stride_axis=0).astype(BF)
    zero = jnp.zeros((128, 128), BF)
    far, mid, near = [bands[:, at : at + 128] for at in (128, 256, 384)]
    toeplitz[:, :128] = jnp.concatenate([near, mid, far, zero], 0)
    toeplitz[:, 128:] = jnp.concatenate([zero, near, mid, far], 0)


def transform(blocks, wins, chans, toeplitz, table):
    rows = []
    for halo, rec in blocks:
        rows.append(jnp.concatenate([halo, rec[:, :HALF]], 1))
        rows += [rec[:, HALF * (m - 1) : HALF * (m + 1)] for m in range(1, 2 * wins)]
    white = dot(jnp.concatenate(rows, 0), toeplitz).astype(BF)
    pieces = [
        jnp.concatenate([white[2 * w * chans : (2 * w + 1) * chans], white[(2 * w + 1) * chans : (2 * w + 2) * chans]], 1)
        for w in range(len(blocks) * wins)
    ]
    return dot(jnp.concatenate(pieces, 0), table)


def virtual_rows(ref, nv):
    rows = [ref[b, r * VSTEP : (r + 1) * VSTEP, :].astype(F32)[0:1] for b in range(ref.shape[0]) for r in range(nv)]
    return jnp.concatenate(rows, 0).astype(BF)


def block_rows(result, b, nv, wins, count):
    parts = [
        result[w * count + b * nv : w * count + (b + 1) * nv, p * BINS : (p + 1) * BINS]
        for w in range(wins)
        for p in range(2)
    ]
    return jnp.concatenate(parts, 0).astype(BF)


def early_kernel(rec_ref, taps_ref, table_ref, virt_ref, rows_ref, toeplitz_ref, forward_ref, row):
    nblk, chans, time = rec_ref.shape
    wins = time // WLEN - 1
    nv = chans // VSTEP
    count = nblk * nv
    build_toeplitz(taps_ref, row, toeplitz_ref)
    forward_ref[...] = table_ref[...].astype(BF)
    rows = virtual_rows(rec_ref, nv)
    rows_ref[...] = rows[:, :WLEN]
    block = (rows[:, HALF:WLEN], rows[:, WLEN:])
    result = transform([block], wins, count, toeplitz_ref[...], forward_ref[...])
    for b in range(nblk):
        virt_ref[b] = block_rows(result, b, nv, wins, count)


def early(records, taps):
    nblk, chans, time = records.shape
    nv = chans // VSTEP
    vmem = pl.BlockSpec(memory_space=pltpu.VMEM)
    return pl.pallas_call(
        early_kernel,
        in_specs=[vmem] * 3,
        out_specs=[vmem] * 4,
        out_shape=[
            jax.ShapeDtypeStruct((nblk, (time // WLEN - 1) * 2 * nv, BINS), BF),
            jax.ShapeDtypeStruct((nblk * nv, WLEN), BF),
            jax.ShapeDtypeStruct((WLEN, HALF), BF),
            jax.ShapeDtypeStruct((WLEN, 2 * BINS), BF),
        ],
        scratch_shapes=[pltpu.VMEM((8, 512), F32)],
        compiler_params=pltpu.CompilerParams(vmem_limit_bytes=40 * MIB),
        cost_estimate=pl.CostEstimate(flops=4 * 10**8, bytes_accessed=records.size * 2, transcendentals=0),
        name="early",
    )(records, taps, jnp.asarray(dft_table()))


def spectra_kernel(start, size, pairs_ref, me_ref, rec_ref, halo_ref, toeplitz_ref, forward_ref, *refs):
    held, sems = refs[-2:]
    nblk, chans, time = rec_ref.shape
    wins = time // WLEN
    nv = chans // VSTEP
    me = me_ref[0]
    copies = []
    for m in range(nblk):
        source = rec_ref.at[me ^ m, pl.ds(start, size)]
        copies.append(pltpu.make_async_copy(source, held.at[m], sems.at[m]))
        copies[-1].start()
    if len(refs) > nblk + 2:
        rows_ref, virt_ref, outs, virt = refs[0], refs[1], refs[2 : nblk + 2], refs[nblk + 2]
        block = (virtual_rows(halo_ref, nv), rows_ref[...])
        result = transform([block], 1, nblk * nv, toeplitz_ref[...], forward_ref[...])
        for b in range(nblk):
            virt[b] = block_rows(result, b, nv, 1, nblk * nv)
        for m in range(nblk):
            for k in range(SLOTS):
                block = pairs_ref[me ^ m, k]
                lo = wins * 2 * size + k * wins * 2 * nv
                outs[m][lo : lo + 2 * nv] = virt[block]
                outs[m][lo + 2 * nv : lo + wins * 2 * nv] = virt_ref[block]
    else:
        outs = refs[:nblk]
    per = 2
    for m in range(0, nblk, per):
        blocks = []
        for u in range(per):
            copies[m + u].wait()
            blocks.append((halo_ref[me ^ (m + u), start : start + size], held[m + u]))
        result = transform(blocks, wins, size, toeplitz_ref[...], forward_ref[...]).astype(BF)
        for u in range(per):
            for w in range(wins):
                for p in range(2):
                    lo = (u * wins + w) * size
                    row = (w * 2 + p) * size
                    outs[m + u][row : row + size] = result[lo : lo + size, p * BINS : (p + 1) * BINS]


def spectra(records, halo, toeplitz, forward, pairs, me, start, size, virtual=()):
    nblk, chans, time = records.shape
    wins = time // WLEN
    nv = chans // VSTEP
    shape = (wins * 2 * size + (SLOTS * wins * 2 * nv if virtual else 0), BINS)
    smem, vmem = pl.BlockSpec(memory_space=pltpu.SMEM), pl.BlockSpec(memory_space=pltpu.VMEM)
    operands = [pairs, me, records, halo, toeplitz, forward, *virtual]
    scratch = [pltpu.VMEM((nblk, 2 * nv, BINS), BF)] if virtual else []
    outs = pl.pallas_call(
        lambda *refs: spectra_kernel(start, size, *refs),
        in_specs=[smem, smem, pl.BlockSpec(memory_space=pl.ANY)] + [vmem] * (len(operands) - 3),
        out_specs=[vmem] * nblk,
        out_shape=[jax.ShapeDtypeStruct(shape, BF)] * nblk,
        scratch_shapes=scratch + [pltpu.VMEM((nblk, size, time), BF), pltpu.SemaphoreType.DMA((nblk,))],
        compiler_params=pltpu.CompilerParams(vmem_limit_bytes=40 * MIB),
        cost_estimate=pl.CostEstimate(
            flops=nblk * size * wins * 3 * 2 * 512 * 256, bytes_accessed=nblk * size * time * 3, transcendentals=0
        ),
        name="spectra",
    )(*operands)
    return list(outs)


def collect_kernel(rows, *refs):
    out_ref = refs[-1]
    for m, ref in enumerate(refs[:-1]):
        at = ref.shape[0] - SLOTS * rows
        for k in range(SLOTS):
            out_ref[m, k] = ref[at + k * rows : at + (k + 1) * rows]


def collect(chunks, rows):
    vmem = pl.BlockSpec(memory_space=pltpu.VMEM)
    return pl.pallas_call(
        lambda *refs: collect_kernel(rows, *refs),
        in_specs=[vmem] * len(chunks),
        out_specs=vmem,
        out_shape=jax.ShapeDtypeStruct((len(chunks), SLOTS, rows, BINS), BF),
        compiler_params=pltpu.CompilerParams(vmem_limit_bytes=32 * MIB),
        cost_estimate=pl.CostEstimate(flops=0, bytes_accessed=len(chunks) * rows * 2048, transcendentals=0),
        name="collect",
    )(*chunks)


def sources_kernel(nsrc, nnar, wins, nv, me_ref, place_ref, *refs):
    virts, out_ref, held, turned = refs[:nnar], refs[nnar], refs[nnar + 1], refs[nnar + 2]
    nw = nsrc * wins
    pitch = BINS + 8
    for n in range(nnar):
        held[place_ref[0] ^ n] = virts[n][...]

    def turn(m, carry):
        tiles = [[held[n, m, k].astype(F32) for n in range(nnar)] for k in range(SLOTS)]
        for w in range(wins):
            for p in range(2):
                at = (w * 2 + p) * nv
                tile = jnp.concatenate([tiles[k][n][at : at + nv] for k in range(SLOTS) for n in range(nnar)], 0)
                row = pl.multiple_of((p * nw + (me_ref[0] ^ m) * wins + w) * pitch, 8)
                turned[pl.ds(row, BINS), :] = tile.T
        return carry

    lax.fori_loop(0, nsrc, turn, 0, unroll=4)

    def one(j, carry):
        re = turned[pl.ds(j, nw, stride=pitch), :]
        im = turned[pl.ds(nw * pitch + j, nw, stride=pitch), :]
        top = jnp.concatenate([re, -im], 1)
        low = jnp.concatenate([im, re], 1)
        out_ref[j] = jnp.concatenate([top, low], 0).astype(BF)
        return carry

    lax.fori_loop(0, BINS, one, 0, unroll=8)


def sources(virts, me, place, wins, nv):
    nnar, nsrc = len(virts), virts[0].shape[0]
    nw = nsrc * wins
    width = SLOTS * nnar * nv
    smem, vmem = pl.BlockSpec(memory_space=pltpu.SMEM), pl.BlockSpec(memory_space=pltpu.VMEM)
    return pl.pallas_call(
        lambda *refs: sources_kernel(nsrc, nnar, wins, nv, *refs),
        in_specs=[smem, smem] + [vmem] * nnar,
        out_specs=vmem,
        out_shape=jax.ShapeDtypeStruct((BINS, 2 * nw, 2 * width), BF),
        scratch_shapes=[
            pltpu.VMEM((nnar,) + virts[0].shape, BF),
            pltpu.VMEM((2 * nw * (BINS + 8), width), F32),
        ],
        compiler_params=pltpu.CompilerParams(vmem_limit_bytes=40 * MIB),
        cost_estimate=pl.CostEstimate(flops=10**8, bytes_accessed=8 * nnar * virts[0].size, transcendentals=0),
        name="sources",
    )(me, place, *virts)


def stack_kernel(nw, wins, size, group, count_ref, me_ref, *refs):
    nsrc = nw // wins
    recvs, src_ref, lag_ref = refs[:nsrc], refs[nsrc], refs[nsrc + 1]
    out_ref, lag, wide, turned, cross = refs[-5:]
    step = pl.program_id(0)
    width = SLOTS * VIRTUAL_SOURCES
    depth = 2 * nw
    pack = src_ref.shape[1] // depth
    full = pack * depth
    pitch, bpitch = size + 8, BINS + 8

    @pl.when(step == 0)
    def _():
        lag[...] = lag_ref[...].astype(BF)
        for m in range(nsrc):
            src = me_ref[0] ^ m
            for w in range(wins):
                for p in range(2):
                    row = pl.multiple_of((p * nw + src * wins + w) * pitch, 8)
                    at = (w * 2 + p) * size
                    wide[pl.ds(row, size), :] = recvs[m][at : at + size].astype(F32)

        def turn(i, carry):
            flat = wide[pl.ds(i, depth, stride=pitch), :]
            flat = jnp.concatenate([flat] * pack, 0).T
            if pack > 1:
                flat = jnp.where(own, flat, 0.0)
            for c in range(0, full, 128):
                part = flat[:, c : min(c + 128, full)]
                turned[c // 128, pl.ds(pl.multiple_of(i * bpitch, 8), BINS), 0 : part.shape[1]] = part
            return carry

        shape = (BINS, full)
        own = lax.broadcasted_iota(jnp.int32, shape, 0) % pack == lax.broadcasted_iota(jnp.int32, shape, 1) // depth
        lax.fori_loop(0, size, turn, 0, unroll=8)
        slot = lax.broadcasted_iota(jnp.int32, (1, 2 * width), 1) % width // VIRTUAL_SOURCES
        scale = jnp.where(slot < count_ref[0], 1.0 / math.sqrt(nw), 0.0).astype(F32)

        def one(j, carry):
            rows = []
            for u in range(pack):
                at = pl.ds(j * pack + u, size, stride=bpitch)
                rows.append(jnp.concatenate([turned[c, at, :] for c in range(turned.shape[0])], 1))
            left = jnp.concatenate(rows, 0)[:, :full].astype(BF)
            value = dot(left, src_ref[j]) * scale
            for u in range(pack):
                at = pl.ds(pl.multiple_of((j * pack + u) * pitch, 8), size)
                for p in range(2):
                    cross[p, at, :] = value[u * size : (u + 1) * size, p * width : (p + 1) * width]
            return carry

        lax.fori_loop(0, BINS // pack, one, 0, unroll=8 // pack)

    for q in range(0, group, 4):
        lefts = []
        for u in range(4):
            at = step * group + q + u
            tiles = [cross[p, pl.ds(at, BINS, stride=pitch), :].astype(BF).T for p in range(2)]
            lefts.append(jnp.concatenate(tiles, 1))
        value = dot(jnp.concatenate(lefts, 0), lag[...]).astype(BF)
        for u in range(4):
            for k in range(SLOTS):
                at = u * width + k * VIRTUAL_SOURCES
                out_ref[0, k, q + u] = value[at : at + VIRTUAL_SOURCES]


def stack(recvs, table, count, me, lag, before, start, size, wins, chans):
    nw = wins * len(recvs)
    group = 16
    pack = 2 if 4 * nw <= 128 else 1
    table = table.reshape(BINS // pack, pack * 2 * nw, table.shape[2])
    shape = (1, SLOTS, chans, VIRTUAL_SOURCES, LAG_COUNT)
    first = start // group
    operands = [count, me, *recvs, table, lag]
    in_specs = [pl.BlockSpec(recv.shape, lambda t, c, e: (0, 0)) for recv in recvs] + [
        pl.BlockSpec(table.shape, lambda t, c, e: (0,) * 3),
        pl.BlockSpec(lag.shape, lambda t, c, e: (0, 0)),
    ]
    aliases = {}
    if before is not None:
        operands.append(before)
        in_specs.append(pl.BlockSpec(memory_space=pl.ANY))
        aliases = {len(operands) - 1: 0}
    return pl.pallas_call(
        lambda *refs: stack_kernel(nw, wins, size, group, *refs),
        grid_spec=pltpu.PrefetchScalarGridSpec(
            num_scalar_prefetch=2,
            grid=(size // group,),
            in_specs=in_specs,
            out_specs=pl.BlockSpec(
                (1, SLOTS, group, VIRTUAL_SOURCES, LAG_COUNT), lambda t, c, e: (0, 0, first + t, 0, 0)
            ),
            scratch_shapes=[
                pltpu.VMEM(lag.shape, BF),
                pltpu.VMEM((2 * nw * (size + 8), BINS), F32),
                pltpu.VMEM((-(-2 * nw * pack // 128), size * (BINS + 8), 128), F32),
                pltpu.VMEM((2, BINS * (size + 8), SLOTS * VIRTUAL_SOURCES), F32),
            ],
        ),
        out_shape=jax.ShapeDtypeStruct(shape, BF),
        input_output_aliases=aliases,
        compiler_params=pltpu.CompilerParams(vmem_limit_bytes=36 * MIB),
        cost_estimate=pl.CostEstimate(
            flops=size * 128 * 256 * 256 * 4, bytes_accessed=2 * (table.size + size * 32768), transcendentals=0
        ),
        name="stack",
    )(*operands)


def swap(value, axis, mask):
    return lax.ppermute(value, axis, [(i, i ^ mask) for i in range(lax.axis_size(axis))])


def after(value, others):
    return lax.optimization_barrier((value, others))[0] if others else value


def on_device(records, taps, pair_sources, pair_counts):
    nblk, chans, time = records.shape
    wins = time // WLEN
    nv = chans // VSTEP
    nwide, nnar = lax.axis_size("wide"), lax.axis_size("narrow")
    half = chans // 2
    me = lax.axis_index("wide").astype(jnp.int32)[None]
    place = lax.axis_index("narrow").astype(jnp.int32)[None]
    halo = lax.ppermute(records[:, :, time - HALF :], "wide", [(i, i + 1) for i in range(nwide - 1)])
    virt, rows, toeplitz, forward = early(records, taps[None])
    near = spectra(records, halo, toeplitz, forward, pair_sources, me, 0, half, (rows, virt))
    order = list(range(nwide - 1, 0, -1))
    for m in order[:-2]:
        near[m] = swap(near[m], "wide", m)
    held = after(halo, [near[n] for n in order[:2]])
    far = spectra(records, held, toeplitz, forward, pair_sources, me, half, half)
    for m in order[-2:]:
        near[m] = swap(after(near[m], [far[0]]), "wide", m)

    top = nnar // 2
    picked = collect(near, wins * 2 * nv)
    slots = {0: picked, **{n: swap(picked, "narrow", n) for n in (top, 1) if n}}
    for i, m in enumerate(order):
        if i == 3:
            waits = [far[n] for n in order[:2]]
            bit = top
            while bit:
                for n in sorted(slots):
                    if n ^ bit not in slots:
                        slots[n ^ bit] = swap(after(slots[n], waits), "narrow", bit)
                bit //= 2
        far[m] = swap(after(far[m], [near[order[min(i + 2, nwide - 2)]]]), "wide", m)
    table = sources([slots[n] for n in range(nnar)], me, place, wins, nv)
    lag = jnp.asarray(lag_table())
    out = stack(near, table, pair_counts, me, lag, None, 0, half, wins, chans)
    return stack(far, table, pair_counts, me, lag, out, half, half, wins, chans)


def solution(mesh):
    return jax.shard_map(
        on_device,
        mesh=mesh,
        in_specs=(P(None, "narrow", "wide"), P(), P(), P("wide")),
        out_specs=P("wide", None, "narrow", None, None),
        check_vma=False,
    )
```

```python
import math

import jax
import jax.numpy as jnp
import numpy as np
from jax import lax
from jax.experimental import pallas as pl
from jax.experimental.pallas import tpu as pltpu
from jax.sharding import PartitionSpec as P

BLOCK_CHANNELS = 512
VIRTUAL_SOURCES = 32
VSTEP = BLOCK_CHANNELS // VIRTUAL_SOURCES
TAPS = 201
WLEN = 512
HALF = 256
BINS = 128
F_LO = 4
LAG_COUNT = 256
SLOTS = 4
BF = jnp.bfloat16
F32 = jnp.float32
MIB = 1 << 20


def dft_table():
    times = np.arange(WLEN, dtype=np.int32)[:, None]
    bins = (F_LO + np.arange(BINS, dtype=np.int32))[None, :]
    angle = np.mod(times * bins, WLEN).astype(np.float32) * np.float32(2.0 * math.pi / WLEN)
    scale = np.float32(1.0 / math.sqrt(WLEN))
    return np.concatenate([np.cos(angle) * scale, -np.sin(angle) * scale], 1).astype(BF).astype(np.float32)


def lag_table():
    bins = (F_LO + np.arange(BINS, dtype=np.int32))[:, None]
    lags = (np.arange(LAG_COUNT, dtype=np.int32) - LAG_COUNT // 2)[None, :]
    angle = np.mod(bins * lags, WLEN).astype(np.float32) * np.float32(2.0 * math.pi / WLEN)
    scale = np.float32(1.0 / math.sqrt(BINS))
    return np.concatenate([np.cos(angle) * scale, -np.sin(angle) * scale], 0).astype(BF).astype(np.float32)


def dot(a, b):
    return lax.dot_general(a, b, (((1,), (0,)), ((), ())), preferred_element_type=F32)


def build_toeplitz(taps_ref, row, toeplitz):
    row[...] = jnp.zeros_like(row)
    row[:, 128 : 128 + TAPS] = jnp.broadcast_to(taps_ref[...].astype(BF).astype(F32), (8, TAPS))
    bands = jnp.broadcast_to(row[0:1, :], (128, 512))
    bands = pltpu.roll(bands, 0, 1, stride=1, stride_axis=0).astype(BF)
    zero = jnp.zeros((128, 128), BF)
    far, mid, near = [bands[:, at : at + 128] for at in (128, 256, 384)]
    toeplitz[:, :128] = jnp.concatenate([near, mid, far, zero], 0)
    toeplitz[:, 128:] = jnp.concatenate([zero, near, mid, far], 0)


def transform(blocks, wins, chans, toeplitz, table):
    rows = []
    for halo, rec in blocks:
        rows.append(jnp.concatenate([halo, rec[:, :HALF]], 1))
        rows += [rec[:, HALF * (m - 1) : HALF * (m + 1)] for m in range(1, 2 * wins)]
    white = dot(jnp.concatenate(rows, 0), toeplitz).astype(BF)
    pieces = [
        jnp.concatenate([white[2 * w * chans : (2 * w + 1) * chans], white[(2 * w + 1) * chans : (2 * w + 2) * chans]], 1)
        for w in range(len(blocks) * wins)
    ]
    return dot(jnp.concatenate(pieces, 0), table)


def virtual_rows(ref, nv):
    rows = [ref[b, r * VSTEP : (r + 1) * VSTEP, :].astype(F32)[0:1] for b in range(ref.shape[0]) for r in range(nv)]
    return jnp.concatenate(rows, 0).astype(BF)


def block_rows(result, b, nv, wins, count):
    parts = [
        result[w * count + b * nv : w * count + (b + 1) * nv, p * BINS : (p + 1) * BINS]
        for w in range(wins)
        for p in range(2)
    ]
    return jnp.concatenate(parts, 0).astype(BF)


def rows_kernel(rec_ref, rows_ref, near_ref, same_ref):
    time = rec_ref.shape[2]
    rows = virtual_rows(rec_ref, rec_ref.shape[1] // VSTEP)
    rows_ref[...] = rows
    near_ref[...] = rows[:, time - HALF :]


def extract(records):
    nblk, chans, time = records.shape
    count = nblk * (chans // VSTEP)
    vmem = pl.BlockSpec(memory_space=pltpu.VMEM)
    return pl.pallas_call(
        rows_kernel,
        in_specs=[vmem],
        out_specs=[vmem] * 3,
        out_shape=[
            jax.ShapeDtypeStruct((count, time), BF),
            jax.ShapeDtypeStruct((count, HALF), BF),
            jax.ShapeDtypeStruct(records.shape, BF),
        ],
        input_output_aliases={0: 2},
        compiler_params=pltpu.CompilerParams(vmem_limit_bytes=40 * MIB),
        cost_estimate=pl.CostEstimate(flops=0, bytes_accessed=records.size, transcendentals=0),
        name="extract",
    )(records)


def virtual_kernel(nblk, pairs_ref, me_ref, rows_ref, halo_ref, taps_ref, table_ref, *refs):
    picks, (toeplitz_ref, forward_ref, row, virt) = refs[:nblk], refs[nblk:]
    count, time = rows_ref.shape
    nv, wins = count // nblk, time // WLEN
    build_toeplitz(taps_ref, row, toeplitz_ref)
    forward_ref[...] = table_ref[...].astype(BF)
    block = (halo_ref[...], rows_ref[...])
    result = transform([block], wins, count, toeplitz_ref[...], forward_ref[...])
    for b in range(nblk):
        virt[b] = block_rows(result, b, nv, wins, count)
    for m in range(nblk):
        for k in range(SLOTS):
            picks[m][k] = virt[pairs_ref[me_ref[0] ^ m, k]]


def virtual(rows, halo, taps, pairs, me, nblk):
    count, time = rows.shape
    size = (time // WLEN) * 2 * (count // nblk)
    smem, vmem = pl.BlockSpec(memory_space=pltpu.SMEM), pl.BlockSpec(memory_space=pltpu.VMEM)
    outs = pl.pallas_call(
        lambda *refs: virtual_kernel(nblk, *refs),
        in_specs=[smem, smem] + [vmem] * 4,
        out_specs=[vmem] * (nblk + 2),
        out_shape=[jax.ShapeDtypeStruct((SLOTS, size, BINS), BF)] * nblk
        + [jax.ShapeDtypeStruct((WLEN, HALF), BF), jax.ShapeDtypeStruct((WLEN, 2 * BINS), BF)],
        scratch_shapes=[pltpu.VMEM((8, 512), F32), pltpu.VMEM((nblk, size, BINS), BF)],
        compiler_params=pltpu.CompilerParams(vmem_limit_bytes=40 * MIB),
        cost_estimate=pl.CostEstimate(flops=10**8, bytes_accessed=rows.size * 8, transcendentals=0),
        name="virtual",
    )(pairs, me, rows, halo, taps, jnp.asarray(dft_table()))
    return list(outs[:nblk]), outs[nblk], outs[nblk + 1]


def spectra_kernel(sizes, me_ref, rec_ref, halo_ref, toeplitz_ref, forward_ref, *refs):
    nblk, chans, time = rec_ref.shape
    wins = time // WLEN
    outs = [refs[nblk * q : nblk * (q + 1)] for q in range(len(sizes))]
    me = me_ref[0]
    per = 2
    for m in range(0, nblk, per):
        blocks = [(halo_ref[me ^ (m + u)], rec_ref[me ^ (m + u)]) for u in range(per)]
        result = transform(blocks, wins, chans, toeplitz_ref[...], forward_ref[...]).astype(BF)
        for u in range(per):
            for w in range(wins):
                for p in range(2):
                    lo = (u * wins + w) * chans
                    for out, size in zip(outs, sizes):
                        row = (w * 2 + p) * size
                        out[m + u][row : row + size] = result[lo : lo + size, p * BINS : (p + 1) * BINS]
                        lo += size


def spectra(records, halo, toeplitz, forward, me, sizes):
    nblk, chans, time = records.shape
    wins = time // WLEN
    shapes = []
    for size in sizes:
        shapes += [(wins * 2 * size, BINS)] * nblk
    smem, vmem = pl.BlockSpec(memory_space=pltpu.SMEM), pl.BlockSpec(memory_space=pltpu.VMEM)
    outs = pl.pallas_call(
        lambda *refs: spectra_kernel(sizes, *refs),
        in_specs=[smem] + [vmem] * 4,
        out_specs=[vmem] * len(shapes),
        out_shape=[jax.ShapeDtypeStruct(shape, BF) for shape in shapes],
        compiler_params=pltpu.CompilerParams(vmem_limit_bytes=40 * MIB),
        cost_estimate=pl.CostEstimate(
            flops=nblk * chans * wins * 3 * 2 * 512 * 256, bytes_accessed=nblk * chans * time * 3, transcendentals=0
        ),
        name="spectra",
    )(me, records, halo, toeplitz, forward)
    return [list(outs[i : i + nblk]) for i in range(0, len(outs), nblk)]


def sources_kernel(nsrc, nnar, wins, nv, me_ref, place_ref, *refs):
    virts, out_ref, held, turned = refs[:nnar], refs[nnar], refs[nnar + 1], refs[nnar + 2]
    nw = nsrc * wins
    pitch = BINS + 8
    for n in range(nnar):
        held[place_ref[0] ^ n] = virts[n][...]

    def turn(m, carry):
        tiles = [[held[n, m, k].astype(F32) for n in range(nnar)] for k in range(SLOTS)]
        for w in range(wins):
            for p in range(2):
                at = (w * 2 + p) * nv
                tile = jnp.concatenate([tiles[k][n][at : at + nv] for k in range(SLOTS) for n in range(nnar)], 0)
                row = pl.multiple_of((p * nw + (me_ref[0] ^ m) * wins + w) * pitch, 8)
                turned[pl.ds(row, BINS), :] = tile.T
        return carry

    lax.fori_loop(0, nsrc, turn, 0, unroll=4)

    def one(j, carry):
        re = turned[pl.ds(j, nw, stride=pitch), :]
        im = turned[pl.ds(nw * pitch + j, nw, stride=pitch), :]
        top = jnp.concatenate([re, -im], 1)
        low = jnp.concatenate([im, re], 1)
        out_ref[j] = jnp.concatenate([top, low], 0).astype(BF)
        return carry

    lax.fori_loop(0, BINS, one, 0, unroll=8)


def sources(virts, me, place, wins, nv):
    nnar, nsrc = len(virts), virts[0].shape[0]
    nw = nsrc * wins
    width = SLOTS * nnar * nv
    smem, vmem = pl.BlockSpec(memory_space=pltpu.SMEM), pl.BlockSpec(memory_space=pltpu.VMEM)
    return pl.pallas_call(
        lambda *refs: sources_kernel(nsrc, nnar, wins, nv, *refs),
        in_specs=[smem, smem] + [vmem] * nnar,
        out_specs=vmem,
        out_shape=jax.ShapeDtypeStruct((BINS, 2 * nw, 2 * width), BF),
        scratch_shapes=[
            pltpu.VMEM((nnar,) + virts[0].shape, BF),
            pltpu.VMEM((2 * nw * (BINS + 8), width), F32),
        ],
        compiler_params=pltpu.CompilerParams(vmem_limit_bytes=40 * MIB),
        cost_estimate=pl.CostEstimate(flops=10**8, bytes_accessed=8 * nnar * virts[0].size, transcendentals=0),
        name="sources",
    )(me, place, *virts)


def stack_kernel(nw, wins, size, group, count_ref, me_ref, *refs):
    nsrc = nw // wins
    recvs, src_ref, lag_ref = refs[:nsrc], refs[nsrc], refs[nsrc + 1]
    out_ref, lag, wide, turned, cross = refs[-5:]
    step = pl.program_id(0)
    width = SLOTS * VIRTUAL_SOURCES
    depth = 2 * nw
    pack = src_ref.shape[1] // depth
    full = pack * depth
    pitch, bpitch = size + 8, BINS + 8

    @pl.when(step == 0)
    def _():
        lag[...] = lag_ref[...].astype(BF)
        for m in range(nsrc):
            src = me_ref[0] ^ m
            for w in range(wins):
                for p in range(2):
                    row = pl.multiple_of((p * nw + src * wins + w) * pitch, 8)
                    at = (w * 2 + p) * size
                    wide[pl.ds(row, size), :] = recvs[m][at : at + size].astype(F32)

        def turn(i, carry):
            flat = wide[pl.ds(i, depth, stride=pitch), :]
            flat = jnp.concatenate([flat] * pack, 0).T
            if pack > 1:
                flat = jnp.where(own, flat, 0.0)
            for c in range(0, full, 128):
                part = flat[:, c : min(c + 128, full)]
                turned[c // 128, pl.ds(pl.multiple_of(i * bpitch, 8), BINS), 0 : part.shape[1]] = part
            return carry

        shape = (BINS, full)
        own = lax.broadcasted_iota(jnp.int32, shape, 0) % pack == lax.broadcasted_iota(jnp.int32, shape, 1) // depth
        lax.fori_loop(0, size, turn, 0, unroll=8)
        slot = lax.broadcasted_iota(jnp.int32, (1, 2 * width), 1) % width // VIRTUAL_SOURCES
        scale = jnp.where(slot < count_ref[0], 1.0 / math.sqrt(nw), 0.0).astype(F32)

        def one(j, carry):
            rows = []
            for u in range(pack):
                at = pl.ds(j * pack + u, size, stride=bpitch)
                rows.append(jnp.concatenate([turned[c, at, :] for c in range(turned.shape[0])], 1))
            left = jnp.concatenate(rows, 0)[:, :full].astype(BF)
            value = dot(left, src_ref[j]) * scale
            for u in range(pack):
                at = pl.ds(pl.multiple_of((j * pack + u) * pitch, 8), size)
                for p in range(2):
                    cross[p, at, :] = value[u * size : (u + 1) * size, p * width : (p + 1) * width]
            return carry

        lax.fori_loop(0, BINS // pack, one, 0, unroll=8 // pack)

    for q in range(0, group, 4):
        lefts = []
        for u in range(4):
            at = step * group + q + u
            tiles = [cross[p, pl.ds(at, BINS, stride=pitch), :].astype(BF).T for p in range(2)]
            lefts.append(jnp.concatenate(tiles, 1))
        value = dot(jnp.concatenate(lefts, 0), lag[...]).astype(BF)
        for u in range(4):
            for k in range(SLOTS):
                at = u * width + k * VIRTUAL_SOURCES
                out_ref[0, k, q + u] = value[at : at + VIRTUAL_SOURCES]


def stack(recvs, table, count, me, lag, before, start, size, wins, chans):
    nw = wins * len(recvs)
    group = 16
    pack = 2 if 4 * nw <= 128 else 1
    table = table.reshape(BINS // pack, pack * 2 * nw, table.shape[2])
    shape = (1, SLOTS, chans, VIRTUAL_SOURCES, LAG_COUNT)
    first = start // group
    operands = [count, me, *recvs, table, lag]
    in_specs = [pl.BlockSpec(recv.shape, lambda t, c, e: (0, 0)) for recv in recvs] + [
        pl.BlockSpec(table.shape, lambda t, c, e: (0,) * 3),
        pl.BlockSpec(lag.shape, lambda t, c, e: (0, 0)),
    ]
    aliases = {}
    if before is not None:
        operands.append(before)
        in_specs.append(pl.BlockSpec(memory_space=pl.ANY))
        aliases = {len(operands) - 1: 0}
    return pl.pallas_call(
        lambda *refs: stack_kernel(nw, wins, size, group, *refs),
        grid_spec=pltpu.PrefetchScalarGridSpec(
            num_scalar_prefetch=2,
            grid=(size // group,),
            in_specs=in_specs,
            out_specs=pl.BlockSpec(
                (1, SLOTS, group, VIRTUAL_SOURCES, LAG_COUNT), lambda t, c, e: (0, 0, first + t, 0, 0)
            ),
            scratch_shapes=[
                pltpu.VMEM(lag.shape, BF),
                pltpu.VMEM((2 * nw * (size + 8), BINS), F32),
                pltpu.VMEM((-(-2 * nw * pack // 128), size * (BINS + 8), 128), F32),
                pltpu.VMEM((2, BINS * (size + 8), SLOTS * VIRTUAL_SOURCES), F32),
            ],
        ),
        out_shape=jax.ShapeDtypeStruct(shape, BF),
        input_output_aliases=aliases,
        compiler_params=pltpu.CompilerParams(vmem_limit_bytes=36 * MIB),
        cost_estimate=pl.CostEstimate(
            flops=size * 128 * 256 * 256 * 4, bytes_accessed=2 * (table.size + size * 32768), transcendentals=0
        ),
        name="stack",
    )(*operands)


def swap(value, axis, mask):
    return lax.ppermute(value, axis, [(i, i ^ mask) for i in range(lax.axis_size(axis))])


def after(value, others):
    return lax.optimization_barrier((value, others))[0] if others else value


def on_device(records, taps, pair_sources, pair_counts):
    nblk, chans, time = records.shape
    wins = time // WLEN
    nv = chans // VSTEP
    nwide, nnar = lax.axis_size("wide"), lax.axis_size("narrow")
    half = chans // 2
    me = lax.axis_index("wide").astype(jnp.int32)[None]
    place = lax.axis_index("narrow").astype(jnp.int32)[None]
    ahead = [(i, i + 1) for i in range(nwide - 1)]
    order = list(range(nwide - 1, 0, -1))
    rows, tip, records = extract(records)
    tip = lax.ppermute(tip, "wide", ahead)
    halo = lax.ppermute(after(records[:, :, time - HALF :], [tip]), "wide", ahead)
    picked, toeplitz, forward = virtual(rows, tip, taps[None], pair_sources, me, nblk)
    for m in order:
        picked[m] = swap(picked[m], "wide", m)

    top = nnar // 2
    picked = jnp.stack(picked)
    slots = {0: picked, **{n: swap(picked, "narrow", n) for n in (top, 1) if n}}
    near, far = spectra(records, halo, toeplitz, forward, me, (half, half))
    for i, m in enumerate(order):
        if i == len(order) - 1:
            bit = top
            while bit:
                for n in sorted(slots):
                    if n ^ bit not in slots:
                        slots[n ^ bit] = swap(after(slots[n], [near[order[1]]]), "narrow", bit)
                bit //= 2
        waits = [slots[n] for n in sorted(slots) if n] if i >= len(order) - 2 else []
        near[m] = swap(after(near[m], waits), "wide", m)
    for i, m in enumerate(order):
        far[m] = swap(after(far[m], [near[order[min(i + 2, nwide - 2)]]]), "wide", m)
    table = sources([slots[n] for n in range(nnar)], me, place, wins, nv)
    lag = jnp.asarray(lag_table())
    out = stack(near, table, pair_counts, me, lag, None, 0, half, wins, chans)
    return stack(far, table, pair_counts, me, lag, out, half, half, wins, chans)


def solution(mesh):
    return jax.shard_map(
        on_device,
        mesh=mesh,
        in_specs=(P(None, "narrow", "wide"), P(), P(), P("wide")),
        out_specs=P("wide", None, "narrow", None, None),
        check_vma=False,
    )
```

```python
import math

import jax
import jax.numpy as jnp
import numpy as np
from jax import lax
from jax.experimental import pallas as pl
from jax.experimental.pallas import tpu as pltpu
from jax.sharding import PartitionSpec as P

BLOCK_CHANNELS = 512
VIRTUAL_SOURCES = 32
VSTEP = BLOCK_CHANNELS // VIRTUAL_SOURCES
TAPS = 201
WLEN = 512
HALF = 256
BINS = 128
F_LO = 4
LAG_COUNT = 256
SLOTS = 4
BF = jnp.bfloat16
F32 = jnp.float32
MIB = 1 << 20


def dft_table():
    times = np.arange(WLEN, dtype=np.int32)[:, None]
    bins = (F_LO + np.arange(BINS, dtype=np.int32))[None, :]
    angle = np.mod(times * bins, WLEN).astype(np.float32) * np.float32(2.0 * math.pi / WLEN)
    scale = np.float32(1.0 / math.sqrt(WLEN))
    return np.concatenate([np.cos(angle) * scale, -np.sin(angle) * scale], 1).astype(BF).astype(np.float32)


def lag_table():
    bins = (F_LO + np.arange(BINS, dtype=np.int32))[:, None]
    lags = (np.arange(LAG_COUNT, dtype=np.int32) - LAG_COUNT // 2)[None, :]
    angle = np.mod(bins * lags, WLEN).astype(np.float32) * np.float32(2.0 * math.pi / WLEN)
    scale = np.float32(1.0 / math.sqrt(BINS))
    return np.concatenate([np.cos(angle) * scale, -np.sin(angle) * scale], 0).astype(BF).astype(np.float32)


def dot(a, b):
    return lax.dot_general(a, b, (((1,), (0,)), ((), ())), preferred_element_type=F32)


def build_toeplitz(taps_ref, row, toeplitz):
    row[...] = jnp.zeros_like(row)
    row[:, 128 : 128 + TAPS] = jnp.broadcast_to(taps_ref[...].astype(BF).astype(F32), (8, TAPS))
    bands = jnp.broadcast_to(row[0:1, :], (128, 512))
    bands = pltpu.roll(bands, 0, 1, stride=1, stride_axis=0).astype(BF)
    zero = jnp.zeros((128, 128), BF)
    far, mid, near = [bands[:, at : at + 128] for at in (128, 256, 384)]
    toeplitz[:, :128] = jnp.concatenate([near, mid, far, zero], 0)
    toeplitz[:, 128:] = jnp.concatenate([zero, near, mid, far], 0)


def transform(blocks, wins, chans, toeplitz, table):
    rows = []
    for halo, rec in blocks:
        rows.append(jnp.concatenate([halo, rec[:, :HALF]], 1))
        rows += [rec[:, HALF * (m - 1) : HALF * (m + 1)] for m in range(1, 2 * wins)]
    white = dot(jnp.concatenate(rows, 0), toeplitz).astype(BF)
    pieces = [
        jnp.concatenate([white[2 * w * chans : (2 * w + 1) * chans], white[(2 * w + 1) * chans : (2 * w + 2) * chans]], 1)
        for w in range(len(blocks) * wins)
    ]
    return dot(jnp.concatenate(pieces, 0), table)


def early_kernel(pairs_ref, rec_ref, taps_ref, table_ref, picked_ref, toeplitz_ref, forward_ref, row, virt):
    nblk, chans, time = rec_ref.shape
    wins = time // WLEN - 1
    nv = chans // VSTEP
    count = nblk * nv
    build_toeplitz(taps_ref, row, toeplitz_ref)
    forward_ref[...] = table_ref[...].astype(BF)
    rows = [
        rec_ref[b, r * VSTEP : (r + 1) * VSTEP, HALF:].astype(F32)[0:1] for b in range(nblk) for r in range(nv)
    ]
    rows = jnp.concatenate(rows, 0).astype(BF)
    result = transform([(rows[:, :HALF], rows[:, HALF:])], wins, count, toeplitz_ref[...], forward_ref[...])
    for b in range(nblk):
        parts = [
            result[w * count + b * nv : w * count + (b + 1) * nv, p * BINS : (p + 1) * BINS]
            for w in range(wins)
            for p in range(2)
        ]
        virt[b] = jnp.concatenate(parts, 0).astype(BF)
    for r in range(nblk):
        for k in range(SLOTS):
            picked_ref[r, k] = virt[pairs_ref[r, k]]


def early(records, taps, pairs):
    nblk, chans, time = records.shape
    rows = (time // WLEN - 1) * 2 * (chans // VSTEP)
    smem, vmem = pl.BlockSpec(memory_space=pltpu.SMEM), pl.BlockSpec(memory_space=pltpu.VMEM)
    return pl.pallas_call(
        early_kernel,
        in_specs=[smem, vmem, vmem, vmem],
        out_specs=[vmem] * 3,
        out_shape=[
            jax.ShapeDtypeStruct((nblk, SLOTS, rows, BINS), BF),
            jax.ShapeDtypeStruct((WLEN, HALF), BF),
            jax.ShapeDtypeStruct((WLEN, 2 * BINS), BF),
        ],
        scratch_shapes=[pltpu.VMEM((8, 512), F32), pltpu.VMEM((nblk, rows, BINS), BF)],
        compiler_params=pltpu.CompilerParams(vmem_limit_bytes=16 * MIB),
        cost_estimate=pl.CostEstimate(flops=4 * 10**8, bytes_accessed=records.size * 2, transcendentals=0),
        name="early",
    )(pairs, records, taps, jnp.asarray(dft_table()))


def spectra_kernel(sizes, pairs_ref, me_ref, rec_ref, halo_ref, toeplitz_ref, forward_ref, *refs):
    nblk, chans, time = rec_ref.shape
    wins = time // WLEN
    nv = chans // VSTEP
    outs = [refs[nblk * q : nblk * (q + 1)] for q in range(len(sizes))]
    spec, virt = refs[nblk * len(sizes) :]
    me = me_ref[0]
    per = 2
    for m in range(0, nblk, per):
        blocks = [(halo_ref[me ^ (m + u)], rec_ref[me ^ (m + u)]) for u in range(per)]
        result = transform(blocks, wins, chans, toeplitz_ref[...], forward_ref[...])
        for u in range(per):
            at = u * wins * chans
            for p in range(2):
                spec[u, p] = result[at : at + chans, p * BINS : (p + 1) * BINS]
            chosen = [spec[u, p, pl.ds(0, nv, stride=VSTEP), :] for p in range(2)]
            virt[me ^ (m + u)] = jnp.concatenate(chosen, 0).astype(BF)
        result = result.astype(BF)
        for u in range(per):
            for w in range(wins):
                for p in range(2):
                    lo = (u * wins + w) * chans
                    for out, size in zip(outs, sizes):
                        at = (w * 2 + p) * size
                        out[m + u][at : at + size] = result[lo : lo + size, p * BINS : (p + 1) * BINS]
                        lo += size
    at = wins * 2 * sizes[0]
    for m in range(nblk):
        for k in range(SLOTS):
            lo = at + k * 2 * nv
            outs[0][m][lo : lo + 2 * nv] = virt[pairs_ref[me ^ m, k]]


def spectra(records, halo, toeplitz, forward, pairs, me, sizes):
    nblk, chans, time = records.shape
    wins = time // WLEN
    nv = chans // VSTEP
    shapes = []
    for q, size in enumerate(sizes):
        shapes += [(wins * 2 * size + (SLOTS * 2 * nv if q == 0 else 0), BINS)] * nblk
    smem, vmem = pl.BlockSpec(memory_space=pltpu.SMEM), pl.BlockSpec(memory_space=pltpu.VMEM)
    outs = pl.pallas_call(
        lambda *refs: spectra_kernel(sizes, *refs),
        in_specs=[smem, smem, vmem, vmem, vmem, vmem],
        out_specs=[vmem] * len(shapes),
        out_shape=[jax.ShapeDtypeStruct(shape, BF) for shape in shapes],
        scratch_shapes=[pltpu.VMEM((2, 2, chans, BINS), F32), pltpu.VMEM((nblk, 2 * nv, BINS), BF)],
        compiler_params=pltpu.CompilerParams(vmem_limit_bytes=16 * MIB),
        cost_estimate=pl.CostEstimate(
            flops=nblk * chans * wins * 3 * 2 * 512 * 256, bytes_accessed=nblk * chans * time * 3, transcendentals=0
        ),
        name="spectra",
    )(pairs, me, records, halo, toeplitz, forward)
    return [list(outs[i : i + nblk]) for i in range(0, len(outs), nblk)]


def collect_kernel(rows, *refs):
    out_ref = refs[-1]
    for m, ref in enumerate(refs[:-1]):
        at = ref.shape[0] - SLOTS * rows
        for k in range(SLOTS):
            out_ref[m, k] = ref[at + k * rows : at + (k + 1) * rows]


def collect(chunks, rows):
    vmem = pl.BlockSpec(memory_space=pltpu.VMEM)
    return pl.pallas_call(
        lambda *refs: collect_kernel(rows, *refs),
        in_specs=[vmem] * len(chunks),
        out_specs=vmem,
        out_shape=jax.ShapeDtypeStruct((len(chunks), SLOTS, rows, BINS), BF),
        compiler_params=pltpu.CompilerParams(vmem_limit_bytes=8 * MIB),
        cost_estimate=pl.CostEstimate(flops=0, bytes_accessed=len(chunks) * rows * 2048, transcendentals=0),
        name="collect",
    )(*chunks)


def sources_kernel(nsrc, nnar, wins, nv, me_ref, place_ref, *refs):
    lates, firsts = refs[:nnar], refs[nnar : 2 * nnar]
    out_ref, late, first, turned = refs[2 * nnar :]
    nw = nsrc * wins
    pitch = BINS + 8
    for n in range(nnar):
        late[place_ref[0] ^ n] = lates[n][...]
        first[place_ref[0] ^ n] = firsts[n][...]

    def turn(src, carry):
        after = [[late[n, src, k].astype(F32) for n in range(nnar)] for k in range(SLOTS)]
        start = [[first[n, me_ref[0] ^ src, k].astype(F32) for n in range(nnar)] for k in range(SLOTS)]
        for w in range(wins):
            held = after if w else start
            for p in range(2):
                at = (max(w - 1, 0) * 2 + p) * nv
                tile = jnp.concatenate([held[k][n][at : at + nv] for k in range(SLOTS) for n in range(nnar)], 0)
                row = pl.multiple_of((p * nw + src * wins + w) * pitch, 8)
                turned[pl.ds(row, BINS), :] = tile.T
        return carry

    lax.fori_loop(0, nsrc, turn, 0, unroll=4)

    def one(j, carry):
        re = turned[pl.ds(j, nw, stride=pitch), :]
        im = turned[pl.ds(nw * pitch + j, nw, stride=pitch), :]
        top = jnp.concatenate([re, -im], 1)
        low = jnp.concatenate([im, re], 1)
        out_ref[j] = jnp.concatenate([top, low], 0).astype(BF)
        return carry

    lax.fori_loop(0, BINS, one, 0, unroll=8)


def sources(lates, firsts, me, place, wins, nv):
    nnar, nsrc = len(lates), lates[0].shape[0]
    nw = nsrc * wins
    width = SLOTS * nnar * nv
    smem, vmem = pl.BlockSpec(memory_space=pltpu.SMEM), pl.BlockSpec(memory_space=pltpu.VMEM)
    return pl.pallas_call(
        lambda *refs: sources_kernel(nsrc, nnar, wins, nv, *refs),
        in_specs=[smem, smem] + [vmem] * (2 * nnar),
        out_specs=vmem,
        out_shape=jax.ShapeDtypeStruct((BINS, 2 * nw, 2 * width), BF),
        scratch_shapes=[
            pltpu.VMEM((nnar,) + lates[0].shape, BF),
            pltpu.VMEM((nnar,) + firsts[0].shape, BF),
            pltpu.VMEM((2 * nw * (BINS + 8), width), F32),
        ],
        compiler_params=pltpu.CompilerParams(vmem_limit_bytes=(10 + 2 * nw * BINS * width * 6 // MIB) * MIB),
        cost_estimate=pl.CostEstimate(flops=10**8, bytes_accessed=8 * nnar * lates[0].size, transcendentals=0),
        name="sources",
    )(me, place, *lates, *firsts)


def stack_kernel(nw, wins, size, group, count_ref, me_ref, *refs):
    nsrc = nw // wins
    recvs, src_ref, lag_ref = refs[:nsrc], refs[nsrc], refs[nsrc + 1]
    out_ref, lag, wide, turned, cross = refs[-5:]
    step = pl.program_id(0)
    width = SLOTS * VIRTUAL_SOURCES
    depth = 2 * nw
    pack = src_ref.shape[1] // depth
    full = pack * depth
    pitch, bpitch = size + 8, BINS + 8

    @pl.when(step == 0)
    def _():
        lag[...] = lag_ref[...].astype(BF)
        for m in range(nsrc):
            src = me_ref[0] ^ m
            for w in range(wins):
                for p in range(2):
                    row = pl.multiple_of((p * nw + src * wins + w) * pitch, 8)
                    at = (w * 2 + p) * size
                    wide[pl.ds(row, size), :] = recvs[m][at : at + size].astype(F32)

        def turn(i, carry):
            flat = wide[pl.ds(i, depth, stride=pitch), :]
            flat = jnp.concatenate([flat] * pack, 0).T
            if pack > 1:
                flat = jnp.where(own, flat, 0.0)
            for c in range(0, full, 128):
                part = flat[:, c : min(c + 128, full)]
                turned[c // 128, pl.ds(pl.multiple_of(i * bpitch, 8), BINS), 0 : part.shape[1]] = part
            return carry

        shape = (BINS, full)
        own = lax.broadcasted_iota(jnp.int32, shape, 0) % pack == lax.broadcasted_iota(jnp.int32, shape, 1) // depth
        lax.fori_loop(0, size, turn, 0, unroll=8)
        slot = lax.broadcasted_iota(jnp.int32, (1, 2 * width), 1) % width // VIRTUAL_SOURCES
        scale = jnp.where(slot < count_ref[0], 1.0 / math.sqrt(nw), 0.0).astype(F32)

        def one(j, carry):
            rows = []
            for u in range(pack):
                at = pl.ds(j * pack + u, size, stride=bpitch)
                rows.append(jnp.concatenate([turned[c, at, :] for c in range(turned.shape[0])], 1))
            left = jnp.concatenate(rows, 0)[:, :full].astype(BF)
            value = dot(left, src_ref[j]) * scale
            for u in range(pack):
                at = pl.ds(pl.multiple_of((j * pack + u) * pitch, 8), size)
                for p in range(2):
                    cross[p, at, :] = value[u * size : (u + 1) * size, p * width : (p + 1) * width]
            return carry

        lax.fori_loop(0, BINS // pack, one, 0, unroll=8 // pack)

    rows = 8
    for q in range(0, group, rows):
        lefts = []
        for u in range(rows):
            at = step * group + q + u
            tiles = [cross[p, pl.ds(at, BINS, stride=pitch), :].astype(BF).T for p in range(2)]
            lefts.append(jnp.concatenate(tiles, 1))
        value = dot(jnp.concatenate(lefts, 0), lag[...]).astype(BF)
        for u in range(rows):
            for k in range(SLOTS):
                at = u * width + k * VIRTUAL_SOURCES
                out_ref[0, k, q + u] = value[at : at + VIRTUAL_SOURCES]


def stack(recvs, table, count, me, lag, before, start, size, wins, chans):
    nsrc = len(recvs)
    nw = nsrc * wins
    group = 16
    pack = 2 if 4 * nw <= 128 else 1
    table = table.reshape(BINS // pack, pack * 2 * nw, table.shape[2])
    shape = (1, SLOTS, chans, VIRTUAL_SOURCES, LAG_COUNT)
    first = start // group
    operands = [count, me, *recvs, table, lag]
    in_specs = [pl.BlockSpec(recv.shape, lambda t, c, e: (0, 0)) for recv in recvs] + [
        pl.BlockSpec(table.shape, lambda t, c, e: (0,) * 3),
        pl.BlockSpec(lag.shape, lambda t, c, e: (0, 0)),
    ]
    aliases = {}
    if before is not None:
        operands.append(before)
        in_specs.append(pl.BlockSpec(memory_space=pl.ANY))
        aliases = {len(operands) - 1: 0}
    return pl.pallas_call(
        lambda *refs: stack_kernel(nw, wins, size, group, *refs),
        grid_spec=pltpu.PrefetchScalarGridSpec(
            num_scalar_prefetch=2,
            grid=(size // group,),
            in_specs=in_specs,
            out_specs=pl.BlockSpec(
                (1, SLOTS, group, VIRTUAL_SOURCES, LAG_COUNT), lambda t, c, e: (0, 0, first + t, 0, 0)
            ),
            scratch_shapes=[
                pltpu.VMEM(lag.shape, BF),
                pltpu.VMEM((2 * nw * (size + 8), BINS), F32),
                pltpu.VMEM((-(-2 * nw * pack // 128), size * (BINS + 8), 128), F32),
                pltpu.VMEM((2, BINS * (size + 8), SLOTS * VIRTUAL_SOURCES), F32),
            ],
        ),
        out_shape=jax.ShapeDtypeStruct(shape, BF),
        input_output_aliases=aliases,
        compiler_params=pltpu.CompilerParams(vmem_limit_bytes=(20 + table.size * 4 // MIB) * MIB),
        cost_estimate=pl.CostEstimate(
            flops=size * 128 * 256 * 256 * 4, bytes_accessed=2 * (table.size + size * 32768), transcendentals=0
        ),
        name="stack",
    )(*operands)


def swap(value, axis, mask):
    return lax.ppermute(value, axis, [(i, i ^ mask) for i in range(lax.axis_size(axis))])


def after(value, others):
    return lax.optimization_barrier((value, others))[0] if others else value


def on_device(records, taps, pair_sources, pair_counts):
    nblk, chans, time = records.shape
    wins = time // WLEN
    nv = chans // VSTEP
    nwide, nnar = lax.axis_size("wide"), lax.axis_size("narrow")
    sizes = (chans // 2,) * 2
    me = lax.axis_index("wide").astype(jnp.int32)[None]
    place = lax.axis_index("narrow").astype(jnp.int32)[None]
    halo = lax.ppermute(records[:, :, time - HALF :], "wide", [(i, i + 1) for i in range(nwide - 1)])
    picked, toeplitz, forward = early(records, taps[None], pair_sources)
    picked = lax.all_to_all(picked, "wide", split_axis=0, concat_axis=0, tiled=True)
    chunks = spectra(records, halo, toeplitz, forward, pair_sources, me, sizes)
    picked, (near, far) = lax.optimization_barrier((picked, chunks))
    order = list(range(nwide - 1, 0, -1))

    top = nnar // 2

    def begin(value):
        return {0: value, **{n: swap(value, "narrow", n) for n in (top, 1) if n}}

    def finish(slots, waits):
        bit = top
        while bit:
            for n in sorted(slots):
                if n ^ bit not in slots:
                    slots[n ^ bit] = swap(after(slots[n], waits), "narrow", bit)
            bit //= 2
        return [slots[n] for n in range(nnar)]

    lates = begin(picked)
    for i, m in enumerate(order):
        waits = []
        if i == len(order) - 2:
            waits = [lates[n] for n in sorted(lates) if n]
            lates = finish(lates, [near[order[1]]])
        near[m] = swap(after(near[m], waits), "wide", m)
    for i, m in enumerate(order):
        far[m] = swap(after(far[m], [near[order[min(i + 2, nwide - 2)]]]), "wide", m)
    firsts = finish(begin(collect(near, 2 * nv)), [far[n] for n in order[:2]])
    table = sources(lates, firsts, me, place, wins, nv)
    lag = jnp.asarray(lag_table())
    out, start = None, 0
    for recvs, size in zip((near, far), sizes):
        out = stack(recvs, table, pair_counts, me, lag, out, start, size, wins, chans)
        start += size
    return out


def solution(mesh):
    return jax.shard_map(
        on_device,
        mesh=mesh,
        in_specs=(P(None, "narrow", "wide"), P(), P(), P("wide")),
        out_specs=P("wide", None, "narrow", None, None),
        check_vma=False,
    )
```

```python
import math

import jax
import jax.numpy as jnp
import numpy as np
from jax import lax
from jax.experimental import pallas as pl
from jax.experimental.pallas import tpu as pltpu
from jax.sharding import PartitionSpec as P

BLOCK_CHANNELS = 512
VIRTUAL_SOURCES = 32
VSTEP = BLOCK_CHANNELS // VIRTUAL_SOURCES
TAPS = 201
WLEN = 512
HALF = 256
BINS = 128
F_LO = 4
LAG_COUNT = 256
SLOTS = 4
BF = jnp.bfloat16
F32 = jnp.float32
MIB = 1 << 20


def dft_table():
    times = np.arange(WLEN, dtype=np.int32)[:, None]
    bins = (F_LO + np.arange(BINS, dtype=np.int32))[None, :]
    angle = np.mod(times * bins, WLEN).astype(np.float32) * np.float32(2.0 * math.pi / WLEN)
    scale = np.float32(1.0 / math.sqrt(WLEN))
    return np.concatenate([np.cos(angle) * scale, -np.sin(angle) * scale], 1).astype(BF).astype(np.float32)


def lag_table():
    bins = (F_LO + np.arange(BINS, dtype=np.int32))[:, None]
    lags = (np.arange(LAG_COUNT, dtype=np.int32) - LAG_COUNT // 2)[None, :]
    angle = np.mod(bins * lags, WLEN).astype(np.float32) * np.float32(2.0 * math.pi / WLEN)
    scale = np.float32(1.0 / math.sqrt(BINS))
    return np.concatenate([np.cos(angle) * scale, -np.sin(angle) * scale], 0).astype(BF).astype(np.float32)


def dot(a, b):
    return lax.dot_general(a, b, (((1,), (0,)), ((), ())), preferred_element_type=F32)


def build_toeplitz(taps_ref, row, toeplitz):
    row[...] = jnp.zeros_like(row)
    row[:, 128 : 128 + TAPS] = jnp.broadcast_to(taps_ref[...].astype(BF).astype(F32), (8, TAPS))
    bands = jnp.broadcast_to(row[0:1, :], (128, 512))
    bands = pltpu.roll(bands, 0, 1, stride=1, stride_axis=0).astype(BF)
    zero = jnp.zeros((128, 128), BF)
    far, mid, near = [bands[:, at : at + 128] for at in (128, 256, 384)]
    toeplitz[:, :128] = jnp.concatenate([near, mid, far, zero], 0)
    toeplitz[:, 128:] = jnp.concatenate([zero, near, mid, far], 0)


def transform(blocks, wins, chans, toeplitz, table):
    rows = []
    for halo, rec in blocks:
        rows.append(jnp.concatenate([halo, rec[:, :HALF]], 1))
        rows += [rec[:, HALF * (m - 1) : HALF * (m + 1)] for m in range(1, 2 * wins)]
    white = dot(jnp.concatenate(rows, 0), toeplitz).astype(BF)
    pieces = [
        jnp.concatenate([white[2 * w * chans : (2 * w + 1) * chans], white[(2 * w + 1) * chans : (2 * w + 2) * chans]], 1)
        for w in range(len(blocks) * wins)
    ]
    return dot(jnp.concatenate(pieces, 0), table)


def early_kernel(pairs_ref, rec_ref, taps_ref, table_ref, picked_ref, toeplitz_ref, forward_ref, row, virt):
    nblk, chans, time = rec_ref.shape
    wins = time // WLEN - 1
    nv = chans // VSTEP
    count = nblk * nv
    build_toeplitz(taps_ref, row, toeplitz_ref)
    forward_ref[...] = table_ref[...].astype(BF)
    rows = [
        rec_ref[b, r * VSTEP : (r + 1) * VSTEP, HALF:].astype(F32)[0:1] for b in range(nblk) for r in range(nv)
    ]
    rows = jnp.concatenate(rows, 0).astype(BF)
    result = transform([(rows[:, :HALF], rows[:, HALF:])], wins, count, toeplitz_ref[...], forward_ref[...])
    for b in range(nblk):
        parts = [
            result[w * count + b * nv : w * count + (b + 1) * nv, p * BINS : (p + 1) * BINS]
            for w in range(wins)
            for p in range(2)
        ]
        virt[b] = jnp.concatenate(parts, 0).astype(BF)
    for r in range(nblk):
        for k in range(SLOTS):
            picked_ref[r, k] = virt[pairs_ref[r, k]]


def early(records, taps, pairs):
    nblk, chans, time = records.shape
    rows = (time // WLEN - 1) * 2 * (chans // VSTEP)
    smem, vmem = pl.BlockSpec(memory_space=pltpu.SMEM), pl.BlockSpec(memory_space=pltpu.VMEM)
    return pl.pallas_call(
        early_kernel,
        in_specs=[smem, vmem, vmem, vmem],
        out_specs=[vmem] * 3,
        out_shape=[
            jax.ShapeDtypeStruct((nblk, SLOTS, rows, BINS), BF),
            jax.ShapeDtypeStruct((WLEN, HALF), BF),
            jax.ShapeDtypeStruct((WLEN, 2 * BINS), BF),
        ],
        scratch_shapes=[pltpu.VMEM((8, 512), F32), pltpu.VMEM((nblk, rows, BINS), BF)],
        compiler_params=pltpu.CompilerParams(vmem_limit_bytes=16 * MIB),
        cost_estimate=pl.CostEstimate(flops=4 * 10**8, bytes_accessed=records.size * 2, transcendentals=0),
        name="early",
    )(pairs, records, taps, jnp.asarray(dft_table()))


def spectra_kernel(sizes, pairs_ref, me_ref, rec_ref, halo_ref, toeplitz_ref, forward_ref, *refs):
    nblk, chans, time = rec_ref.shape
    wins = time // WLEN
    nv = chans // VSTEP
    outs = [refs[nblk * q : nblk * (q + 1)] for q in range(len(sizes))]
    spec, virt = refs[nblk * len(sizes) :]
    me = me_ref[0]
    per = 2
    for m in range(0, nblk, per):
        blocks = [(halo_ref[me ^ (m + u)], rec_ref[me ^ (m + u)]) for u in range(per)]
        result = transform(blocks, wins, chans, toeplitz_ref[...], forward_ref[...])
        for u in range(per):
            at = u * wins * chans
            for p in range(2):
                spec[u, p] = result[at : at + chans, p * BINS : (p + 1) * BINS]
            chosen = [spec[u, p, pl.ds(0, nv, stride=VSTEP), :] for p in range(2)]
            virt[me ^ (m + u)] = jnp.concatenate(chosen, 0).astype(BF)
        result = result.astype(BF)
        for u in range(per):
            for w in range(wins):
                for p in range(2):
                    lo = (u * wins + w) * chans
                    for out, size in zip(outs, sizes):
                        at = (w * 2 + p) * size
                        out[m + u][at : at + size] = result[lo : lo + size, p * BINS : (p + 1) * BINS]
                        lo += size
    at = wins * 2 * sizes[0]
    for m in range(nblk):
        for k in range(SLOTS):
            lo = at + k * 2 * nv
            outs[0][m][lo : lo + 2 * nv] = virt[pairs_ref[me ^ m, k]]


def spectra(records, halo, toeplitz, forward, pairs, me, sizes):
    nblk, chans, time = records.shape
    wins = time // WLEN
    nv = chans // VSTEP
    shapes = []
    for q, size in enumerate(sizes):
        shapes += [(wins * 2 * size + (SLOTS * 2 * nv if q == 0 else 0), BINS)] * nblk
    smem, vmem = pl.BlockSpec(memory_space=pltpu.SMEM), pl.BlockSpec(memory_space=pltpu.VMEM)
    outs = pl.pallas_call(
        lambda *refs: spectra_kernel(sizes, *refs),
        in_specs=[smem, smem, vmem, vmem, vmem, vmem],
        out_specs=[vmem] * len(shapes),
        out_shape=[jax.ShapeDtypeStruct(shape, BF) for shape in shapes],
        scratch_shapes=[pltpu.VMEM((2, 2, chans, BINS), F32), pltpu.VMEM((nblk, 2 * nv, BINS), BF)],
        compiler_params=pltpu.CompilerParams(vmem_limit_bytes=16 * MIB),
        cost_estimate=pl.CostEstimate(
            flops=nblk * chans * wins * 3 * 2 * 512 * 256, bytes_accessed=nblk * chans * time * 3, transcendentals=0
        ),
        name="spectra",
    )(pairs, me, records, halo, toeplitz, forward)
    return [list(outs[i : i + nblk]) for i in range(0, len(outs), nblk)]


def collect_kernel(rows, *refs):
    out_ref = refs[-1]
    for m, ref in enumerate(refs[:-1]):
        at = ref.shape[0] - SLOTS * rows
        for k in range(SLOTS):
            out_ref[m, k] = ref[at + k * rows : at + (k + 1) * rows]


def collect(chunks, rows):
    vmem = pl.BlockSpec(memory_space=pltpu.VMEM)
    return pl.pallas_call(
        lambda *refs: collect_kernel(rows, *refs),
        in_specs=[vmem] * len(chunks),
        out_specs=vmem,
        out_shape=jax.ShapeDtypeStruct((len(chunks), SLOTS, rows, BINS), BF),
        compiler_params=pltpu.CompilerParams(vmem_limit_bytes=8 * MIB),
        cost_estimate=pl.CostEstimate(flops=0, bytes_accessed=len(chunks) * rows * 2048, transcendentals=0),
        name="collect",
    )(*chunks)


def sources_kernel(nsrc, nnar, wins, nv, me_ref, place_ref, *refs):
    lates, firsts = refs[:nnar], refs[nnar : 2 * nnar]
    out_ref, late, first, turned = refs[2 * nnar :]
    nw = nsrc * wins
    pitch = BINS + 8
    for n in range(nnar):
        late[place_ref[0] ^ n] = lates[n][...]
        first[place_ref[0] ^ n] = firsts[n][...]

    def turn(src, carry):
        after = [[late[n, src, k].astype(F32) for n in range(nnar)] for k in range(SLOTS)]
        start = [[first[n, me_ref[0] ^ src, k].astype(F32) for n in range(nnar)] for k in range(SLOTS)]
        for w in range(wins):
            held = after if w else start
            for p in range(2):
                at = (max(w - 1, 0) * 2 + p) * nv
                tile = jnp.concatenate([held[k][n][at : at + nv] for k in range(SLOTS) for n in range(nnar)], 0)
                row = pl.multiple_of((p * nw + src * wins + w) * pitch, 8)
                turned[pl.ds(row, BINS), :] = tile.T
        return carry

    lax.fori_loop(0, nsrc, turn, 0, unroll=4)

    def one(j, carry):
        re = turned[pl.ds(j, nw, stride=pitch), :]
        im = turned[pl.ds(nw * pitch + j, nw, stride=pitch), :]
        top = jnp.concatenate([re, -im], 1)
        low = jnp.concatenate([im, re], 1)
        out_ref[j] = jnp.concatenate([top, low], 0).astype(BF)
        return carry

    lax.fori_loop(0, BINS, one, 0, unroll=8)


def sources(lates, firsts, me, place, wins, nv):
    nnar, nsrc = len(lates), lates[0].shape[0]
    nw = nsrc * wins
    width = SLOTS * nnar * nv
    smem, vmem = pl.BlockSpec(memory_space=pltpu.SMEM), pl.BlockSpec(memory_space=pltpu.VMEM)
    return pl.pallas_call(
        lambda *refs: sources_kernel(nsrc, nnar, wins, nv, *refs),
        in_specs=[smem, smem] + [vmem] * (2 * nnar),
        out_specs=vmem,
        out_shape=jax.ShapeDtypeStruct((BINS, 2 * nw, 2 * width), BF),
        scratch_shapes=[
            pltpu.VMEM((nnar,) + lates[0].shape, BF),
            pltpu.VMEM((nnar,) + firsts[0].shape, BF),
            pltpu.VMEM((2 * nw * (BINS + 8), width), F32),
        ],
        compiler_params=pltpu.CompilerParams(vmem_limit_bytes=(10 + 2 * nw * BINS * width * 6 // MIB) * MIB),
        cost_estimate=pl.CostEstimate(flops=10**8, bytes_accessed=8 * nnar * lates[0].size, transcendentals=0),
        name="sources",
    )(me, place, *lates, *firsts)


def stack_kernel(nw, wins, size, group, count_ref, me_ref, *refs):
    nsrc = nw // wins
    recvs, src_ref, lag_ref = refs[:nsrc], refs[nsrc], refs[nsrc + 1]
    out_ref, lag, wide, turned, cross = refs[-5:]
    step = pl.program_id(0)
    width = SLOTS * VIRTUAL_SOURCES
    depth = 2 * nw
    pack = src_ref.shape[1] // depth
    full = pack * depth
    pitch, bpitch = size + 8, BINS + 8

    @pl.when(step == 0)
    def _():
        lag[...] = lag_ref[...].astype(BF)
        for m in range(nsrc):
            src = me_ref[0] ^ m
            for w in range(wins):
                for p in range(2):
                    row = pl.multiple_of((p * nw + src * wins + w) * pitch, 8)
                    at = (w * 2 + p) * size
                    wide[pl.ds(row, size), :] = recvs[m][at : at + size].astype(F32)

        def turn(i, carry):
            flat = wide[pl.ds(i, depth, stride=pitch), :]
            flat = jnp.concatenate([flat] * pack, 0).T
            if pack > 1:
                flat = jnp.where(own, flat, 0.0)
            for c in range(0, full, 128):
                part = flat[:, c : min(c + 128, full)]
                turned[c // 128, pl.ds(pl.multiple_of(i * bpitch, 8), BINS), 0 : part.shape[1]] = part
            return carry

        shape = (BINS, full)
        own = lax.broadcasted_iota(jnp.int32, shape, 0) % pack == lax.broadcasted_iota(jnp.int32, shape, 1) // depth
        lax.fori_loop(0, size, turn, 0, unroll=8)
        slot = lax.broadcasted_iota(jnp.int32, (1, 2 * width), 1) % width // VIRTUAL_SOURCES
        scale = jnp.where(slot < count_ref[0], 1.0 / math.sqrt(nw), 0.0).astype(F32)

        def one(j, carry):
            rows = []
            for u in range(pack):
                at = pl.ds(j * pack + u, size, stride=bpitch)
                rows.append(jnp.concatenate([turned[c, at, :] for c in range(turned.shape[0])], 1))
            left = jnp.concatenate(rows, 0)[:, :full].astype(BF)
            value = dot(left, src_ref[j]) * scale
            for u in range(pack):
                at = pl.ds(pl.multiple_of((j * pack + u) * pitch, 8), size)
                for p in range(2):
                    cross[p, at, :] = value[u * size : (u + 1) * size, p * width : (p + 1) * width]
            return carry

        lax.fori_loop(0, BINS // pack, one, 0, unroll=8 // pack)

    rows = 2
    for q in range(0, group, rows):
        lefts = []
        for u in range(rows):
            at = step * group + q + u
            tiles = [cross[p, pl.ds(at, BINS, stride=pitch), :].astype(BF).T for p in range(2)]
            lefts.append(jnp.concatenate(tiles, 1))
        value = dot(jnp.concatenate(lefts, 0), lag[...]).astype(BF)
        for u in range(rows):
            for k in range(SLOTS):
                at = u * width + k * VIRTUAL_SOURCES
                out_ref[0, k, q + u] = value[at : at + VIRTUAL_SOURCES]


def stack(recvs, table, count, me, lag, before, start, size, wins, chans):
    nsrc = len(recvs)
    nw = nsrc * wins
    group = 16
    pack = 2 if 4 * nw <= 128 else 1
    table = table.reshape(BINS // pack, pack * 2 * nw, table.shape[2])
    shape = (1, SLOTS, chans, VIRTUAL_SOURCES, LAG_COUNT)
    first = start // group
    operands = [count, me, *recvs, table, lag]
    in_specs = [pl.BlockSpec(recv.shape, lambda t, c, e: (0, 0)) for recv in recvs] + [
        pl.BlockSpec(table.shape, lambda t, c, e: (0,) * 3),
        pl.BlockSpec(lag.shape, lambda t, c, e: (0, 0)),
    ]
    aliases = {}
    if before is not None:
        operands.append(before)
        in_specs.append(pl.BlockSpec(memory_space=pl.ANY))
        aliases = {len(operands) - 1: 0}
    return pl.pallas_call(
        lambda *refs: stack_kernel(nw, wins, size, group, *refs),
        grid_spec=pltpu.PrefetchScalarGridSpec(
            num_scalar_prefetch=2,
            grid=(size // group,),
            in_specs=in_specs,
            out_specs=pl.BlockSpec(
                (1, SLOTS, group, VIRTUAL_SOURCES, LAG_COUNT), lambda t, c, e: (0, 0, first + t, 0, 0)
            ),
            scratch_shapes=[
                pltpu.VMEM(lag.shape, BF),
                pltpu.VMEM((2 * nw * (size + 8), BINS), F32),
                pltpu.VMEM((-(-2 * nw * pack // 128), size * (BINS + 8), 128), F32),
                pltpu.VMEM((2, BINS * (size + 8), SLOTS * VIRTUAL_SOURCES), F32),
            ],
        ),
        out_shape=jax.ShapeDtypeStruct(shape, BF),
        input_output_aliases=aliases,
        compiler_params=pltpu.CompilerParams(vmem_limit_bytes=(20 + table.size * 4 // MIB) * MIB),
        cost_estimate=pl.CostEstimate(
            flops=size * 128 * 256 * 256 * 4, bytes_accessed=2 * (table.size + size * 32768), transcendentals=0
        ),
        name="stack",
    )(*operands)


def swap(value, axis, mask):
    return lax.ppermute(value, axis, [(i, i ^ mask) for i in range(lax.axis_size(axis))])


def after(value, others):
    return lax.optimization_barrier((value, others))[0] if others else value


def on_device(records, taps, pair_sources, pair_counts):
    nblk, chans, time = records.shape
    wins = time // WLEN
    nv = chans // VSTEP
    nwide, nnar = lax.axis_size("wide"), lax.axis_size("narrow")
    sizes = (chans // 2,) * 2
    me = lax.axis_index("wide").astype(jnp.int32)[None]
    place = lax.axis_index("narrow").astype(jnp.int32)[None]
    halo = lax.ppermute(records[:, :, time - HALF :], "wide", [(i, i + 1) for i in range(nwide - 1)])
    picked, toeplitz, forward = early(records, taps[None], pair_sources)
    picked = lax.all_to_all(picked, "wide", split_axis=0, concat_axis=0, tiled=True)
    chunks = spectra(records, halo, toeplitz, forward, pair_sources, me, sizes)
    picked, (near, far) = lax.optimization_barrier((picked, chunks))
    order = list(range(nwide - 1, 0, -1))

    def gather(value):
        return [value] + [swap(value, "narrow", n) for n in range(nnar - 1, 0, -1)][::-1]

    lates = gather(picked)
    for i, m in enumerate(order):
        near[m] = swap(after(near[m], lates[1:] if i >= len(order) - 2 else []), "wide", m)
    firsts = gather(collect(near, 2 * nv))
    for m in order:
        far[m] = swap(after(far[m], firsts[1:]), "wide", m)
    table = sources(lates, firsts, me, place, wins, nv)
    lag = jnp.asarray(lag_table())
    out, start = None, 0
    for recvs, size in zip((near, far), sizes):
        out = stack(recvs, table, pair_counts, me, lag, out, start, size, wins, chans)
        start += size
    return out


def solution(mesh):
    return jax.shard_map(
        on_device,
        mesh=mesh,
        in_specs=(P(None, "narrow", "wide"), P(), P(), P("wide")),
        out_specs=P("wide", None, "narrow", None, None),
        check_vma=False,
    )
```

```python
import math

import jax
import jax.numpy as jnp
import numpy as np
from jax import lax
from jax.experimental import pallas as pl
from jax.experimental.pallas import tpu as pltpu
from jax.sharding import PartitionSpec as P

BLOCK_CHANNELS = 512
VIRTUAL_SOURCES = 32
VSTEP = BLOCK_CHANNELS // VIRTUAL_SOURCES
TAPS = 201
WLEN = 512
HALF = 256
BINS = 128
F_LO = 4
LAG_COUNT = 256
SLOTS = 4
BF = jnp.bfloat16
F32 = jnp.float32
MIB = 1 << 20


def dft_table():
    times = np.arange(WLEN, dtype=np.int32)[:, None]
    bins = (F_LO + np.arange(BINS, dtype=np.int32))[None, :]
    angle = np.mod(times * bins, WLEN).astype(np.float32) * np.float32(2.0 * math.pi / WLEN)
    scale = np.float32(1.0 / math.sqrt(WLEN))
    return np.concatenate([np.cos(angle) * scale, -np.sin(angle) * scale], 1).astype(BF).astype(np.float32)


def lag_table():
    bins = (F_LO + np.arange(BINS, dtype=np.int32))[:, None]
    lags = (np.arange(LAG_COUNT, dtype=np.int32) - LAG_COUNT // 2)[None, :]
    angle = np.mod(bins * lags, WLEN).astype(np.float32) * np.float32(2.0 * math.pi / WLEN)
    scale = np.float32(1.0 / math.sqrt(BINS))
    return np.concatenate([np.cos(angle) * scale, -np.sin(angle) * scale], 0).astype(BF).astype(np.float32)


def dot(a, b):
    return lax.dot_general(a, b, (((1,), (0,)), ((), ())), preferred_element_type=F32)


def build_toeplitz(taps_ref, row, toeplitz):
    row[...] = jnp.zeros_like(row)
    row[:, 128 : 128 + TAPS] = jnp.broadcast_to(taps_ref[...].astype(BF).astype(F32), (8, TAPS))
    bands = jnp.broadcast_to(row[0:1, :], (128, 512))
    bands = pltpu.roll(bands, 0, 1, stride=1, stride_axis=0).astype(BF)
    zero = jnp.zeros((128, 128), BF)
    far, mid, near = [bands[:, at : at + 128] for at in (128, 256, 384)]
    toeplitz[:, :128] = jnp.concatenate([near, mid, far, zero], 0)
    toeplitz[:, 128:] = jnp.concatenate([zero, near, mid, far], 0)


def transform(blocks, wins, chans, toeplitz, table):
    rows = []
    for halo, rec in blocks:
        rows.append(jnp.concatenate([halo, rec[:, :HALF]], 1))
        rows += [rec[:, HALF * (m - 1) : HALF * (m + 1)] for m in range(1, 2 * wins)]
    white = dot(jnp.concatenate(rows, 0), toeplitz).astype(BF)
    pieces = [
        jnp.concatenate([white[2 * w * chans : (2 * w + 1) * chans], white[(2 * w + 1) * chans : (2 * w + 2) * chans]], 1)
        for w in range(len(blocks) * wins)
    ]
    return dot(jnp.concatenate(pieces, 0), table)


def early_kernel(pairs_ref, rec_ref, taps_ref, table_ref, picked_ref, toeplitz_ref, forward_ref, row, virt):
    nblk, chans, time = rec_ref.shape
    wins = time // WLEN - 1
    nv = chans // VSTEP
    count = nblk * nv
    build_toeplitz(taps_ref, row, toeplitz_ref)
    forward_ref[...] = table_ref[...].astype(BF)
    rows = [
        rec_ref[b, r * VSTEP : (r + 1) * VSTEP, HALF:].astype(F32)[0:1] for b in range(nblk) for r in range(nv)
    ]
    rows = jnp.concatenate(rows, 0).astype(BF)
    result = transform([(rows[:, :HALF], rows[:, HALF:])], wins, count, toeplitz_ref[...], forward_ref[...])
    for b in range(nblk):
        parts = [
            result[w * count + b * nv : w * count + (b + 1) * nv, p * BINS : (p + 1) * BINS]
            for w in range(wins)
            for p in range(2)
        ]
        virt[b] = jnp.concatenate(parts, 0).astype(BF)
    for r in range(nblk):
        for k in range(SLOTS):
            picked_ref[r, k] = virt[pairs_ref[r, k]]


def early(records, taps, pairs):
    nblk, chans, time = records.shape
    rows = (time // WLEN - 1) * 2 * (chans // VSTEP)
    smem, vmem = pl.BlockSpec(memory_space=pltpu.SMEM), pl.BlockSpec(memory_space=pltpu.VMEM)
    return pl.pallas_call(
        early_kernel,
        in_specs=[smem, vmem, vmem, vmem],
        out_specs=[vmem] * 3,
        out_shape=[
            jax.ShapeDtypeStruct((nblk, SLOTS, rows, BINS), BF),
            jax.ShapeDtypeStruct((WLEN, HALF), BF),
            jax.ShapeDtypeStruct((WLEN, 2 * BINS), BF),
        ],
        scratch_shapes=[pltpu.VMEM((8, 512), F32), pltpu.VMEM((nblk, rows, BINS), BF)],
        compiler_params=pltpu.CompilerParams(vmem_limit_bytes=16 * MIB),
        cost_estimate=pl.CostEstimate(flops=4 * 10**8, bytes_accessed=records.size * 2, transcendentals=0),
        name="early",
    )(pairs, records, taps, jnp.asarray(dft_table()))


def spectra_kernel(sizes, pairs_ref, me_ref, rec_ref, halo_ref, toeplitz_ref, forward_ref, *refs):
    nblk, chans, time = rec_ref.shape
    wins = time // WLEN
    nv = chans // VSTEP
    outs = [refs[nblk * q : nblk * (q + 1)] for q in range(len(sizes))]
    spec, virt = refs[nblk * len(sizes) :]
    me = me_ref[0]
    per = 2
    for m in range(0, nblk, per):
        blocks = [(halo_ref[me ^ (m + u)], rec_ref[me ^ (m + u)]) for u in range(per)]
        result = transform(blocks, wins, chans, toeplitz_ref[...], forward_ref[...])
        for u in range(per):
            at = u * wins * chans
            for p in range(2):
                spec[u, p] = result[at : at + chans, p * BINS : (p + 1) * BINS]
            chosen = [spec[u, p, pl.ds(0, nv, stride=VSTEP), :] for p in range(2)]
            virt[me ^ (m + u)] = jnp.concatenate(chosen, 0).astype(BF)
        result = result.astype(BF)
        for u in range(per):
            for w in range(wins):
                for p in range(2):
                    lo = (u * wins + w) * chans
                    for out, size in zip(outs, sizes):
                        at = (w * 2 + p) * size
                        out[m + u][at : at + size] = result[lo : lo + size, p * BINS : (p + 1) * BINS]
                        lo += size
    at = wins * 2 * sizes[0]
    for m in range(nblk):
        for k in range(SLOTS):
            lo = at + k * 2 * nv
            outs[0][m][lo : lo + 2 * nv] = virt[pairs_ref[me ^ m, k]]


def spectra(records, halo, toeplitz, forward, pairs, me, sizes):
    nblk, chans, time = records.shape
    wins = time // WLEN
    nv = chans // VSTEP
    shapes = []
    for q, size in enumerate(sizes):
        shapes += [(wins * 2 * size + (SLOTS * 2 * nv if q == 0 else 0), BINS)] * nblk
    smem, vmem = pl.BlockSpec(memory_space=pltpu.SMEM), pl.BlockSpec(memory_space=pltpu.VMEM)
    outs = pl.pallas_call(
        lambda *refs: spectra_kernel(sizes, *refs),
        in_specs=[smem, smem, vmem, vmem, vmem, vmem],
        out_specs=[vmem] * len(shapes),
        out_shape=[jax.ShapeDtypeStruct(shape, BF) for shape in shapes],
        scratch_shapes=[pltpu.VMEM((2, 2, chans, BINS), F32), pltpu.VMEM((nblk, 2 * nv, BINS), BF)],
        compiler_params=pltpu.CompilerParams(vmem_limit_bytes=16 * MIB),
        cost_estimate=pl.CostEstimate(
            flops=nblk * chans * wins * 3 * 2 * 512 * 256, bytes_accessed=nblk * chans * time * 3, transcendentals=0
        ),
        name="spectra",
    )(pairs, me, records, halo, toeplitz, forward)
    return [list(outs[i : i + nblk]) for i in range(0, len(outs), nblk)]


def collect_kernel(rows, *refs):
    out_ref = refs[-1]
    for m, ref in enumerate(refs[:-1]):
        at = ref.shape[0] - SLOTS * rows
        for k in range(SLOTS):
            out_ref[m, k] = ref[at + k * rows : at + (k + 1) * rows]


def collect(chunks, rows):
    vmem = pl.BlockSpec(memory_space=pltpu.VMEM)
    return pl.pallas_call(
        lambda *refs: collect_kernel(rows, *refs),
        in_specs=[vmem] * len(chunks),
        out_specs=vmem,
        out_shape=jax.ShapeDtypeStruct((len(chunks), SLOTS, rows, BINS), BF),
        compiler_params=pltpu.CompilerParams(vmem_limit_bytes=8 * MIB),
        cost_estimate=pl.CostEstimate(flops=0, bytes_accessed=len(chunks) * rows * 2048, transcendentals=0),
        name="collect",
    )(*chunks)


def sources_kernel(nsrc, nnar, wins, nv, me_ref, place_ref, *refs):
    lates, firsts = refs[:nnar], refs[nnar : 2 * nnar]
    out_ref, late, first, turned = refs[2 * nnar :]
    nw = nsrc * wins
    pitch = BINS + 8
    for n in range(nnar):
        late[place_ref[0] ^ n] = lates[n][...]
        first[place_ref[0] ^ n] = firsts[n][...]

    def turn(src, carry):
        after = [[late[n, src, k].astype(F32) for n in range(nnar)] for k in range(SLOTS)]
        start = [[first[n, me_ref[0] ^ src, k].astype(F32) for n in range(nnar)] for k in range(SLOTS)]
        for w in range(wins):
            held = after if w else start
            for p in range(2):
                at = (max(w - 1, 0) * 2 + p) * nv
                tile = jnp.concatenate([held[k][n][at : at + nv] for k in range(SLOTS) for n in range(nnar)], 0)
                row = pl.multiple_of((p * nw + src * wins + w) * pitch, 8)
                turned[pl.ds(row, BINS), :] = tile.T
        return carry

    lax.fori_loop(0, nsrc, turn, 0, unroll=4)

    def one(j, carry):
        re = turned[pl.ds(j, nw, stride=pitch), :]
        im = turned[pl.ds(nw * pitch + j, nw, stride=pitch), :]
        top = jnp.concatenate([re, -im], 1)
        low = jnp.concatenate([im, re], 1)
        out_ref[j] = jnp.concatenate([top, low], 0).astype(BF)
        return carry

    lax.fori_loop(0, BINS, one, 0, unroll=8)


def sources(lates, firsts, me, place, wins, nv):
    nnar, nsrc = len(lates), lates[0].shape[0]
    nw = nsrc * wins
    width = SLOTS * nnar * nv
    smem, vmem = pl.BlockSpec(memory_space=pltpu.SMEM), pl.BlockSpec(memory_space=pltpu.VMEM)
    return pl.pallas_call(
        lambda *refs: sources_kernel(nsrc, nnar, wins, nv, *refs),
        in_specs=[smem, smem] + [vmem] * (2 * nnar),
        out_specs=vmem,
        out_shape=jax.ShapeDtypeStruct((BINS, 2 * nw, 2 * width), BF),
        scratch_shapes=[
            pltpu.VMEM((nnar,) + lates[0].shape, BF),
            pltpu.VMEM((nnar,) + firsts[0].shape, BF),
            pltpu.VMEM((2 * nw * (BINS + 8), width), F32),
        ],
        compiler_params=pltpu.CompilerParams(vmem_limit_bytes=(10 + 2 * nw * BINS * width * 6 // MIB) * MIB),
        cost_estimate=pl.CostEstimate(flops=10**8, bytes_accessed=8 * nnar * lates[0].size, transcendentals=0),
        name="sources",
    )(me, place, *lates, *firsts)


def stack_kernel(nw, wins, size, group, count_ref, me_ref, *refs):
    nsrc = nw // wins
    recvs, src_ref, lag_ref = refs[:nsrc], refs[nsrc], refs[nsrc + 1]
    out_ref, lag, wide, turned, cross = refs[-5:]
    step = pl.program_id(0)
    width = SLOTS * VIRTUAL_SOURCES
    depth = 2 * nw
    pack = src_ref.shape[1] // depth
    full = pack * depth
    pitch, bpitch = size + 8, BINS + 8

    @pl.when(step == 0)
    def _():
        lag[...] = lag_ref[...].astype(BF)
        for m in range(nsrc):
            src = me_ref[0] ^ m
            for w in range(wins):
                for p in range(2):
                    row = pl.multiple_of((p * nw + src * wins + w) * pitch, 8)
                    at = (w * 2 + p) * size
                    wide[pl.ds(row, size), :] = recvs[m][at : at + size].astype(F32)

        def turn(i, carry):
            flat = wide[pl.ds(i, depth, stride=pitch), :]
            flat = jnp.concatenate([flat] * pack, 0).T
            if pack > 1:
                flat = jnp.where(own, flat, 0.0)
            for c in range(0, full, 128):
                part = flat[:, c : min(c + 128, full)]
                turned[c // 128, pl.ds(pl.multiple_of(i * bpitch, 8), BINS), 0 : part.shape[1]] = part
            return carry

        shape = (BINS, full)
        own = lax.broadcasted_iota(jnp.int32, shape, 0) % pack == lax.broadcasted_iota(jnp.int32, shape, 1) // depth
        lax.fori_loop(0, size, turn, 0, unroll=8)
        slot = lax.broadcasted_iota(jnp.int32, (1, 2 * width), 1) % width // VIRTUAL_SOURCES
        scale = jnp.where(slot < count_ref[0], 1.0 / math.sqrt(nw), 0.0).astype(F32)

        def one(j, carry):
            rows = []
            for u in range(pack):
                at = pl.ds(j * pack + u, size, stride=bpitch)
                rows.append(jnp.concatenate([turned[c, at, :] for c in range(turned.shape[0])], 1))
            left = jnp.concatenate(rows, 0)[:, :full].astype(BF)
            value = dot(left, src_ref[j]) * scale
            for u in range(pack):
                at = pl.ds(pl.multiple_of((j * pack + u) * pitch, 8), size)
                for p in range(2):
                    cross[p, at, :] = value[u * size : (u + 1) * size, p * width : (p + 1) * width]
            return carry

        lax.fori_loop(0, BINS // pack, one, 0, unroll=8 // pack)

    rows = 4
    for q in range(0, group, rows):
        lefts = []
        for u in range(rows):
            at = step * group + q + u
            tiles = [cross[p, pl.ds(at, BINS, stride=pitch), :].astype(BF).T for p in range(2)]
            lefts.append(jnp.concatenate(tiles, 1))
        value = dot(jnp.concatenate(lefts, 0), lag[...]).astype(BF)
        for u in range(rows):
            for k in range(SLOTS):
                at = u * width + k * VIRTUAL_SOURCES
                out_ref[0, k, q + u] = value[at : at + VIRTUAL_SOURCES]


def stack(recvs, table, count, me, lag, before, start, size, wins, chans):
    nsrc = len(recvs)
    nw = nsrc * wins
    group = 16
    pack = 2 if 4 * nw <= 128 else 1
    table = table.reshape(BINS // pack, pack * 2 * nw, table.shape[2])
    shape = (1, SLOTS, chans, VIRTUAL_SOURCES, LAG_COUNT)
    first = start // group
    operands = [count, me, *recvs, table, lag]
    in_specs = [pl.BlockSpec(recv.shape, lambda t, c, e: (0, 0)) for recv in recvs] + [
        pl.BlockSpec(table.shape, lambda t, c, e: (0,) * 3),
        pl.BlockSpec(lag.shape, lambda t, c, e: (0, 0)),
    ]
    aliases = {}
    if before is not None:
        operands.append(before)
        in_specs.append(pl.BlockSpec(memory_space=pl.ANY))
        aliases = {len(operands) - 1: 0}
    return pl.pallas_call(
        lambda *refs: stack_kernel(nw, wins, size, group, *refs),
        grid_spec=pltpu.PrefetchScalarGridSpec(
            num_scalar_prefetch=2,
            grid=(size // group,),
            in_specs=in_specs,
            out_specs=pl.BlockSpec(
                (1, SLOTS, group, VIRTUAL_SOURCES, LAG_COUNT), lambda t, c, e: (0, 0, first + t, 0, 0)
            ),
            scratch_shapes=[
                pltpu.VMEM(lag.shape, BF),
                pltpu.VMEM((2 * nw * (size + 8), BINS), F32),
                pltpu.VMEM((-(-2 * nw * pack // 128), size * (BINS + 8), 128), F32),
                pltpu.VMEM((2, BINS * (size + 8), SLOTS * VIRTUAL_SOURCES), F32),
            ],
        ),
        out_shape=jax.ShapeDtypeStruct(shape, BF),
        input_output_aliases=aliases,
        compiler_params=pltpu.CompilerParams(vmem_limit_bytes=(20 + table.size * 4 // MIB) * MIB),
        cost_estimate=pl.CostEstimate(
            flops=size * 128 * 256 * 256 * 4, bytes_accessed=2 * (table.size + size * 32768), transcendentals=0
        ),
        name="stack",
    )(*operands)


def swap(value, axis, mask):
    return lax.ppermute(value, axis, [(i, i ^ mask) for i in range(lax.axis_size(axis))])


def after(value, others):
    return lax.optimization_barrier((value, others))[0] if others else value


def on_device(records, taps, pair_sources, pair_counts):
    nblk, chans, time = records.shape
    wins = time // WLEN
    nv = chans // VSTEP
    nwide, nnar = lax.axis_size("wide"), lax.axis_size("narrow")
    sizes = (chans // 2,) * 2
    me = lax.axis_index("wide").astype(jnp.int32)[None]
    place = lax.axis_index("narrow").astype(jnp.int32)[None]
    halo = lax.ppermute(records[:, :, time - HALF :], "wide", [(i, i + 1) for i in range(nwide - 1)])
    picked, toeplitz, forward = early(records, taps[None], pair_sources)
    picked = lax.all_to_all(picked, "wide", split_axis=0, concat_axis=0, tiled=True)
    chunks = spectra(records, halo, toeplitz, forward, pair_sources, me, sizes)
    picked, (near, far) = lax.optimization_barrier((picked, chunks))
    order = list(range(nwide - 1, 0, -1))

    def gather(value):
        return [value] + [swap(value, "narrow", n) for n in range(nnar - 1, 0, -1)][::-1]

    lates = gather(picked)
    for i, m in enumerate(order):
        near[m] = swap(after(near[m], lates[1:] if i >= len(order) - 2 else []), "wide", m)
    for i, m in enumerate(order):
        far[m] = swap(after(far[m], [near[order[min(i + 2, nwide - 2)]]]), "wide", m)
    firsts = gather(after(collect(near, 2 * nv), [far[n] for n in order[:2]]))
    table = sources(lates, firsts, me, place, wins, nv)
    lag = jnp.asarray(lag_table())
    out, start = None, 0
    for recvs, size in zip((near, far), sizes):
        out = stack(recvs, table, pair_counts, me, lag, out, start, size, wins, chans)
        start += size
    return out


def solution(mesh):
    return jax.shard_map(
        on_device,
        mesh=mesh,
        in_specs=(P(None, "narrow", "wide"), P(), P(), P("wide")),
        out_specs=P("wide", None, "narrow", None, None),
        check_vma=False,
    )
```

```python
import math

import jax
import jax.numpy as jnp
import numpy as np
from jax import lax
from jax.experimental import pallas as pl
from jax.experimental.pallas import tpu as pltpu
from jax.sharding import PartitionSpec as P

BLOCK_CHANNELS = 512
VIRTUAL_SOURCES = 32
VSTEP = BLOCK_CHANNELS // VIRTUAL_SOURCES
TAPS = 201
WLEN = 512
HALF = 256
BINS = 128
F_LO = 4
LAG_COUNT = 256
SLOTS = 4
BF = jnp.bfloat16
F32 = jnp.float32
MIB = 1 << 20


def dft_table():
    times = np.arange(WLEN, dtype=np.int32)[:, None]
    bins = (F_LO + np.arange(BINS, dtype=np.int32))[None, :]
    angle = np.mod(times * bins, WLEN).astype(np.float32) * np.float32(2.0 * math.pi / WLEN)
    scale = np.float32(1.0 / math.sqrt(WLEN))
    return np.concatenate([np.cos(angle) * scale, -np.sin(angle) * scale], 1).astype(BF).astype(np.float32)


def lag_table():
    bins = (F_LO + np.arange(BINS, dtype=np.int32))[:, None]
    lags = (np.arange(LAG_COUNT, dtype=np.int32) - LAG_COUNT // 2)[None, :]
    angle = np.mod(bins * lags, WLEN).astype(np.float32) * np.float32(2.0 * math.pi / WLEN)
    scale = np.float32(1.0 / math.sqrt(BINS))
    return np.concatenate([np.cos(angle) * scale, -np.sin(angle) * scale], 0).astype(BF).astype(np.float32)


def dot(a, b):
    return lax.dot_general(a, b, (((1,), (0,)), ((), ())), preferred_element_type=F32)


def build_toeplitz(taps_ref, row, toeplitz):
    row[...] = jnp.zeros_like(row)
    row[:, 128 : 128 + TAPS] = jnp.broadcast_to(taps_ref[...].astype(BF).astype(F32), (8, TAPS))
    bands = jnp.broadcast_to(row[0:1, :], (128, 512))
    bands = pltpu.roll(bands, 0, 1, stride=1, stride_axis=0).astype(BF)
    zero = jnp.zeros((128, 128), BF)
    far, mid, near = [bands[:, at : at + 128] for at in (128, 256, 384)]
    toeplitz[:, :128] = jnp.concatenate([near, mid, far, zero], 0)
    toeplitz[:, 128:] = jnp.concatenate([zero, near, mid, far], 0)


def transform(blocks, wins, chans, toeplitz, table):
    rows = []
    for halo, rec in blocks:
        rows.append(jnp.concatenate([halo, rec[:, :HALF]], 1))
        rows += [rec[:, HALF * (m - 1) : HALF * (m + 1)] for m in range(1, 2 * wins)]
    white = dot(jnp.concatenate(rows, 0), toeplitz).astype(BF)
    pieces = [
        jnp.concatenate([white[2 * w * chans : (2 * w + 1) * chans], white[(2 * w + 1) * chans : (2 * w + 2) * chans]], 1)
        for w in range(len(blocks) * wins)
    ]
    return dot(jnp.concatenate(pieces, 0), table)


def virtual_rows(ref, nv):
    rows = [ref[b, r * VSTEP : (r + 1) * VSTEP, :].astype(F32)[0:1] for b in range(ref.shape[0]) for r in range(nv)]
    return jnp.concatenate(rows, 0).astype(BF)


def block_rows(result, b, nv, wins, count):
    parts = [
        result[w * count + b * nv : w * count + (b + 1) * nv, p * BINS : (p + 1) * BINS]
        for w in range(wins)
        for p in range(2)
    ]
    return jnp.concatenate(parts, 0).astype(BF)


def rows_kernel(rec_ref, rows_ref, near_ref):
    time = rec_ref.shape[2]
    rows = virtual_rows(rec_ref, rec_ref.shape[1] // VSTEP)
    rows_ref[...] = rows
    near_ref[...] = rows[:, time - HALF :]


def extract(records):
    nblk, chans, time = records.shape
    count = nblk * (chans // VSTEP)
    vmem = pl.BlockSpec(memory_space=pltpu.VMEM)
    return pl.pallas_call(
        rows_kernel,
        in_specs=[vmem],
        out_specs=[vmem] * 2,
        out_shape=[jax.ShapeDtypeStruct((count, time), BF), jax.ShapeDtypeStruct((count, HALF), BF)],
        compiler_params=pltpu.CompilerParams(vmem_limit_bytes=8 * MIB),
        cost_estimate=pl.CostEstimate(flops=0, bytes_accessed=records.size, transcendentals=0),
        name="extract",
    )(records)


def virtual_kernel(nblk, pairs_ref, rows_ref, halo_ref, taps_ref, table_ref, *refs):
    picked_ref, toeplitz_ref, forward_ref, row, virt = refs
    count, time = rows_ref.shape
    nv, wins = count // nblk, time // WLEN
    build_toeplitz(taps_ref, row, toeplitz_ref)
    forward_ref[...] = table_ref[...].astype(BF)
    block = (halo_ref[...], rows_ref[...])
    result = transform([block], wins, count, toeplitz_ref[...], forward_ref[...])
    for b in range(nblk):
        virt[b] = block_rows(result, b, nv, wins, count)
    for r in range(nblk):
        for k in range(SLOTS):
            picked_ref[r, k] = virt[pairs_ref[r, k]]


def virtual(rows, halo, taps, pairs, nblk):
    count, time = rows.shape
    size = (time // WLEN) * 2 * (count // nblk)
    smem, vmem = pl.BlockSpec(memory_space=pltpu.SMEM), pl.BlockSpec(memory_space=pltpu.VMEM)
    return pl.pallas_call(
        lambda *refs: virtual_kernel(nblk, *refs),
        in_specs=[smem] + [vmem] * 4,
        out_specs=[vmem] * 3,
        out_shape=[
            jax.ShapeDtypeStruct((nblk, SLOTS, size, BINS), BF),
            jax.ShapeDtypeStruct((WLEN, HALF), BF),
            jax.ShapeDtypeStruct((WLEN, 2 * BINS), BF),
        ],
        scratch_shapes=[pltpu.VMEM((8, 512), F32), pltpu.VMEM((nblk, size, BINS), BF)],
        compiler_params=pltpu.CompilerParams(vmem_limit_bytes=16 * MIB),
        cost_estimate=pl.CostEstimate(flops=10**8, bytes_accessed=rows.size * 8, transcendentals=0),
        name="virtual",
    )(pairs, rows, halo, taps, jnp.asarray(dft_table()))


def spectra_kernel(sizes, me_ref, rec_ref, halo_ref, toeplitz_ref, forward_ref, *refs):
    nblk, chans, time = rec_ref.shape
    wins = time // WLEN
    outs = [refs[nblk * q : nblk * (q + 1)] for q in range(len(sizes))]
    me = me_ref[0]
    per = 2
    for m in range(0, nblk, per):
        blocks = [(halo_ref[me ^ (m + u)], rec_ref[me ^ (m + u)]) for u in range(per)]
        result = transform(blocks, wins, chans, toeplitz_ref[...], forward_ref[...]).astype(BF)
        for u in range(per):
            for w in range(wins):
                for p in range(2):
                    lo = (u * wins + w) * chans
                    for out, size in zip(outs, sizes):
                        row = (w * 2 + p) * size
                        out[m + u][row : row + size] = result[lo : lo + size, p * BINS : (p + 1) * BINS]
                        lo += size


def spectra(records, halo, toeplitz, forward, me, sizes):
    nblk, chans, time = records.shape
    wins = time // WLEN
    shapes = []
    for size in sizes:
        shapes += [(wins * 2 * size, BINS)] * nblk
    smem, vmem = pl.BlockSpec(memory_space=pltpu.SMEM), pl.BlockSpec(memory_space=pltpu.VMEM)
    outs = pl.pallas_call(
        lambda *refs: spectra_kernel(sizes, *refs),
        in_specs=[smem] + [vmem] * 4,
        out_specs=[vmem] * len(shapes),
        out_shape=[jax.ShapeDtypeStruct(shape, BF) for shape in shapes],
        compiler_params=pltpu.CompilerParams(vmem_limit_bytes=16 * MIB),
        cost_estimate=pl.CostEstimate(
            flops=nblk * chans * wins * 3 * 2 * 512 * 256, bytes_accessed=nblk * chans * time * 3, transcendentals=0
        ),
        name="spectra",
    )(me, records, halo, toeplitz, forward)
    return [list(outs[i : i + nblk]) for i in range(0, len(outs), nblk)]


def sources_kernel(nsrc, nnar, wins, nv, place_ref, *refs):
    virts, out_ref, held, turned = refs[:nnar], refs[nnar], refs[nnar + 1], refs[nnar + 2]
    nw = nsrc * wins
    pitch = BINS + 8
    for n in range(nnar):
        held[place_ref[0] ^ n] = virts[n][...]

    def turn(src, carry):
        tiles = [[held[n, src, k].astype(F32) for n in range(nnar)] for k in range(SLOTS)]
        for w in range(wins):
            for p in range(2):
                at = (w * 2 + p) * nv
                tile = jnp.concatenate([tiles[k][n][at : at + nv] for k in range(SLOTS) for n in range(nnar)], 0)
                row = pl.multiple_of((p * nw + src * wins + w) * pitch, 8)
                turned[pl.ds(row, BINS), :] = tile.T
        return carry

    lax.fori_loop(0, nsrc, turn, 0, unroll=4)

    def one(j, carry):
        re = turned[pl.ds(j, nw, stride=pitch), :]
        im = turned[pl.ds(nw * pitch + j, nw, stride=pitch), :]
        top = jnp.concatenate([re, -im], 1)
        low = jnp.concatenate([im, re], 1)
        out_ref[j] = jnp.concatenate([top, low], 0).astype(BF)
        return carry

    lax.fori_loop(0, BINS, one, 0, unroll=8)


def sources(virts, place, wins, nv):
    nnar, nsrc = len(virts), virts[0].shape[0]
    nw = nsrc * wins
    width = SLOTS * nnar * nv
    smem, vmem = pl.BlockSpec(memory_space=pltpu.SMEM), pl.BlockSpec(memory_space=pltpu.VMEM)
    return pl.pallas_call(
        lambda *refs: sources_kernel(nsrc, nnar, wins, nv, *refs),
        in_specs=[smem] + [vmem] * nnar,
        out_specs=vmem,
        out_shape=jax.ShapeDtypeStruct((BINS, 2 * nw, 2 * width), BF),
        scratch_shapes=[
            pltpu.VMEM((nnar,) + virts[0].shape, BF),
            pltpu.VMEM((2 * nw * (BINS + 8), width), F32),
        ],
        compiler_params=pltpu.CompilerParams(vmem_limit_bytes=(10 + 2 * nw * BINS * width * 6 // MIB) * MIB),
        cost_estimate=pl.CostEstimate(flops=10**8, bytes_accessed=8 * nnar * virts[0].size, transcendentals=0),
        name="sources",
    )(place, *virts)


def stack_kernel(nw, wins, size, group, count_ref, me_ref, *refs):
    nsrc = nw // wins
    recvs, src_ref, lag_ref = refs[:nsrc], refs[nsrc], refs[nsrc + 1]
    out_ref, lag, wide, turned, cross = refs[-5:]
    step = pl.program_id(0)
    width = SLOTS * VIRTUAL_SOURCES
    depth = 2 * nw
    pack = src_ref.shape[1] // depth
    full = pack * depth
    pitch, bpitch = size + 8, BINS + 8

    @pl.when(step == 0)
    def _():
        lag[...] = lag_ref[...].astype(BF)
        for m in range(nsrc):
            src = me_ref[0] ^ m
            for w in range(wins):
                for p in range(2):
                    row = pl.multiple_of((p * nw + src * wins + w) * pitch, 8)
                    at = (w * 2 + p) * size
                    wide[pl.ds(row, size), :] = recvs[m][at : at + size].astype(F32)

        def turn(i, carry):
            flat = wide[pl.ds(i, depth, stride=pitch), :]
            flat = jnp.concatenate([flat] * pack, 0).T
            if pack > 1:
                flat = jnp.where(own, flat, 0.0)
            for c in range(0, full, 128):
                part = flat[:, c : min(c + 128, full)]
                turned[c // 128, pl.ds(pl.multiple_of(i * bpitch, 8), BINS), 0 : part.shape[1]] = part
            return carry

        shape = (BINS, full)
        own = lax.broadcasted_iota(jnp.int32, shape, 0) % pack == lax.broadcasted_iota(jnp.int32, shape, 1) // depth
        lax.fori_loop(0, size, turn, 0, unroll=8)
        slot = lax.broadcasted_iota(jnp.int32, (1, 2 * width), 1) % width // VIRTUAL_SOURCES
        scale = jnp.where(slot < count_ref[0], 1.0 / math.sqrt(nw), 0.0).astype(F32)

        def one(j, carry):
            rows = []
            for u in range(pack):
                at = pl.ds(j * pack + u, size, stride=bpitch)
                rows.append(jnp.concatenate([turned[c, at, :] for c in range(turned.shape[0])], 1))
            left = jnp.concatenate(rows, 0)[:, :full].astype(BF)
            value = dot(left, src_ref[j]) * scale
            for u in range(pack):
                at = pl.ds(pl.multiple_of((j * pack + u) * pitch, 8), size)
                for p in range(2):
                    cross[p, at, :] = value[u * size : (u + 1) * size, p * width : (p + 1) * width]
            return carry

        lax.fori_loop(0, BINS // pack, one, 0, unroll=8 // pack)

    for q in range(0, group, 4):
        lefts = []
        for u in range(4):
            at = step * group + q + u
            tiles = [cross[p, pl.ds(at, BINS, stride=pitch), :].astype(BF).T for p in range(2)]
            lefts.append(jnp.concatenate(tiles, 1))
        value = dot(jnp.concatenate(lefts, 0), lag[...]).astype(BF)
        for u in range(4):
            for k in range(SLOTS):
                at = u * width + k * VIRTUAL_SOURCES
                out_ref[0, k, q + u] = value[at : at + VIRTUAL_SOURCES]


def stack(recvs, table, count, me, lag, before, start, size, wins, chans):
    nw = wins * len(recvs)
    group = 16
    pack = 2 if 4 * nw <= 128 else 1
    table = table.reshape(BINS // pack, pack * 2 * nw, table.shape[2])
    shape = (1, SLOTS, chans, VIRTUAL_SOURCES, LAG_COUNT)
    first = start // group
    operands = [count, me, *recvs, table, lag]
    in_specs = [pl.BlockSpec(recv.shape, lambda t, c, e: (0, 0)) for recv in recvs] + [
        pl.BlockSpec(table.shape, lambda t, c, e: (0,) * 3),
        pl.BlockSpec(lag.shape, lambda t, c, e: (0, 0)),
    ]
    aliases = {}
    if before is not None:
        operands.append(before)
        in_specs.append(pl.BlockSpec(memory_space=pl.ANY))
        aliases = {len(operands) - 1: 0}
    return pl.pallas_call(
        lambda *refs: stack_kernel(nw, wins, size, group, *refs),
        grid_spec=pltpu.PrefetchScalarGridSpec(
            num_scalar_prefetch=2,
            grid=(size // group,),
            in_specs=in_specs,
            out_specs=pl.BlockSpec(
                (1, SLOTS, group, VIRTUAL_SOURCES, LAG_COUNT), lambda t, c, e: (0, 0, first + t, 0, 0)
            ),
            scratch_shapes=[
                pltpu.VMEM(lag.shape, BF),
                pltpu.VMEM((2 * nw * (size + 8), BINS), F32),
                pltpu.VMEM((-(-2 * nw * pack // 128), size * (BINS + 8), 128), F32),
                pltpu.VMEM((2, BINS * (size + 8), SLOTS * VIRTUAL_SOURCES), F32),
            ],
        ),
        out_shape=jax.ShapeDtypeStruct(shape, BF),
        input_output_aliases=aliases,
        compiler_params=pltpu.CompilerParams(vmem_limit_bytes=(20 + table.size * 4 // MIB) * MIB),
        cost_estimate=pl.CostEstimate(
            flops=size * 128 * 256 * 256 * 4, bytes_accessed=2 * (table.size + size * 32768), transcendentals=0
        ),
        name="stack",
    )(*operands)


def swap(value, axis, mask):
    return lax.ppermute(value, axis, [(i, i ^ mask) for i in range(lax.axis_size(axis))])


def after(value, others):
    return lax.optimization_barrier((value, others))[0] if others else value


def on_device(records, taps, pair_sources, pair_counts):
    nblk, chans, time = records.shape
    wins = time // WLEN
    nv = chans // VSTEP
    nwide, nnar = lax.axis_size("wide"), lax.axis_size("narrow")
    half = chans // 2
    me = lax.axis_index("wide").astype(jnp.int32)[None]
    place = lax.axis_index("narrow").astype(jnp.int32)[None]
    ahead = [(i, i + 1) for i in range(nwide - 1)]
    order = list(range(nwide - 1, 0, -1))
    rows, tip = extract(records)
    tip = lax.ppermute(tip, "wide", ahead)
    halo = lax.ppermute(after(records[:, :, time - HALF :], [tip]), "wide", ahead)
    picked, toeplitz, forward = virtual(rows, tip, taps[None], pair_sources, nblk)
    picked = lax.all_to_all(picked, "wide", split_axis=0, concat_axis=0, tiled=True)
    chunks = spectra(records, halo, toeplitz, forward, me, (half, half))
    picked, (near, far) = lax.optimization_barrier((picked, chunks))

    top = nnar // 2
    slots = {0: picked, **{n: swap(picked, "narrow", n) for n in (top, 1) if n}}
    for i, m in enumerate(order):
        waits = []
        if i == len(order) - 2:
            waits = [slots[n] for n in sorted(slots) if n]
        near[m] = swap(after(near[m], waits), "wide", m)
    bit = top
    while bit:
        for n in sorted(slots):
            if n ^ bit not in slots:
                slots[n ^ bit] = swap(after(slots[n], [near[m] for m in order[:3]]), "narrow", bit)
        bit //= 2
    for i, m in enumerate(order):
        waits = [near[order[min(i + 2, nwide - 2)]]] + ([slots[n] for n in sorted(slots) if n] if i >= 2 else [])
        far[m] = swap(after(far[m], waits), "wide", m)
    table = sources([slots[n] for n in range(nnar)], place, wins, nv)
    lag = jnp.asarray(lag_table())
    out = stack(near, table, pair_counts, me, lag, None, 0, half, wins, chans)
    return stack(far, table, pair_counts, me, lag, out, half, half, wins, chans)


def solution(mesh):
    return jax.shard_map(
        on_device,
        mesh=mesh,
        in_specs=(P(None, "narrow", "wide"), P(), P(), P("wide")),
        out_specs=P("wide", None, "narrow", None, None),
        check_vma=False,
    )
```

```python
import math

import jax
import jax.numpy as jnp
import numpy as np
from jax import lax
from jax.experimental import pallas as pl
from jax.experimental.pallas import tpu as pltpu
from jax.sharding import PartitionSpec as P

BLOCK_CHANNELS = 512
VIRTUAL_SOURCES = 32
VSTEP = BLOCK_CHANNELS // VIRTUAL_SOURCES
TAPS = 201
WLEN = 512
HALF = 256
BINS = 128
F_LO = 4
LAG_COUNT = 256
SLOTS = 4
BF = jnp.bfloat16
F32 = jnp.float32
MIB = 1 << 20


def dft_table():
    times = np.arange(WLEN, dtype=np.int32)[:, None]
    bins = (F_LO + np.arange(BINS, dtype=np.int32))[None, :]
    angle = np.mod(times * bins, WLEN).astype(np.float32) * np.float32(2.0 * math.pi / WLEN)
    scale = np.float32(1.0 / math.sqrt(WLEN))
    return np.concatenate([np.cos(angle) * scale, -np.sin(angle) * scale], 1).astype(BF).astype(np.float32)


def lag_table():
    bins = (F_LO + np.arange(BINS, dtype=np.int32))[:, None]
    lags = (np.arange(LAG_COUNT, dtype=np.int32) - LAG_COUNT // 2)[None, :]
    angle = np.mod(bins * lags, WLEN).astype(np.float32) * np.float32(2.0 * math.pi / WLEN)
    scale = np.float32(1.0 / math.sqrt(BINS))
    return np.concatenate([np.cos(angle) * scale, -np.sin(angle) * scale], 0).astype(BF).astype(np.float32)


def dot(a, b):
    return lax.dot_general(a, b, (((1,), (0,)), ((), ())), preferred_element_type=F32)


def build_toeplitz(taps_ref, row, toeplitz):
    row[...] = jnp.zeros_like(row)
    row[:, 128 : 128 + TAPS] = jnp.broadcast_to(taps_ref[...].astype(BF).astype(F32), (8, TAPS))
    bands = jnp.broadcast_to(row[0:1, :], (128, 512))
    bands = pltpu.roll(bands, 0, 1, stride=1, stride_axis=0).astype(BF)
    zero = jnp.zeros((128, 128), BF)
    far, mid, near = [bands[:, at : at + 128] for at in (128, 256, 384)]
    toeplitz[:, :128] = jnp.concatenate([near, mid, far, zero], 0)
    toeplitz[:, 128:] = jnp.concatenate([zero, near, mid, far], 0)


def transform(blocks, wins, chans, toeplitz, table):
    rows = []
    for halo, rec in blocks:
        rows.append(jnp.concatenate([halo, rec[:, :HALF]], 1))
        rows += [rec[:, HALF * (m - 1) : HALF * (m + 1)] for m in range(1, 2 * wins)]
    white = dot(jnp.concatenate(rows, 0), toeplitz).astype(BF)
    pieces = [
        jnp.concatenate([white[2 * w * chans : (2 * w + 1) * chans], white[(2 * w + 1) * chans : (2 * w + 2) * chans]], 1)
        for w in range(len(blocks) * wins)
    ]
    return dot(jnp.concatenate(pieces, 0), table)


def virtual_rows(ref, nv):
    rows = [ref[b, r * VSTEP : (r + 1) * VSTEP, :].astype(F32)[0:1] for b in range(ref.shape[0]) for r in range(nv)]
    return jnp.concatenate(rows, 0).astype(BF)


def block_rows(result, b, nv, wins, count):
    parts = [
        result[w * count + b * nv : w * count + (b + 1) * nv, p * BINS : (p + 1) * BINS]
        for w in range(wins)
        for p in range(2)
    ]
    return jnp.concatenate(parts, 0).astype(BF)


def rows_kernel(rec_ref, rows_ref, near_ref):
    time = rec_ref.shape[2]
    rows = virtual_rows(rec_ref, rec_ref.shape[1] // VSTEP)
    rows_ref[...] = rows
    near_ref[...] = rows[:, time - HALF :]


def extract(records):
    nblk, chans, time = records.shape
    count = nblk * (chans // VSTEP)
    vmem = pl.BlockSpec(memory_space=pltpu.VMEM)
    return pl.pallas_call(
        rows_kernel,
        in_specs=[vmem],
        out_specs=[vmem] * 2,
        out_shape=[jax.ShapeDtypeStruct((count, time), BF), jax.ShapeDtypeStruct((count, HALF), BF)],
        compiler_params=pltpu.CompilerParams(vmem_limit_bytes=8 * MIB),
        cost_estimate=pl.CostEstimate(flops=0, bytes_accessed=records.size, transcendentals=0),
        name="extract",
    )(records)


def virtual_kernel(nblk, pairs_ref, rows_ref, halo_ref, taps_ref, table_ref, *refs):
    picked_ref, toeplitz_ref, forward_ref, row, virt = refs
    count, time = rows_ref.shape
    nv, wins = count // nblk, time // WLEN
    build_toeplitz(taps_ref, row, toeplitz_ref)
    forward_ref[...] = table_ref[...].astype(BF)
    block = (halo_ref[...], rows_ref[...])
    result = transform([block], wins, count, toeplitz_ref[...], forward_ref[...])
    for b in range(nblk):
        virt[b] = block_rows(result, b, nv, wins, count)
    for r in range(nblk):
        for k in range(SLOTS):
            picked_ref[r, k] = virt[pairs_ref[k, r]]


def virtual(rows, halo, taps, pairs, nblk):
    count, time = rows.shape
    size = (time // WLEN) * 2 * (count // nblk)
    smem, vmem = pl.BlockSpec(memory_space=pltpu.SMEM), pl.BlockSpec(memory_space=pltpu.VMEM)
    return pl.pallas_call(
        lambda *refs: virtual_kernel(nblk, *refs),
        in_specs=[smem] + [vmem] * 4,
        out_specs=[vmem] * 3,
        out_shape=[
            jax.ShapeDtypeStruct((nblk, SLOTS, size, BINS), BF),
            jax.ShapeDtypeStruct((WLEN, HALF), BF),
            jax.ShapeDtypeStruct((WLEN, 2 * BINS), BF),
        ],
        scratch_shapes=[pltpu.VMEM((8, 512), F32), pltpu.VMEM((nblk, size, BINS), BF)],
        compiler_params=pltpu.CompilerParams(vmem_limit_bytes=16 * MIB),
        cost_estimate=pl.CostEstimate(flops=10**8, bytes_accessed=rows.size * 8, transcendentals=0),
        name="virtual",
    )(pairs, rows, halo, taps, jnp.asarray(dft_table()))


def spectra_kernel(sizes, me_ref, rec_ref, halo_ref, toeplitz_ref, forward_ref, *refs):
    nblk, chans, time = rec_ref.shape
    wins = time // WLEN
    outs = [refs[nblk * q : nblk * (q + 1)] for q in range(len(sizes))]
    me = me_ref[0]
    per = 2
    for m in range(0, nblk, per):
        blocks = [(halo_ref[me ^ (m + u)], rec_ref[me ^ (m + u)]) for u in range(per)]
        result = transform(blocks, wins, chans, toeplitz_ref[...], forward_ref[...]).astype(BF)
        for u in range(per):
            for w in range(wins):
                for p in range(2):
                    lo = (u * wins + w) * chans
                    for out, size in zip(outs, sizes):
                        row = (w * 2 + p) * size
                        out[m + u][row : row + size] = result[lo : lo + size, p * BINS : (p + 1) * BINS]
                        lo += size


def spectra(records, halo, toeplitz, forward, me, sizes):
    nblk, chans, time = records.shape
    wins = time // WLEN
    shapes = []
    for size in sizes:
        shapes += [(wins * 2 * size, BINS)] * nblk
    smem, vmem = pl.BlockSpec(memory_space=pltpu.SMEM), pl.BlockSpec(memory_space=pltpu.VMEM)
    outs = pl.pallas_call(
        lambda *refs: spectra_kernel(sizes, *refs),
        in_specs=[smem] + [vmem] * 4,
        out_specs=[vmem] * len(shapes),
        out_shape=[jax.ShapeDtypeStruct(shape, BF) for shape in shapes],
        compiler_params=pltpu.CompilerParams(vmem_limit_bytes=16 * MIB),
        cost_estimate=pl.CostEstimate(
            flops=nblk * chans * wins * 3 * 2 * 512 * 256, bytes_accessed=nblk * chans * time * 3, transcendentals=0
        ),
        name="spectra",
    )(me, records, halo, toeplitz, forward)
    return [list(outs[i : i + nblk]) for i in range(0, len(outs), nblk)]


def sources_kernel(nsrc, nnar, wins, nv, place_ref, *refs):
    virts, out_ref, held, turned = refs[:nnar], refs[nnar], refs[nnar + 1], refs[nnar + 2]
    nw = nsrc * wins
    pitch = BINS + 8
    for n in range(nnar):
        held[place_ref[0] ^ n] = virts[n][...]

    def turn(src, carry):
        tiles = [[held[n, src, k].astype(F32) for n in range(nnar)] for k in range(SLOTS)]
        for w in range(wins):
            for p in range(2):
                at = (w * 2 + p) * nv
                tile = jnp.concatenate([tiles[k][n][at : at + nv] for k in range(SLOTS) for n in range(nnar)], 0)
                row = pl.multiple_of((p * nw + src * wins + w) * pitch, 8)
                turned[pl.ds(row, BINS), :] = tile.T
        return carry

    lax.fori_loop(0, nsrc, turn, 0, unroll=4)

    def one(j, carry):
        re = turned[pl.ds(j, nw, stride=pitch), :]
        im = turned[pl.ds(nw * pitch + j, nw, stride=pitch), :]
        top = jnp.concatenate([re, -im], 1)
        low = jnp.concatenate([im, re], 1)
        out_ref[j] = jnp.concatenate([top, low], 0).astype(BF)
        return carry

    lax.fori_loop(0, BINS, one, 0, unroll=8)


def sources(virts, place, wins, nv):
    nnar, nsrc = len(virts), virts[0].shape[0]
    nw = nsrc * wins
    width = SLOTS * nnar * nv
    smem, vmem = pl.BlockSpec(memory_space=pltpu.SMEM), pl.BlockSpec(memory_space=pltpu.VMEM)
    return pl.pallas_call(
        lambda *refs: sources_kernel(nsrc, nnar, wins, nv, *refs),
        in_specs=[smem] + [vmem] * nnar,
        out_specs=vmem,
        out_shape=jax.ShapeDtypeStruct((BINS, 2 * nw, 2 * width), BF),
        scratch_shapes=[
            pltpu.VMEM((nnar,) + virts[0].shape, BF),
            pltpu.VMEM((2 * nw * (BINS + 8), width), F32),
        ],
        compiler_params=pltpu.CompilerParams(vmem_limit_bytes=(10 + 2 * nw * BINS * width * 6 // MIB) * MIB),
        cost_estimate=pl.CostEstimate(flops=10**8, bytes_accessed=8 * nnar * virts[0].size, transcendentals=0),
        name="sources",
    )(place, *virts)


def stack_kernel(nw, wins, size, group, count_ref, me_ref, *refs):
    nsrc = nw // wins
    recvs, src_ref, lag_ref = refs[:nsrc], refs[nsrc], refs[nsrc + 1]
    out_ref, lag, wide, turned, cross = refs[-5:]
    step = pl.program_id(0)
    width = SLOTS * VIRTUAL_SOURCES
    depth = 2 * nw
    pack = src_ref.shape[1] // depth
    full = pack * depth
    pitch, bpitch = size + 8, BINS + 8

    @pl.when(step == 0)
    def _():
        lag[...] = lag_ref[...].astype(BF)
        for m in range(nsrc):
            src = me_ref[0] ^ m
            for w in range(wins):
                for p in range(2):
                    row = pl.multiple_of((p * nw + src * wins + w) * pitch, 8)
                    at = (w * 2 + p) * size
                    wide[pl.ds(row, size), :] = recvs[m][at : at + size].astype(F32)

        def turn(i, carry):
            flat = wide[pl.ds(i, depth, stride=pitch), :]
            flat = jnp.concatenate([flat] * pack, 0).T
            if pack > 1:
                flat = jnp.where(own, flat, 0.0)
            for c in range(0, full, 128):
                part = flat[:, c : min(c + 128, full)]
                turned[c // 128, pl.ds(pl.multiple_of(i * bpitch, 8), BINS), 0 : part.shape[1]] = part
            return carry

        shape = (BINS, full)
        own = lax.broadcasted_iota(jnp.int32, shape, 0) % pack == lax.broadcasted_iota(jnp.int32, shape, 1) // depth
        lax.fori_loop(0, size, turn, 0, unroll=8)
        slot = lax.broadcasted_iota(jnp.int32, (1, 2 * width), 1) % width // VIRTUAL_SOURCES
        scale = jnp.where(slot < count_ref[0], 1.0 / math.sqrt(nw), 0.0).astype(F32)

        def one(j, carry):
            rows = []
            for u in range(pack):
                at = pl.ds(j * pack + u, size, stride=bpitch)
                rows.append(jnp.concatenate([turned[c, at, :] for c in range(turned.shape[0])], 1))
            left = jnp.concatenate(rows, 0)[:, :full].astype(BF)
            value = dot(left, src_ref[j]) * scale
            for u in range(pack):
                at = pl.ds(pl.multiple_of((j * pack + u) * pitch, 8), size)
                for p in range(2):
                    cross[p, at, :] = value[u * size : (u + 1) * size, p * width : (p + 1) * width]
            return carry

        lax.fori_loop(0, BINS // pack, one, 0, unroll=8 // pack)

    for q in range(0, group, 4):
        lefts = []
        for u in range(4):
            at = step * group + q + u
            tiles = [cross[p, pl.ds(at, BINS, stride=pitch), :].astype(BF).T for p in range(2)]
            lefts.append(jnp.concatenate(tiles, 1))
        value = dot(jnp.concatenate(lefts, 0), lag[...]).astype(BF)
        for u in range(4):
            for k in range(SLOTS):
                at = u * width + k * VIRTUAL_SOURCES
                out_ref[0, k, q + u] = value[at : at + VIRTUAL_SOURCES]


def stack(recvs, table, count, me, lag, before, start, size, wins, chans):
    nw = wins * len(recvs)
    group = 16
    pack = 2 if 4 * nw <= 128 else 1
    table = table.reshape(BINS // pack, pack * 2 * nw, table.shape[2])
    shape = (1, SLOTS, chans, VIRTUAL_SOURCES, LAG_COUNT)
    first = start // group
    operands = [count, me, *recvs, table, lag]
    in_specs = [pl.BlockSpec(recv.shape, lambda t, c, e: (0, 0)) for recv in recvs] + [
        pl.BlockSpec(table.shape, lambda t, c, e: (0,) * 3),
        pl.BlockSpec(lag.shape, lambda t, c, e: (0, 0)),
    ]
    aliases = {}
    if before is not None:
        operands.append(before)
        in_specs.append(pl.BlockSpec(memory_space=pl.ANY))
        aliases = {len(operands) - 1: 0}
    return pl.pallas_call(
        lambda *refs: stack_kernel(nw, wins, size, group, *refs),
        grid_spec=pltpu.PrefetchScalarGridSpec(
            num_scalar_prefetch=2,
            grid=(size // group,),
            in_specs=in_specs,
            out_specs=pl.BlockSpec(
                (1, SLOTS, group, VIRTUAL_SOURCES, LAG_COUNT), lambda t, c, e: (0, 0, first + t, 0, 0)
            ),
            scratch_shapes=[
                pltpu.VMEM(lag.shape, BF),
                pltpu.VMEM((2 * nw * (size + 8), BINS), F32),
                pltpu.VMEM((-(-2 * nw * pack // 128), size * (BINS + 8), 128), F32),
                pltpu.VMEM((2, BINS * (size + 8), SLOTS * VIRTUAL_SOURCES), F32),
            ],
        ),
        out_shape=jax.ShapeDtypeStruct(shape, BF),
        input_output_aliases=aliases,
        compiler_params=pltpu.CompilerParams(vmem_limit_bytes=(20 + table.size * 4 // MIB) * MIB),
        cost_estimate=pl.CostEstimate(
            flops=size * 128 * 256 * 256 * 4, bytes_accessed=2 * (table.size + size * 32768), transcendentals=0
        ),
        name="stack",
    )(*operands)


def swap(value, axis, mask):
    return lax.ppermute(value, axis, [(i, i ^ mask) for i in range(lax.axis_size(axis))])


def after(value, others):
    return lax.optimization_barrier((value, others))[0] if others else value


def on_device(records, taps, pair_sources, pair_counts):
    nblk, chans, time = records.shape
    wins = time // WLEN
    nv = chans // VSTEP
    nwide, nnar = lax.axis_size("wide"), lax.axis_size("narrow")
    half = chans // 2
    me = lax.axis_index("wide").astype(jnp.int32)[None]
    place = lax.axis_index("narrow").astype(jnp.int32)[None]
    ahead = [(i, i + 1) for i in range(nwide - 1)]
    order = list(range(nwide - 1, 0, -1))
    rows, tip = extract(records)
    tip = lax.ppermute(tip, "wide", ahead)
    halo = lax.ppermute(after(records[:, :, time - HALF :], [tip]), "wide", ahead)
    picked, toeplitz, forward = virtual(rows, tip, taps[None], pair_sources.T, nblk)
    picked = lax.all_to_all(picked, "wide", split_axis=0, concat_axis=0, tiled=True)
    near, far = spectra(records, halo, toeplitz, forward, me, (half, half))
    picked = after(picked, [near[0]])

    slots = [picked] + [swap(picked, "narrow", n) for n in range(nnar - 1, 0, -1)][::-1]
    for i, m in enumerate(order):
        near[m] = swap(after(near[m], slots[1:3] if i == len(order) - 1 else []), "wide", m)
    for i, m in enumerate(order):
        waits = [near[order[min(i + 2, nwide - 2)]]] + (slots[1:] if i >= 2 else [])
        far[m] = swap(after(far[m], waits), "wide", m)
    table = sources(slots, place, wins, nv)
    lag = jnp.asarray(lag_table())
    out = stack(near, table, pair_counts, me, lag, None, 0, half, wins, chans)
    return stack(far, table, pair_counts, me, lag, out, half, half, wins, chans)


def solution(mesh):
    return jax.shard_map(
        on_device,
        mesh=mesh,
        in_specs=(P(None, "narrow", "wide"), P(), P(), P("wide")),
        out_specs=P("wide", None, "narrow", None, None),
        check_vma=False,
    )
```

```python
import math

import jax
import jax.numpy as jnp
import numpy as np
from jax import lax
from jax.experimental import pallas as pl
from jax.experimental.pallas import tpu as pltpu
from jax.sharding import PartitionSpec as P

BLOCK_CHANNELS = 512
VIRTUAL_SOURCES = 32
VSTEP = BLOCK_CHANNELS // VIRTUAL_SOURCES
TAPS = 201
WLEN = 512
HALF = 256
BINS = 128
F_LO = 4
LAG_COUNT = 256
SLOTS = 4
BF = jnp.bfloat16
F32 = jnp.float32
MIB = 1 << 20


def dft_table():
    times = np.arange(WLEN, dtype=np.int32)[:, None]
    bins = (F_LO + np.arange(BINS, dtype=np.int32))[None, :]
    angle = np.mod(times * bins, WLEN).astype(np.float32) * np.float32(2.0 * math.pi / WLEN)
    scale = np.float32(1.0 / math.sqrt(WLEN))
    return np.concatenate([np.cos(angle) * scale, -np.sin(angle) * scale], 1).astype(BF).astype(np.float32)


def lag_table():
    bins = (F_LO + np.arange(BINS, dtype=np.int32))[:, None]
    lags = (np.arange(LAG_COUNT, dtype=np.int32) - LAG_COUNT // 2)[None, :]
    angle = np.mod(bins * lags, WLEN).astype(np.float32) * np.float32(2.0 * math.pi / WLEN)
    scale = np.float32(1.0 / math.sqrt(BINS))
    return np.concatenate([np.cos(angle) * scale, -np.sin(angle) * scale], 0).astype(BF).astype(np.float32)


def dot(a, b):
    return lax.dot_general(a, b, (((1,), (0,)), ((), ())), preferred_element_type=F32)


def build_toeplitz(taps_ref, row, toeplitz):
    row[...] = jnp.zeros_like(row)
    row[:, 128 : 128 + TAPS] = jnp.broadcast_to(taps_ref[...].astype(BF).astype(F32), (8, TAPS))
    bands = jnp.broadcast_to(row[0:1, :], (128, 512))
    bands = pltpu.roll(bands, 0, 1, stride=1, stride_axis=0).astype(BF)
    zero = jnp.zeros((128, 128), BF)
    far, mid, near = [bands[:, at : at + 128] for at in (128, 256, 384)]
    toeplitz[:, :128] = jnp.concatenate([near, mid, far, zero], 0)
    toeplitz[:, 128:] = jnp.concatenate([zero, near, mid, far], 0)


def transform(blocks, wins, chans, toeplitz, table):
    rows = []
    for halo, rec in blocks:
        rows.append(jnp.concatenate([halo, rec[:, :HALF]], 1))
        rows += [rec[:, HALF * (m - 1) : HALF * (m + 1)] for m in range(1, 2 * wins)]
    white = dot(jnp.concatenate(rows, 0), toeplitz).astype(BF)
    pieces = [
        jnp.concatenate([white[2 * w * chans : (2 * w + 1) * chans], white[(2 * w + 1) * chans : (2 * w + 2) * chans]], 1)
        for w in range(len(blocks) * wins)
    ]
    return dot(jnp.concatenate(pieces, 0), table)


def virtual_rows(ref, nv):
    rows = [ref[b, r * VSTEP : (r + 1) * VSTEP, :].astype(F32)[0:1] for b in range(ref.shape[0]) for r in range(nv)]
    return jnp.concatenate(rows, 0).astype(BF)


def block_rows(result, b, nv, wins, count):
    parts = [
        result[w * count + b * nv : w * count + (b + 1) * nv, p * BINS : (p + 1) * BINS]
        for w in range(wins)
        for p in range(2)
    ]
    return jnp.concatenate(parts, 0).astype(BF)


def rows_kernel(rec_ref, rows_ref, near_ref):
    time = rec_ref.shape[2]
    rows = virtual_rows(rec_ref, rec_ref.shape[1] // VSTEP)
    rows_ref[...] = rows
    near_ref[...] = rows[:, time - HALF :]


def extract(records):
    nblk, chans, time = records.shape
    count = nblk * (chans // VSTEP)
    vmem = pl.BlockSpec(memory_space=pltpu.VMEM)
    return pl.pallas_call(
        rows_kernel,
        in_specs=[vmem],
        out_specs=[vmem] * 2,
        out_shape=[jax.ShapeDtypeStruct((count, time), BF), jax.ShapeDtypeStruct((count, HALF), BF)],
        compiler_params=pltpu.CompilerParams(vmem_limit_bytes=8 * MIB),
        cost_estimate=pl.CostEstimate(flops=0, bytes_accessed=records.size, transcendentals=0),
        name="extract",
    )(records)


def virtual_kernel(nblk, pairs_ref, rows_ref, halo_ref, taps_ref, table_ref, *refs):
    picked_ref, toeplitz_ref, forward_ref, row, virt = refs
    count, time = rows_ref.shape
    nv, wins = count // nblk, time // WLEN
    build_toeplitz(taps_ref, row, toeplitz_ref)
    forward_ref[...] = table_ref[...].astype(BF)
    block = (halo_ref[...], rows_ref[...])
    result = transform([block], wins, count, toeplitz_ref[...], forward_ref[...])
    for b in range(nblk):
        virt[b] = block_rows(result, b, nv, wins, count)
    for r in range(nblk):
        for k in range(SLOTS):
            picked_ref[r, k] = virt[pairs_ref[r, k]]


def virtual(rows, halo, taps, pairs, nblk):
    count, time = rows.shape
    size = (time // WLEN) * 2 * (count // nblk)
    smem, vmem = pl.BlockSpec(memory_space=pltpu.SMEM), pl.BlockSpec(memory_space=pltpu.VMEM)
    return pl.pallas_call(
        lambda *refs: virtual_kernel(nblk, *refs),
        in_specs=[smem] + [vmem] * 4,
        out_specs=[vmem] * 3,
        out_shape=[
            jax.ShapeDtypeStruct((nblk, SLOTS, size, BINS), BF),
            jax.ShapeDtypeStruct((WLEN, HALF), BF),
            jax.ShapeDtypeStruct((WLEN, 2 * BINS), BF),
        ],
        scratch_shapes=[pltpu.VMEM((8, 512), F32), pltpu.VMEM((nblk, size, BINS), BF)],
        compiler_params=pltpu.CompilerParams(vmem_limit_bytes=16 * MIB),
        cost_estimate=pl.CostEstimate(flops=10**8, bytes_accessed=rows.size * 8, transcendentals=0),
        name="virtual",
    )(pairs, rows, halo, taps, jnp.asarray(dft_table()))


def spectra_kernel(sizes, me_ref, rec_ref, halo_ref, toeplitz_ref, forward_ref, *refs):
    nblk, chans, time = rec_ref.shape
    wins = time // WLEN
    outs = [refs[nblk * q : nblk * (q + 1)] for q in range(len(sizes))]
    me = me_ref[0]
    per = 2
    for m in range(0, nblk, per):
        blocks = [(halo_ref[me ^ (m + u)], rec_ref[me ^ (m + u)]) for u in range(per)]
        result = transform(blocks, wins, chans, toeplitz_ref[...], forward_ref[...]).astype(BF)
        for u in range(per):
            for w in range(wins):
                for p in range(2):
                    lo = (u * wins + w) * chans
                    for out, size in zip(outs, sizes):
                        row = (w * 2 + p) * size
                        out[m + u][row : row + size] = result[lo : lo + size, p * BINS : (p + 1) * BINS]
                        lo += size


def spectra(records, halo, toeplitz, forward, me, sizes):
    nblk, chans, time = records.shape
    wins = time // WLEN
    shapes = []
    for size in sizes:
        shapes += [(wins * 2 * size, BINS)] * nblk
    smem, vmem = pl.BlockSpec(memory_space=pltpu.SMEM), pl.BlockSpec(memory_space=pltpu.VMEM)
    outs = pl.pallas_call(
        lambda *refs: spectra_kernel(sizes, *refs),
        in_specs=[smem] + [vmem] * 4,
        out_specs=[vmem] * len(shapes),
        out_shape=[jax.ShapeDtypeStruct(shape, BF) for shape in shapes],
        compiler_params=pltpu.CompilerParams(vmem_limit_bytes=16 * MIB),
        cost_estimate=pl.CostEstimate(
            flops=nblk * chans * wins * 3 * 2 * 512 * 256, bytes_accessed=nblk * chans * time * 3, transcendentals=0
        ),
        name="spectra",
    )(me, records, halo, toeplitz, forward)
    return [list(outs[i : i + nblk]) for i in range(0, len(outs), nblk)]


def sources_kernel(nsrc, nnar, wins, nv, place_ref, *refs):
    virts, out_ref, held, turned = refs[:nnar], refs[nnar], refs[nnar + 1], refs[nnar + 2]
    nw = nsrc * wins
    pitch = BINS + 8
    for n in range(nnar):
        held[place_ref[0] ^ n] = virts[n][...]

    def turn(src, carry):
        tiles = [[held[n, src, k].astype(F32) for n in range(nnar)] for k in range(SLOTS)]
        for w in range(wins):
            for p in range(2):
                at = (w * 2 + p) * nv
                tile = jnp.concatenate([tiles[k][n][at : at + nv] for k in range(SLOTS) for n in range(nnar)], 0)
                row = pl.multiple_of((p * nw + src * wins + w) * pitch, 8)
                turned[pl.ds(row, BINS), :] = tile.T
        return carry

    lax.fori_loop(0, nsrc, turn, 0, unroll=4)

    def one(j, carry):
        re = turned[pl.ds(j, nw, stride=pitch), :]
        im = turned[pl.ds(nw * pitch + j, nw, stride=pitch), :]
        top = jnp.concatenate([re, -im], 1)
        low = jnp.concatenate([im, re], 1)
        out_ref[j] = jnp.concatenate([top, low], 0).astype(BF)
        return carry

    lax.fori_loop(0, BINS, one, 0, unroll=8)


def sources(virts, place, wins, nv):
    nnar, nsrc = len(virts), virts[0].shape[0]
    nw = nsrc * wins
    width = SLOTS * nnar * nv
    smem, vmem = pl.BlockSpec(memory_space=pltpu.SMEM), pl.BlockSpec(memory_space=pltpu.VMEM)
    return pl.pallas_call(
        lambda *refs: sources_kernel(nsrc, nnar, wins, nv, *refs),
        in_specs=[smem] + [vmem] * nnar,
        out_specs=vmem,
        out_shape=jax.ShapeDtypeStruct((BINS, 2 * nw, 2 * width), BF),
        scratch_shapes=[
            pltpu.VMEM((nnar,) + virts[0].shape, BF),
            pltpu.VMEM((2 * nw * (BINS + 8), width), F32),
        ],
        compiler_params=pltpu.CompilerParams(vmem_limit_bytes=(10 + 2 * nw * BINS * width * 6 // MIB) * MIB),
        cost_estimate=pl.CostEstimate(flops=10**8, bytes_accessed=8 * nnar * virts[0].size, transcendentals=0),
        name="sources",
    )(place, *virts)


def stack_kernel(nw, wins, start, size, group, count_ref, me_ref, *refs):
    nsrc = nw // wins
    recvs, src_ref, lag_ref = refs[:nsrc], refs[nsrc], refs[nsrc + 1]
    out_ref, wide, turned, cross, held, sems = refs[-6:]
    width = SLOTS * VIRTUAL_SOURCES
    depth = 2 * nw
    pack = src_ref.shape[1] // depth
    full = pack * depth
    pitch, bpitch = size + 8, BINS + 8

    lag = lag_ref[...].astype(BF)
    for m in range(nsrc):
        src = me_ref[0] ^ m
        for w in range(wins):
            for p in range(2):
                row = pl.multiple_of((p * nw + src * wins + w) * pitch, 8)
                at = (w * 2 + p) * size
                wide[pl.ds(row, size), :] = recvs[m][at : at + size].astype(F32)

    shape = (BINS, full)
    own = lax.broadcasted_iota(jnp.int32, shape, 0) % pack == lax.broadcasted_iota(jnp.int32, shape, 1) // depth

    def turn(i, carry):
        flat = wide[pl.ds(i, depth, stride=pitch), :]
        flat = jnp.concatenate([flat] * pack, 0).T
        if pack > 1:
            flat = jnp.where(own, flat, 0.0)
        for c in range(0, full, 128):
            part = flat[:, c : min(c + 128, full)]
            turned[c // 128, pl.ds(pl.multiple_of(i * bpitch, 8), BINS), 0 : part.shape[1]] = part
        return carry

    lax.fori_loop(0, size, turn, 0, unroll=8)
    slot = lax.broadcasted_iota(jnp.int32, (1, 2 * width), 1) % width // VIRTUAL_SOURCES
    scale = jnp.where(slot < count_ref[0], 1.0 / math.sqrt(nw), 0.0).astype(F32)

    def one(j, carry):
        rows = []
        for u in range(pack):
            at = pl.ds(j * pack + u, size, stride=bpitch)
            rows.append(jnp.concatenate([turned[c, at, :] for c in range(turned.shape[0])], 1))
        left = jnp.concatenate(rows, 0)[:, :full].astype(BF)
        value = dot(left, src_ref[j]) * scale
        for u in range(pack):
            at = pl.ds(pl.multiple_of((j * pack + u) * pitch, 8), size)
            for p in range(2):
                cross[p, at, :] = value[u * size : (u + 1) * size, p * width : (p + 1) * width]
        return carry

    lax.fori_loop(0, BINS // pack, one, 0, unroll=8 // pack)

    rows = 4
    copies = []
    for step in range(size // group):
        for q in range(0, group, rows):
            lefts = []
            for u in range(rows):
                at = step * group + q + u
                tiles = [cross[p, pl.ds(at, BINS, stride=pitch), :].astype(BF).T for p in range(2)]
                lefts.append(jnp.concatenate(tiles, 1))
            value = dot(jnp.concatenate(lefts, 0), lag).astype(BF)
            for u in range(rows):
                for k in range(SLOTS):
                    at = u * width + k * VIRTUAL_SOURCES
                    held[step, k, q + u] = value[at : at + VIRTUAL_SOURCES]
        target = out_ref.at[0, :, pl.ds(start + step * group, group)]
        copies.append(pltpu.make_async_copy(held.at[step], target, sems.at[step]))
        copies[-1].start()
    for copy in copies:
        copy.wait()


def stack(recvs, table, count, me, lag, before, start, size, wins, chans):
    nw = wins * len(recvs)
    group = 8
    pack = 2 if 4 * nw <= 128 else 1
    table = table.reshape(BINS // pack, pack * 2 * nw, table.shape[2])
    shape = (1, SLOTS, chans, VIRTUAL_SOURCES, LAG_COUNT)
    smem, vmem = pl.BlockSpec(memory_space=pltpu.SMEM), pl.BlockSpec(memory_space=pltpu.VMEM)
    operands = [count, me, *recvs, table, lag]
    in_specs = [smem, smem] + [vmem] * (len(operands) - 2)
    aliases = {}
    if before is not None:
        operands.append(before)
        in_specs.append(pl.BlockSpec(memory_space=pl.ANY))
        aliases = {len(operands) - 1: 0}
    steps = size // group
    return pl.pallas_call(
        lambda *refs: stack_kernel(nw, wins, start, size, group, *refs),
        in_specs=in_specs,
        out_specs=pl.BlockSpec(memory_space=pl.ANY),
        scratch_shapes=[
            pltpu.VMEM((2 * nw * (size + 8), BINS), F32),
            pltpu.VMEM((-(-2 * nw * pack // 128), size * (BINS + 8), 128), F32),
            pltpu.VMEM((2, BINS * (size + 8), SLOTS * VIRTUAL_SOURCES), F32),
            pltpu.VMEM((steps, SLOTS, group, VIRTUAL_SOURCES, LAG_COUNT), BF),
            pltpu.SemaphoreType.DMA((steps,)),
        ],
        out_shape=jax.ShapeDtypeStruct(shape, BF),
        input_output_aliases=aliases,
        compiler_params=pltpu.CompilerParams(vmem_limit_bytes=32 * MIB),
        cost_estimate=pl.CostEstimate(
            flops=size * 128 * 256 * 256 * 4, bytes_accessed=2 * (table.size + size * 32768), transcendentals=0
        ),
        name="stack",
    )(*operands)


def swap(value, axis, mask):
    return lax.ppermute(value, axis, [(i, i ^ mask) for i in range(lax.axis_size(axis))])


def after(value, others):
    return lax.optimization_barrier((value, others))[0] if others else value


def on_device(records, taps, pair_sources, pair_counts):
    nblk, chans, time = records.shape
    wins = time // WLEN
    nv = chans // VSTEP
    nwide, nnar = lax.axis_size("wide"), lax.axis_size("narrow")
    half = chans // 2
    me = lax.axis_index("wide").astype(jnp.int32)[None]
    place = lax.axis_index("narrow").astype(jnp.int32)[None]
    ahead = [(i, i + 1) for i in range(nwide - 1)]
    order = list(range(nwide - 1, 0, -1))
    rows, tip = extract(records)
    tip = lax.ppermute(tip, "wide", ahead)
    halo = lax.ppermute(after(records[:, :, time - HALF :], [tip]), "wide", ahead)
    picked, toeplitz, forward = virtual(rows, tip, taps[None], pair_sources, nblk)
    picked = lax.all_to_all(picked, "wide", split_axis=0, concat_axis=0, tiled=True)
    chunks = spectra(records, halo, toeplitz, forward, me, (half, half))
    picked, (near, far) = lax.optimization_barrier((picked, chunks))

    top = nnar // 2
    slots = {0: picked, **{n: swap(picked, "narrow", n) for n in (top, 1) if n}}
    for i, m in enumerate(order):
        waits = []
        if i == len(order) - 2:
            waits = [slots[n] for n in sorted(slots) if n]
        near[m] = swap(after(near[m], waits), "wide", m)
    bit = top
    while bit:
        for n in sorted(slots):
            if n ^ bit not in slots:
                slots[n ^ bit] = swap(after(slots[n], [near[m] for m in order[:3]]), "narrow", bit)
        bit //= 2
    for i, m in enumerate(order):
        waits = [near[order[min(i + 2, nwide - 2)]]] + ([slots[n] for n in sorted(slots) if n] if i >= 2 else [])
        far[m] = swap(after(far[m], waits), "wide", m)
    table = sources([slots[n] for n in range(nnar)], place, wins, nv)
    lag = jnp.asarray(lag_table())
    out = stack(near, table, pair_counts, me, lag, None, 0, half, wins, chans)
    return stack(far, table, pair_counts, me, lag, out, half, half, wins, chans)


def solution(mesh):
    return jax.shard_map(
        on_device,
        mesh=mesh,
        in_specs=(P(None, "narrow", "wide"), P(), P(), P("wide")),
        out_specs=P("wide", None, "narrow", None, None),
        check_vma=False,
    )
```

```python
import math

import jax
import jax.numpy as jnp
import numpy as np
from jax import lax
from jax.experimental import pallas as pl
from jax.experimental.pallas import tpu as pltpu
from jax.sharding import PartitionSpec as P

BLOCK_CHANNELS = 512
VIRTUAL_SOURCES = 32
VSTEP = BLOCK_CHANNELS // VIRTUAL_SOURCES
TAPS = 201
WLEN = 512
HALF = 256
BINS = 128
F_LO = 4
LAG_COUNT = 256
SLOTS = 4
BF = jnp.bfloat16
F32 = jnp.float32
MIB = 1 << 20


def dft_table():
    times = np.arange(WLEN, dtype=np.int32)[:, None]
    bins = (F_LO + np.arange(BINS, dtype=np.int32))[None, :]
    angle = np.mod(times * bins, WLEN).astype(np.float32) * np.float32(2.0 * math.pi / WLEN)
    scale = np.float32(1.0 / math.sqrt(WLEN))
    return np.concatenate([np.cos(angle) * scale, -np.sin(angle) * scale], 1).astype(BF).astype(np.float32)


def lag_table():
    bins = (F_LO + np.arange(BINS, dtype=np.int32))[:, None]
    lags = (np.arange(LAG_COUNT, dtype=np.int32) - LAG_COUNT // 2)[None, :]
    angle = np.mod(bins * lags, WLEN).astype(np.float32) * np.float32(2.0 * math.pi / WLEN)
    scale = np.float32(1.0 / math.sqrt(BINS))
    return np.concatenate([np.cos(angle) * scale, -np.sin(angle) * scale], 0).astype(BF).astype(np.float32)


def dot(a, b):
    return lax.dot_general(a, b, (((1,), (0,)), ((), ())), preferred_element_type=F32)


def build_toeplitz(taps_ref, row, toeplitz):
    row[...] = jnp.zeros_like(row)
    row[:, 128 : 128 + TAPS] = jnp.broadcast_to(taps_ref[...].astype(BF).astype(F32), (8, TAPS))
    bands = jnp.broadcast_to(row[0:1, :], (128, 512))
    bands = pltpu.roll(bands, 0, 1, stride=1, stride_axis=0).astype(BF)
    zero = jnp.zeros((128, 128), BF)
    far, mid, near = [bands[:, at : at + 128] for at in (128, 256, 384)]
    toeplitz[:, :128] = jnp.concatenate([near, mid, far, zero], 0)
    toeplitz[:, 128:] = jnp.concatenate([zero, near, mid, far], 0)


def transform(blocks, wins, chans, toeplitz, table):
    rows = []
    for halo, rec in blocks:
        rows.append(jnp.concatenate([halo, rec[:, :HALF]], 1))
        rows += [rec[:, HALF * (m - 1) : HALF * (m + 1)] for m in range(1, 2 * wins)]
    white = dot(jnp.concatenate(rows, 0), toeplitz).astype(BF)
    pieces = [
        jnp.concatenate([white[2 * w * chans : (2 * w + 1) * chans], white[(2 * w + 1) * chans : (2 * w + 2) * chans]], 1)
        for w in range(len(blocks) * wins)
    ]
    return dot(jnp.concatenate(pieces, 0), table)


def virtual_rows(ref, nv):
    rows = [ref[b, r * VSTEP : (r + 1) * VSTEP, :].astype(F32)[0:1] for b in range(ref.shape[0]) for r in range(nv)]
    return jnp.concatenate(rows, 0).astype(BF)


def block_rows(result, b, nv, wins, count):
    parts = [
        result[w * count + b * nv : w * count + (b + 1) * nv, p * BINS : (p + 1) * BINS]
        for w in range(wins)
        for p in range(2)
    ]
    return jnp.concatenate(parts, 0).astype(BF)


def rows_kernel(rec_ref, rows_ref, near_ref):
    time = rec_ref.shape[2]
    rows = virtual_rows(rec_ref, rec_ref.shape[1] // VSTEP)
    rows_ref[...] = rows
    near_ref[...] = rows[:, time - HALF :]


def extract(records):
    nblk, chans, time = records.shape
    count = nblk * (chans // VSTEP)
    vmem = pl.BlockSpec(memory_space=pltpu.VMEM)
    return pl.pallas_call(
        rows_kernel,
        in_specs=[vmem],
        out_specs=[vmem] * 2,
        out_shape=[jax.ShapeDtypeStruct((count, time), BF), jax.ShapeDtypeStruct((count, HALF), BF)],
        compiler_params=pltpu.CompilerParams(vmem_limit_bytes=8 * MIB),
        cost_estimate=pl.CostEstimate(flops=0, bytes_accessed=records.size, transcendentals=0),
        name="extract",
    )(records)


def virtual_kernel(nblk, pairs_ref, rows_ref, halo_ref, taps_ref, table_ref, *refs):
    picked_ref, toeplitz_ref, forward_ref, row, virt = refs
    count, time = rows_ref.shape
    nv, wins = count // nblk, time // WLEN
    build_toeplitz(taps_ref, row, toeplitz_ref)
    forward_ref[...] = table_ref[...].astype(BF)
    block = (halo_ref[...], rows_ref[...])
    result = transform([block], wins, count, toeplitz_ref[...], forward_ref[...])
    for b in range(nblk):
        virt[b] = block_rows(result, b, nv, wins, count)
    for r in range(nblk):
        for k in range(SLOTS):
            picked_ref[r, k] = virt[pairs_ref[r, k]]


def virtual(rows, halo, taps, pairs, nblk):
    count, time = rows.shape
    size = (time // WLEN) * 2 * (count // nblk)
    smem, vmem = pl.BlockSpec(memory_space=pltpu.SMEM), pl.BlockSpec(memory_space=pltpu.VMEM)
    return pl.pallas_call(
        lambda *refs: virtual_kernel(nblk, *refs),
        in_specs=[smem] + [vmem] * 4,
        out_specs=[vmem] * 3,
        out_shape=[
            jax.ShapeDtypeStruct((nblk, SLOTS, size, BINS), BF),
            jax.ShapeDtypeStruct((WLEN, HALF), BF),
            jax.ShapeDtypeStruct((WLEN, 2 * BINS), BF),
        ],
        scratch_shapes=[pltpu.VMEM((8, 512), F32), pltpu.VMEM((nblk, size, BINS), BF)],
        compiler_params=pltpu.CompilerParams(vmem_limit_bytes=16 * MIB),
        cost_estimate=pl.CostEstimate(flops=10**8, bytes_accessed=rows.size * 8, transcendentals=0),
        name="virtual",
    )(pairs, rows, halo, taps, jnp.asarray(dft_table()))


def spectra_kernel(sizes, me_ref, rec_ref, halo_ref, toeplitz_ref, forward_ref, *refs):
    nblk, chans, time = rec_ref.shape
    wins = time // WLEN
    outs = [refs[nblk * q : nblk * (q + 1)] for q in range(len(sizes))]
    me = me_ref[0]
    per = 4
    for m in range(0, nblk, per):
        blocks = [(halo_ref[me ^ (m + u)], rec_ref[me ^ (m + u)]) for u in range(per)]
        result = transform(blocks, wins, chans, toeplitz_ref[...], forward_ref[...]).astype(BF)
        for u in range(per):
            for w in range(wins):
                for p in range(2):
                    lo = (u * wins + w) * chans
                    for out, size in zip(outs, sizes):
                        row = (w * 2 + p) * size
                        out[m + u][row : row + size] = result[lo : lo + size, p * BINS : (p + 1) * BINS]
                        lo += size


def spectra(records, halo, toeplitz, forward, me, sizes):
    nblk, chans, time = records.shape
    wins = time // WLEN
    shapes = []
    for size in sizes:
        shapes += [(wins * 2 * size, BINS)] * nblk
    smem, vmem = pl.BlockSpec(memory_space=pltpu.SMEM), pl.BlockSpec(memory_space=pltpu.VMEM)
    outs = pl.pallas_call(
        lambda *refs: spectra_kernel(sizes, *refs),
        in_specs=[smem] + [vmem] * 4,
        out_specs=[vmem] * len(shapes),
        out_shape=[jax.ShapeDtypeStruct(shape, BF) for shape in shapes],
        compiler_params=pltpu.CompilerParams(vmem_limit_bytes=24 * MIB),
        cost_estimate=pl.CostEstimate(
            flops=nblk * chans * wins * 3 * 2 * 512 * 256, bytes_accessed=nblk * chans * time * 3, transcendentals=0
        ),
        name="spectra",
    )(me, records, halo, toeplitz, forward)
    return [list(outs[i : i + nblk]) for i in range(0, len(outs), nblk)]


def sources_kernel(nsrc, nnar, wins, nv, place_ref, *refs):
    virts, out_ref, held, turned = refs[:nnar], refs[nnar], refs[nnar + 1], refs[nnar + 2]
    nw = nsrc * wins
    pitch = BINS + 8
    for n in range(nnar):
        held[place_ref[0] ^ n] = virts[n][...]

    def turn(src, carry):
        tiles = [[held[n, src, k].astype(F32) for n in range(nnar)] for k in range(SLOTS)]
        for w in range(wins):
            for p in range(2):
                at = (w * 2 + p) * nv
                tile = jnp.concatenate([tiles[k][n][at : at + nv] for k in range(SLOTS) for n in range(nnar)], 0)
                row = pl.multiple_of((p * nw + src * wins + w) * pitch, 8)
                turned[pl.ds(row, BINS), :] = tile.T
        return carry

    lax.fori_loop(0, nsrc, turn, 0, unroll=4)

    def one(j, carry):
        re = turned[pl.ds(j, nw, stride=pitch), :]
        im = turned[pl.ds(nw * pitch + j, nw, stride=pitch), :]
        top = jnp.concatenate([re, -im], 1)
        low = jnp.concatenate([im, re], 1)
        out_ref[j] = jnp.concatenate([top, low], 0).astype(BF)
        return carry

    lax.fori_loop(0, BINS, one, 0, unroll=8)


def sources(virts, place, wins, nv):
    nnar, nsrc = len(virts), virts[0].shape[0]
    nw = nsrc * wins
    width = SLOTS * nnar * nv
    smem, vmem = pl.BlockSpec(memory_space=pltpu.SMEM), pl.BlockSpec(memory_space=pltpu.VMEM)
    return pl.pallas_call(
        lambda *refs: sources_kernel(nsrc, nnar, wins, nv, *refs),
        in_specs=[smem] + [vmem] * nnar,
        out_specs=vmem,
        out_shape=jax.ShapeDtypeStruct((BINS, 2 * nw, 2 * width), BF),
        scratch_shapes=[
            pltpu.VMEM((nnar,) + virts[0].shape, BF),
            pltpu.VMEM((2 * nw * (BINS + 8), width), F32),
        ],
        compiler_params=pltpu.CompilerParams(vmem_limit_bytes=(10 + 2 * nw * BINS * width * 6 // MIB) * MIB),
        cost_estimate=pl.CostEstimate(flops=10**8, bytes_accessed=8 * nnar * virts[0].size, transcendentals=0),
        name="sources",
    )(place, *virts)


def stack_kernel(nw, wins, start, size, group, count_ref, me_ref, *refs):
    nsrc = nw // wins
    recvs, src_ref, lag_ref = refs[:nsrc], refs[nsrc], refs[nsrc + 1]
    out_ref, wide, turned, cross, held, sems = refs[-6:]
    width = SLOTS * VIRTUAL_SOURCES
    depth = 2 * nw
    pack = src_ref.shape[1] // depth
    full = pack * depth
    pitch, bpitch = size + 8, BINS + 8

    lag = lag_ref[...].astype(BF)
    for m in range(nsrc):
        src = me_ref[0] ^ m
        for w in range(wins):
            for p in range(2):
                row = pl.multiple_of((p * nw + src * wins + w) * pitch, 8)
                at = (w * 2 + p) * size
                wide[pl.ds(row, size), :] = recvs[m][at : at + size].astype(F32)

    shape = (BINS, full)
    own = lax.broadcasted_iota(jnp.int32, shape, 0) % pack == lax.broadcasted_iota(jnp.int32, shape, 1) // depth

    def turn(i, carry):
        flat = wide[pl.ds(i, depth, stride=pitch), :]
        flat = jnp.concatenate([flat] * pack, 0).T
        if pack > 1:
            flat = jnp.where(own, flat, 0.0)
        for c in range(0, full, 128):
            part = flat[:, c : min(c + 128, full)]
            turned[c // 128, pl.ds(pl.multiple_of(i * bpitch, 8), BINS), 0 : part.shape[1]] = part
        return carry

    lax.fori_loop(0, size, turn, 0, unroll=8)
    slot = lax.broadcasted_iota(jnp.int32, (1, 2 * width), 1) % width // VIRTUAL_SOURCES
    scale = jnp.where(slot < count_ref[0], 1.0 / math.sqrt(nw), 0.0).astype(F32)

    def one(j, carry):
        rows = []
        for u in range(pack):
            at = pl.ds(j * pack + u, size, stride=bpitch)
            rows.append(jnp.concatenate([turned[c, at, :] for c in range(turned.shape[0])], 1))
        left = jnp.concatenate(rows, 0)[:, :full].astype(BF)
        value = dot(left, src_ref[j]) * scale
        for u in range(pack):
            at = pl.ds(pl.multiple_of((j * pack + u) * pitch, 8), size)
            for p in range(2):
                cross[p, at, :] = value[u * size : (u + 1) * size, p * width : (p + 1) * width]
        return carry

    lax.fori_loop(0, BINS // pack, one, 0, unroll=16 // pack)

    rows = 4
    copies = []
    for step in range(size // group):
        for q in range(0, group, rows):
            lefts = []
            for u in range(rows):
                at = step * group + q + u
                tiles = [cross[p, pl.ds(at, BINS, stride=pitch), :].astype(BF).T for p in range(2)]
                lefts.append(jnp.concatenate(tiles, 1))
            value = dot(jnp.concatenate(lefts, 0), lag).astype(BF)
            for u in range(rows):
                for k in range(SLOTS):
                    at = u * width + k * VIRTUAL_SOURCES
                    held[step, k, q + u] = value[at : at + VIRTUAL_SOURCES]
        target = out_ref.at[0, :, pl.ds(start + step * group, group)]
        copies.append(pltpu.make_async_copy(held.at[step], target, sems.at[step]))
        copies[-1].start()
    for copy in copies:
        copy.wait()


def stack(recvs, table, count, me, lag, before, start, size, wins, chans):
    nw = wins * len(recvs)
    group = 8
    pack = 2 if 4 * nw <= 128 else 1
    table = table.reshape(BINS // pack, pack * 2 * nw, table.shape[2])
    shape = (1, SLOTS, chans, VIRTUAL_SOURCES, LAG_COUNT)
    smem, vmem = pl.BlockSpec(memory_space=pltpu.SMEM), pl.BlockSpec(memory_space=pltpu.VMEM)
    operands = [count, me, *recvs, table, lag]
    in_specs = [smem, smem] + [vmem] * (len(operands) - 2)
    aliases = {}
    if before is not None:
        operands.append(before)
        in_specs.append(pl.BlockSpec(memory_space=pl.ANY))
        aliases = {len(operands) - 1: 0}
    steps = size // group
    return pl.pallas_call(
        lambda *refs: stack_kernel(nw, wins, start, size, group, *refs),
        in_specs=in_specs,
        out_specs=pl.BlockSpec(memory_space=pl.ANY),
        scratch_shapes=[
            pltpu.VMEM((2 * nw * (size + 8), BINS), F32),
            pltpu.VMEM((-(-2 * nw * pack // 128), size * (BINS + 8), 128), F32),
            pltpu.VMEM((2, BINS * (size + 8), SLOTS * VIRTUAL_SOURCES), F32),
            pltpu.VMEM((steps, SLOTS, group, VIRTUAL_SOURCES, LAG_COUNT), BF),
            pltpu.SemaphoreType.DMA((steps,)),
        ],
        out_shape=jax.ShapeDtypeStruct(shape, BF),
        input_output_aliases=aliases,
        compiler_params=pltpu.CompilerParams(vmem_limit_bytes=32 * MIB),
        cost_estimate=pl.CostEstimate(
            flops=size * 128 * 256 * 256 * 4, bytes_accessed=2 * (table.size + size * 32768), transcendentals=0
        ),
        name="stack",
    )(*operands)


def swap(value, axis, mask):
    return lax.ppermute(value, axis, [(i, i ^ mask) for i in range(lax.axis_size(axis))])


def after(value, others):
    return lax.optimization_barrier((value, others))[0] if others else value


def on_device(records, taps, pair_sources, pair_counts):
    nblk, chans, time = records.shape
    wins = time // WLEN
    nv = chans // VSTEP
    nwide, nnar = lax.axis_size("wide"), lax.axis_size("narrow")
    half = chans // 2
    me = lax.axis_index("wide").astype(jnp.int32)[None]
    place = lax.axis_index("narrow").astype(jnp.int32)[None]
    ahead = [(i, i + 1) for i in range(nwide - 1)]
    order = list(range(nwide - 1, 0, -1))
    rows, tip = extract(records)
    tip = lax.ppermute(tip, "wide", ahead)
    halo = lax.ppermute(after(records[:, :, time - HALF :], [tip]), "wide", ahead)
    picked, toeplitz, forward = virtual(rows, tip, taps[None], pair_sources, nblk)
    picked = lax.all_to_all(picked, "wide", split_axis=0, concat_axis=0, tiled=True)
    chunks = spectra(records, halo, toeplitz, forward, me, (half, half))
    picked, (near, far) = lax.optimization_barrier((picked, chunks))

    top = nnar // 2
    slots = {0: picked, **{n: swap(picked, "narrow", n) for n in (top, 1) if n}}
    for i, m in enumerate(order):
        waits = []
        if i == len(order) - 2:
            waits = [slots[n] for n in sorted(slots) if n]
        near[m] = swap(after(near[m], waits), "wide", m)
    bit = top
    while bit:
        for n in sorted(slots):
            if n ^ bit not in slots:
                slots[n ^ bit] = swap(after(slots[n], [near[m] for m in order[:3]]), "narrow", bit)
        bit //= 2
    for i, m in enumerate(order):
        waits = [near[order[min(i + 2, nwide - 2)]]] + ([slots[n] for n in sorted(slots) if n] if i >= 2 else [])
        far[m] = swap(after(far[m], waits), "wide", m)
    table = sources([slots[n] for n in range(nnar)], place, wins, nv)
    lag = jnp.asarray(lag_table())
    out = stack(near, table, pair_counts, me, lag, None, 0, half, wins, chans)
    return stack(far, table, pair_counts, me, lag, out, half, half, wins, chans)


def solution(mesh):
    return jax.shard_map(
        on_device,
        mesh=mesh,
        in_specs=(P(None, "narrow", "wide"), P(), P(), P("wide")),
        out_specs=P("wide", None, "narrow", None, None),
        check_vma=False,
    )
```

```python
import math

import jax
import jax.numpy as jnp
import numpy as np
from jax import lax
from jax.experimental import pallas as pl
from jax.experimental.pallas import tpu as pltpu
from jax.sharding import PartitionSpec as P

BLOCK_CHANNELS = 512
VIRTUAL_SOURCES = 32
VSTEP = BLOCK_CHANNELS // VIRTUAL_SOURCES
TAPS = 201
WLEN = 512
HALF = 256
BINS = 128
F_LO = 4
LAG_COUNT = 256
SLOTS = 4
BF = jnp.bfloat16
F32 = jnp.float32
MIB = 1 << 20


def dft_table():
    times = np.arange(WLEN, dtype=np.int32)[:, None]
    bins = (F_LO + np.arange(BINS, dtype=np.int32))[None, :]
    angle = np.mod(times * bins, WLEN).astype(np.float32) * np.float32(2.0 * math.pi / WLEN)
    scale = np.float32(1.0 / math.sqrt(WLEN))
    return np.concatenate([np.cos(angle) * scale, -np.sin(angle) * scale], 1).astype(BF).astype(np.float32)


def lag_table():
    bins = (F_LO + np.arange(BINS, dtype=np.int32))[:, None]
    lags = (np.arange(LAG_COUNT, dtype=np.int32) - LAG_COUNT // 2)[None, :]
    angle = np.mod(bins * lags, WLEN).astype(np.float32) * np.float32(2.0 * math.pi / WLEN)
    scale = np.float32(1.0 / math.sqrt(BINS))
    return np.concatenate([np.cos(angle) * scale, -np.sin(angle) * scale], 0).astype(BF).astype(np.float32)


def dot(a, b):
    return lax.dot_general(a, b, (((1,), (0,)), ((), ())), preferred_element_type=F32)


def build_toeplitz(taps_ref, row, toeplitz):
    row[...] = jnp.zeros_like(row)
    row[:, 128 : 128 + TAPS] = jnp.broadcast_to(taps_ref[...].astype(BF).astype(F32), (8, TAPS))
    bands = jnp.broadcast_to(row[0:1, :], (128, 512))
    bands = pltpu.roll(bands, 0, 1, stride=1, stride_axis=0).astype(BF)
    zero = jnp.zeros((128, 128), BF)
    far, mid, near = [bands[:, at : at + 128] for at in (128, 256, 384)]
    toeplitz[:, :128] = jnp.concatenate([near, mid, far, zero], 0)
    toeplitz[:, 128:] = jnp.concatenate([zero, near, mid, far], 0)


def transform(blocks, wins, chans, toeplitz, table):
    rows = []
    for halo, rec in blocks:
        rows.append(jnp.concatenate([halo, rec[:, :HALF]], 1))
        rows += [rec[:, HALF * (m - 1) : HALF * (m + 1)] for m in range(1, 2 * wins)]
    white = dot(jnp.concatenate(rows, 0), toeplitz).astype(BF)
    pieces = [
        jnp.concatenate([white[2 * w * chans : (2 * w + 1) * chans], white[(2 * w + 1) * chans : (2 * w + 2) * chans]], 1)
        for w in range(len(blocks) * wins)
    ]
    return dot(jnp.concatenate(pieces, 0), table)


def virtual_rows(ref, nv):
    rows = [ref[b, r * VSTEP : (r + 1) * VSTEP, :].astype(F32)[0:1] for b in range(ref.shape[0]) for r in range(nv)]
    return jnp.concatenate(rows, 0).astype(BF)


def block_rows(result, b, nv, wins, count):
    parts = [
        result[w * count + b * nv : w * count + (b + 1) * nv, p * BINS : (p + 1) * BINS]
        for w in range(wins)
        for p in range(2)
    ]
    return jnp.concatenate(parts, 0).astype(BF)


def rows_kernel(rec_ref, rows_ref, near_ref):
    time = rec_ref.shape[2]
    rows = virtual_rows(rec_ref, rec_ref.shape[1] // VSTEP)
    rows_ref[...] = rows
    near_ref[...] = rows[:, time - HALF :]


def extract(records):
    nblk, chans, time = records.shape
    count = nblk * (chans // VSTEP)
    vmem = pl.BlockSpec(memory_space=pltpu.VMEM)
    return pl.pallas_call(
        rows_kernel,
        in_specs=[vmem],
        out_specs=[vmem] * 2,
        out_shape=[jax.ShapeDtypeStruct((count, time), BF), jax.ShapeDtypeStruct((count, HALF), BF)],
        compiler_params=pltpu.CompilerParams(vmem_limit_bytes=8 * MIB),
        cost_estimate=pl.CostEstimate(flops=0, bytes_accessed=records.size, transcendentals=0),
        name="extract",
    )(records)


def virtual_kernel(nblk, pairs_ref, rows_ref, halo_ref, taps_ref, table_ref, *refs):
    picked_ref, toeplitz_ref, forward_ref, row, virt = refs
    count, time = rows_ref.shape
    nv, wins = count // nblk, time // WLEN
    build_toeplitz(taps_ref, row, toeplitz_ref)
    forward_ref[...] = table_ref[...].astype(BF)
    block = (halo_ref[...], rows_ref[...])
    result = transform([block], wins, count, toeplitz_ref[...], forward_ref[...])
    for b in range(nblk):
        virt[b] = block_rows(result, b, nv, wins, count)
    for r in range(nblk):
        for k in range(SLOTS):
            picked_ref[r, k] = virt[pairs_ref[r, k]]


def virtual(rows, halo, taps, pairs, nblk):
    count, time = rows.shape
    size = (time // WLEN) * 2 * (count // nblk)
    smem, vmem = pl.BlockSpec(memory_space=pltpu.SMEM), pl.BlockSpec(memory_space=pltpu.VMEM)
    return pl.pallas_call(
        lambda *refs: virtual_kernel(nblk, *refs),
        in_specs=[smem] + [vmem] * 4,
        out_specs=[vmem] * 3,
        out_shape=[
            jax.ShapeDtypeStruct((nblk, SLOTS, size, BINS), BF),
            jax.ShapeDtypeStruct((WLEN, HALF), BF),
            jax.ShapeDtypeStruct((WLEN, 2 * BINS), BF),
        ],
        scratch_shapes=[pltpu.VMEM((8, 512), F32), pltpu.VMEM((nblk, size, BINS), BF)],
        compiler_params=pltpu.CompilerParams(vmem_limit_bytes=16 * MIB),
        cost_estimate=pl.CostEstimate(flops=10**8, bytes_accessed=rows.size * 8, transcendentals=0),
        name="virtual",
    )(pairs, rows, halo, taps, jnp.asarray(dft_table()))


def spectra_kernel(sizes, me_ref, rec_ref, halo_ref, toeplitz_ref, forward_ref, *refs):
    nblk, chans, time = rec_ref.shape
    wins = time // WLEN
    outs = [refs[nblk * q : nblk * (q + 1)] for q in range(len(sizes))]
    me = me_ref[0]
    per = 4
    for m in range(0, nblk, per):
        blocks = [(halo_ref[me ^ (m + u)], rec_ref[me ^ (m + u)]) for u in range(per)]
        result = transform(blocks, wins, chans, toeplitz_ref[...], forward_ref[...]).astype(BF)
        for u in range(per):
            for w in range(wins):
                for p in range(2):
                    lo = (u * wins + w) * chans
                    for out, size in zip(outs, sizes):
                        row = (w * 2 + p) * size
                        out[m + u][row : row + size] = result[lo : lo + size, p * BINS : (p + 1) * BINS]
                        lo += size


def spectra(records, halo, toeplitz, forward, me, sizes):
    nblk, chans, time = records.shape
    wins = time // WLEN
    shapes = []
    for size in sizes:
        shapes += [(wins * 2 * size, BINS)] * nblk
    smem, vmem = pl.BlockSpec(memory_space=pltpu.SMEM), pl.BlockSpec(memory_space=pltpu.VMEM)
    outs = pl.pallas_call(
        lambda *refs: spectra_kernel(sizes, *refs),
        in_specs=[smem] + [vmem] * 4,
        out_specs=[vmem] * len(shapes),
        out_shape=[jax.ShapeDtypeStruct(shape, BF) for shape in shapes],
        compiler_params=pltpu.CompilerParams(vmem_limit_bytes=24 * MIB),
        cost_estimate=pl.CostEstimate(
            flops=nblk * chans * wins * 3 * 2 * 512 * 256, bytes_accessed=nblk * chans * time * 3, transcendentals=0
        ),
        name="spectra",
    )(me, records, halo, toeplitz, forward)
    return [list(outs[i : i + nblk]) for i in range(0, len(outs), nblk)]


def sources_kernel(nsrc, nnar, wins, nv, place_ref, *refs):
    virts, out_ref, held, turned = refs[:nnar], refs[nnar], refs[nnar + 1], refs[nnar + 2]
    nw = nsrc * wins
    pitch = BINS + 8
    for n in range(nnar):
        held[place_ref[0] ^ n] = virts[n][...]

    def turn(src, carry):
        tiles = [[held[n, src, k].astype(F32) for n in range(nnar)] for k in range(SLOTS)]
        for w in range(wins):
            for p in range(2):
                at = (w * 2 + p) * nv
                tile = jnp.concatenate([tiles[k][n][at : at + nv] for k in range(SLOTS) for n in range(nnar)], 0)
                row = pl.multiple_of((p * nw + src * wins + w) * pitch, 8)
                turned[pl.ds(row, BINS), :] = tile.T
        return carry

    lax.fori_loop(0, nsrc, turn, 0, unroll=4)

    def one(j, carry):
        re = turned[pl.ds(j, nw, stride=pitch), :]
        im = turned[pl.ds(nw * pitch + j, nw, stride=pitch), :]
        top = jnp.concatenate([re, -im], 1)
        low = jnp.concatenate([im, re], 1)
        out_ref[j] = jnp.concatenate([top, low], 0).astype(BF)
        return carry

    lax.fori_loop(0, BINS, one, 0, unroll=8)


def sources(virts, place, wins, nv):
    nnar, nsrc = len(virts), virts[0].shape[0]
    nw = nsrc * wins
    width = SLOTS * nnar * nv
    smem, vmem = pl.BlockSpec(memory_space=pltpu.SMEM), pl.BlockSpec(memory_space=pltpu.VMEM)
    return pl.pallas_call(
        lambda *refs: sources_kernel(nsrc, nnar, wins, nv, *refs),
        in_specs=[smem] + [vmem] * nnar,
        out_specs=vmem,
        out_shape=jax.ShapeDtypeStruct((BINS, 2 * nw, 2 * width), BF),
        scratch_shapes=[
            pltpu.VMEM((nnar,) + virts[0].shape, BF),
            pltpu.VMEM((2 * nw * (BINS + 8), width), F32),
        ],
        compiler_params=pltpu.CompilerParams(vmem_limit_bytes=(10 + 2 * nw * BINS * width * 6 // MIB) * MIB),
        cost_estimate=pl.CostEstimate(flops=10**8, bytes_accessed=8 * nnar * virts[0].size, transcendentals=0),
        name="sources",
    )(place, *virts)


def stack_kernel(nw, wins, start, size, group, count_ref, me_ref, *refs):
    nsrc = nw // wins
    recvs, src_ref, lag_ref = refs[:nsrc], refs[nsrc], refs[nsrc + 1]
    out_ref, wide, turned, cross, held, sems = refs[-6:]
    width = SLOTS * VIRTUAL_SOURCES
    depth = 2 * nw
    pack = src_ref.shape[1] // depth
    full = pack * depth
    pitch, bpitch = size + 8, BINS + 8

    lag = lag_ref[...].astype(BF)
    for m in range(nsrc):
        src = me_ref[0] ^ m
        for w in range(wins):
            for p in range(2):
                row = pl.multiple_of((p * nw + src * wins + w) * pitch, 8)
                at = (w * 2 + p) * size
                wide[pl.ds(row, size), :] = recvs[m][at : at + size].astype(F32)

    shape = (BINS, full)
    own = lax.broadcasted_iota(jnp.int32, shape, 0) % pack == lax.broadcasted_iota(jnp.int32, shape, 1) // depth

    def turn(i, carry):
        flat = wide[pl.ds(i, depth, stride=pitch), :]
        flat = jnp.concatenate([flat] * pack, 0).T
        if pack > 1:
            flat = jnp.where(own, flat, 0.0)
        for c in range(0, full, 128):
            part = flat[:, c : min(c + 128, full)]
            turned[c // 128, pl.ds(pl.multiple_of(i * bpitch, 8), BINS), 0 : part.shape[1]] = part
        return carry

    lax.fori_loop(0, size, turn, 0, unroll=16)
    slot = lax.broadcasted_iota(jnp.int32, (1, 2 * width), 1) % width // VIRTUAL_SOURCES
    scale = jnp.where(slot < count_ref[0], 1.0 / math.sqrt(nw), 0.0).astype(F32)

    def one(j, carry):
        rows = []
        for u in range(pack):
            at = pl.ds(j * pack + u, size, stride=bpitch)
            rows.append(jnp.concatenate([turned[c, at, :] for c in range(turned.shape[0])], 1))
        left = jnp.concatenate(rows, 0)[:, :full].astype(BF)
        value = dot(left, src_ref[j]) * scale
        for u in range(pack):
            at = pl.ds(pl.multiple_of((j * pack + u) * pitch, 8), size)
            for p in range(2):
                cross[p, at, :] = value[u * size : (u + 1) * size, p * width : (p + 1) * width]
        return carry

    lax.fori_loop(0, BINS // pack, one, 0, unroll=32 // pack)

    rows = 4
    copies = []
    for step in range(size // group):
        for q in range(0, group, rows):
            lefts = []
            for u in range(rows):
                at = step * group + q + u
                tiles = [cross[p, pl.ds(at, BINS, stride=pitch), :].astype(BF).T for p in range(2)]
                lefts.append(jnp.concatenate(tiles, 1))
            value = dot(jnp.concatenate(lefts, 0), lag).astype(BF)
            for u in range(rows):
                for k in range(SLOTS):
                    at = u * width + k * VIRTUAL_SOURCES
                    held[step, k, q + u] = value[at : at + VIRTUAL_SOURCES]
        target = out_ref.at[0, :, pl.ds(start + step * group, group)]
        copies.append(pltpu.make_async_copy(held.at[step], target, sems.at[step]))
        copies[-1].start()
    for copy in copies:
        copy.wait()


def stack(recvs, table, count, me, lag, before, start, size, wins, chans):
    nw = wins * len(recvs)
    group = 8
    pack = 2 if 4 * nw <= 128 else 1
    table = table.reshape(BINS // pack, pack * 2 * nw, table.shape[2])
    shape = (1, SLOTS, chans, VIRTUAL_SOURCES, LAG_COUNT)
    smem, vmem = pl.BlockSpec(memory_space=pltpu.SMEM), pl.BlockSpec(memory_space=pltpu.VMEM)
    operands = [count, me, *recvs, table, lag]
    in_specs = [smem, smem] + [vmem] * (len(operands) - 2)
    aliases = {}
    if before is not None:
        operands.append(before)
        in_specs.append(pl.BlockSpec(memory_space=pl.ANY))
        aliases = {len(operands) - 1: 0}
    steps = size // group
    return pl.pallas_call(
        lambda *refs: stack_kernel(nw, wins, start, size, group, *refs),
        in_specs=in_specs,
        out_specs=pl.BlockSpec(memory_space=pl.ANY),
        scratch_shapes=[
            pltpu.VMEM((2 * nw * (size + 8), BINS), F32),
            pltpu.VMEM((-(-2 * nw * pack // 128), size * (BINS + 8), 128), F32),
            pltpu.VMEM((2, BINS * (size + 8), SLOTS * VIRTUAL_SOURCES), F32),
            pltpu.VMEM((steps, SLOTS, group, VIRTUAL_SOURCES, LAG_COUNT), BF),
            pltpu.SemaphoreType.DMA((steps,)),
        ],
        out_shape=jax.ShapeDtypeStruct(shape, BF),
        input_output_aliases=aliases,
        compiler_params=pltpu.CompilerParams(vmem_limit_bytes=32 * MIB),
        cost_estimate=pl.CostEstimate(
            flops=size * 128 * 256 * 256 * 4, bytes_accessed=2 * (table.size + size * 32768), transcendentals=0
        ),
        name="stack",
    )(*operands)


def swap(value, axis, mask):
    return lax.ppermute(value, axis, [(i, i ^ mask) for i in range(lax.axis_size(axis))])


def after(value, others):
    return lax.optimization_barrier((value, others))[0] if others else value


def on_device(records, taps, pair_sources, pair_counts):
    nblk, chans, time = records.shape
    wins = time // WLEN
    nv = chans // VSTEP
    nwide, nnar = lax.axis_size("wide"), lax.axis_size("narrow")
    half = chans // 2
    me = lax.axis_index("wide").astype(jnp.int32)[None]
    place = lax.axis_index("narrow").astype(jnp.int32)[None]
    ahead = [(i, i + 1) for i in range(nwide - 1)]
    order = list(range(nwide - 1, 0, -1))
    rows, tip = extract(records)
    tip = lax.ppermute(tip, "wide", ahead)
    halo = lax.ppermute(after(records[:, :, time - HALF :], [tip]), "wide", ahead)
    picked, toeplitz, forward = virtual(rows, tip, taps[None], pair_sources, nblk)
    picked = lax.all_to_all(picked, "wide", split_axis=0, concat_axis=0, tiled=True)
    chunks = spectra(records, halo, toeplitz, forward, me, (half, half))
    picked, (near, far) = lax.optimization_barrier((picked, chunks))

    top = nnar // 2
    slots = {0: picked, **{n: swap(picked, "narrow", n) for n in (top, 1) if n}}
    for i, m in enumerate(order):
        waits = []
        if i == len(order) - 2:
            waits = [slots[n] for n in sorted(slots) if n]
        near[m] = swap(after(near[m], waits), "wide", m)
    bit = top
    while bit:
        for n in sorted(slots):
            if n ^ bit not in slots:
                slots[n ^ bit] = swap(after(slots[n], [near[m] for m in order[:3]]), "narrow", bit)
        bit //= 2
    for i, m in enumerate(order):
        waits = [near[order[min(i + 2, nwide - 2)]]] + ([slots[n] for n in sorted(slots) if n] if i >= 2 else [])
        far[m] = swap(after(far[m], waits), "wide", m)
    table = sources([slots[n] for n in range(nnar)], place, wins, nv)
    lag = jnp.asarray(lag_table())
    out = stack(near, table, pair_counts, me, lag, None, 0, half, wins, chans)
    return stack(far, table, pair_counts, me, lag, out, half, half, wins, chans)


def solution(mesh):
    return jax.shard_map(
        on_device,
        mesh=mesh,
        in_specs=(P(None, "narrow", "wide"), P(), P(), P("wide")),
        out_specs=P("wide", None, "narrow", None, None),
        check_vma=False,
    )
```

```python
import math

import jax
import jax.numpy as jnp
import numpy as np
from jax import lax
from jax.experimental import pallas as pl
from jax.experimental.pallas import tpu as pltpu
from jax.sharding import PartitionSpec as P

BLOCK_CHANNELS = 512
VIRTUAL_SOURCES = 32
VSTEP = BLOCK_CHANNELS // VIRTUAL_SOURCES
TAPS = 201
WLEN = 512
HALF = 256
BINS = 128
F_LO = 4
LAG_COUNT = 256
SLOTS = 4
BF = jnp.bfloat16
F32 = jnp.float32
MIB = 1 << 20


def dft_table():
    times = np.arange(WLEN, dtype=np.int32)[:, None]
    bins = (F_LO + np.arange(BINS, dtype=np.int32))[None, :]
    angle = np.mod(times * bins, WLEN).astype(np.float32) * np.float32(2.0 * math.pi / WLEN)
    scale = np.float32(1.0 / math.sqrt(WLEN))
    return np.concatenate([np.cos(angle) * scale, -np.sin(angle) * scale], 1).astype(BF).astype(np.float32)


def lag_table():
    bins = (F_LO + np.arange(BINS, dtype=np.int32))[:, None]
    lags = (np.arange(LAG_COUNT, dtype=np.int32) - LAG_COUNT // 2)[None, :]
    angle = np.mod(bins * lags, WLEN).astype(np.float32) * np.float32(2.0 * math.pi / WLEN)
    scale = np.float32(1.0 / math.sqrt(BINS))
    return np.concatenate([np.cos(angle) * scale, -np.sin(angle) * scale], 0).astype(BF).astype(np.float32)


def dot(a, b):
    return lax.dot_general(a, b, (((1,), (0,)), ((), ())), preferred_element_type=F32)


def build_toeplitz(taps_ref, row, toeplitz):
    row[...] = jnp.zeros_like(row)
    row[:, 128 : 128 + TAPS] = jnp.broadcast_to(taps_ref[...].astype(BF).astype(F32), (8, TAPS))
    bands = jnp.broadcast_to(row[0:1, :], (128, 512))
    bands = pltpu.roll(bands, 0, 1, stride=1, stride_axis=0).astype(BF)
    zero = jnp.zeros((128, 128), BF)
    far, mid, near = [bands[:, at : at + 128] for at in (128, 256, 384)]
    toeplitz[:, :128] = jnp.concatenate([near, mid, far, zero], 0)
    toeplitz[:, 128:] = jnp.concatenate([zero, near, mid, far], 0)


def transform(blocks, wins, chans, toeplitz, table):
    rows = []
    for halo, rec in blocks:
        rows.append(jnp.concatenate([halo, rec[:, :HALF]], 1))
        rows += [rec[:, HALF * (m - 1) : HALF * (m + 1)] for m in range(1, 2 * wins)]
    white = dot(jnp.concatenate(rows, 0), toeplitz).astype(BF)
    pieces = [
        jnp.concatenate([white[2 * w * chans : (2 * w + 1) * chans], white[(2 * w + 1) * chans : (2 * w + 2) * chans]], 1)
        for w in range(len(blocks) * wins)
    ]
    return dot(jnp.concatenate(pieces, 0), table)


def virtual_rows(ref, nv):
    rows = [ref[b, r * VSTEP : (r + 1) * VSTEP, :].astype(F32)[0:1] for b in range(ref.shape[0]) for r in range(nv)]
    return jnp.concatenate(rows, 0).astype(BF)


def block_rows(result, b, nv, wins, count):
    parts = [
        result[w * count + b * nv : w * count + (b + 1) * nv, p * BINS : (p + 1) * BINS]
        for w in range(wins)
        for p in range(2)
    ]
    return jnp.concatenate(parts, 0).astype(BF)


def rows_kernel(rec_ref, rows_ref, near_ref):
    time = rec_ref.shape[2]
    rows = virtual_rows(rec_ref, rec_ref.shape[1] // VSTEP)
    rows_ref[...] = rows
    near_ref[...] = rows[:, time - HALF :]


def extract(records):
    nblk, chans, time = records.shape
    count = nblk * (chans // VSTEP)
    vmem = pl.BlockSpec(memory_space=pltpu.VMEM)
    return pl.pallas_call(
        rows_kernel,
        in_specs=[vmem],
        out_specs=[vmem] * 2,
        out_shape=[jax.ShapeDtypeStruct((count, time), BF), jax.ShapeDtypeStruct((count, HALF), BF)],
        compiler_params=pltpu.CompilerParams(vmem_limit_bytes=8 * MIB),
        cost_estimate=pl.CostEstimate(flops=0, bytes_accessed=records.size, transcendentals=0),
        name="extract",
    )(records)


def virtual_kernel(nblk, pairs_ref, rows_ref, halo_ref, taps_ref, table_ref, *refs):
    picked_ref, toeplitz_ref, forward_ref, row, virt = refs
    count, time = rows_ref.shape
    nv, wins = count // nblk, time // WLEN
    build_toeplitz(taps_ref, row, toeplitz_ref)
    forward_ref[...] = table_ref[...].astype(BF)
    block = (halo_ref[...], rows_ref[...])
    result = transform([block], wins, count, toeplitz_ref[...], forward_ref[...])
    for b in range(nblk):
        virt[b] = block_rows(result, b, nv, wins, count)
    for r in range(nblk):
        for k in range(SLOTS):
            picked_ref[r, k] = virt[pairs_ref[r, k]]


def virtual(rows, halo, taps, pairs, nblk):
    count, time = rows.shape
    size = (time // WLEN) * 2 * (count // nblk)
    smem, vmem = pl.BlockSpec(memory_space=pltpu.SMEM), pl.BlockSpec(memory_space=pltpu.VMEM)
    return pl.pallas_call(
        lambda *refs: virtual_kernel(nblk, *refs),
        in_specs=[smem] + [vmem] * 4,
        out_specs=[vmem] * 3,
        out_shape=[
            jax.ShapeDtypeStruct((nblk, SLOTS, size, BINS), BF),
            jax.ShapeDtypeStruct((WLEN, HALF), BF),
            jax.ShapeDtypeStruct((WLEN, 2 * BINS), BF),
        ],
        scratch_shapes=[pltpu.VMEM((8, 512), F32), pltpu.VMEM((nblk, size, BINS), BF)],
        compiler_params=pltpu.CompilerParams(vmem_limit_bytes=16 * MIB),
        cost_estimate=pl.CostEstimate(flops=10**8, bytes_accessed=rows.size * 8, transcendentals=0),
        name="virtual",
    )(pairs, rows, halo, taps, jnp.asarray(dft_table()))


def spectra_kernel(sizes, me_ref, rec_ref, halo_ref, toeplitz_ref, forward_ref, *refs):
    nblk, chans, time = rec_ref.shape
    wins = time // WLEN
    outs = [refs[nblk * q : nblk * (q + 1)] for q in range(len(sizes))]
    me = me_ref[0]
    per = 4
    for m in range(0, nblk, per):
        blocks = [(halo_ref[me ^ (m + u)], rec_ref[me ^ (m + u)]) for u in range(per)]
        result = transform(blocks, wins, chans, toeplitz_ref[...], forward_ref[...]).astype(BF)
        for u in range(per):
            for w in range(wins):
                for p in range(2):
                    lo = (u * wins + w) * chans
                    for out, size in zip(outs, sizes):
                        row = (w * 2 + p) * size
                        out[m + u][row : row + size] = result[lo : lo + size, p * BINS : (p + 1) * BINS]
                        lo += size


def spectra(records, halo, toeplitz, forward, me, sizes):
    nblk, chans, time = records.shape
    wins = time // WLEN
    shapes = []
    for size in sizes:
        shapes += [(wins * 2 * size, BINS)] * nblk
    smem, vmem = pl.BlockSpec(memory_space=pltpu.SMEM), pl.BlockSpec(memory_space=pltpu.VMEM)
    outs = pl.pallas_call(
        lambda *refs: spectra_kernel(sizes, *refs),
        in_specs=[smem] + [vmem] * 4,
        out_specs=[vmem] * len(shapes),
        out_shape=[jax.ShapeDtypeStruct(shape, BF) for shape in shapes],
        compiler_params=pltpu.CompilerParams(vmem_limit_bytes=24 * MIB),
        cost_estimate=pl.CostEstimate(
            flops=nblk * chans * wins * 3 * 2 * 512 * 256, bytes_accessed=nblk * chans * time * 3, transcendentals=0
        ),
        name="spectra",
    )(me, records, halo, toeplitz, forward)
    return [list(outs[i : i + nblk]) for i in range(0, len(outs), nblk)]


def sources_kernel(nsrc, nnar, wins, nv, place_ref, *refs):
    virts, out_ref, held, turned = refs[:nnar], refs[nnar], refs[nnar + 1], refs[nnar + 2]
    nw = nsrc * wins
    pitch = BINS + 8
    for n in range(nnar):
        held[place_ref[0] ^ n] = virts[n][...]

    def turn(src, carry):
        tiles = [[held[n, src, k].astype(F32) for n in range(nnar)] for k in range(SLOTS)]
        for w in range(wins):
            for p in range(2):
                at = (w * 2 + p) * nv
                tile = jnp.concatenate([tiles[k][n][at : at + nv] for k in range(SLOTS) for n in range(nnar)], 0)
                row = pl.multiple_of((p * nw + src * wins + w) * pitch, 8)
                turned[pl.ds(row, BINS), :] = tile.T
        return carry

    lax.fori_loop(0, nsrc, turn, 0, unroll=4)

    def one(j, carry):
        re = turned[pl.ds(j, nw, stride=pitch), :]
        im = turned[pl.ds(nw * pitch + j, nw, stride=pitch), :]
        top = jnp.concatenate([re, -im], 1)
        low = jnp.concatenate([im, re], 1)
        out_ref[j] = jnp.concatenate([top, low], 0).astype(BF)
        return carry

    lax.fori_loop(0, BINS, one, 0, unroll=32)


def sources(virts, place, wins, nv):
    nnar, nsrc = len(virts), virts[0].shape[0]
    nw = nsrc * wins
    width = SLOTS * nnar * nv
    smem, vmem = pl.BlockSpec(memory_space=pltpu.SMEM), pl.BlockSpec(memory_space=pltpu.VMEM)
    return pl.pallas_call(
        lambda *refs: sources_kernel(nsrc, nnar, wins, nv, *refs),
        in_specs=[smem] + [vmem] * nnar,
        out_specs=vmem,
        out_shape=jax.ShapeDtypeStruct((BINS, 2 * nw, 2 * width), BF),
        scratch_shapes=[
            pltpu.VMEM((nnar,) + virts[0].shape, BF),
            pltpu.VMEM((2 * nw * (BINS + 8), width), F32),
        ],
        compiler_params=pltpu.CompilerParams(vmem_limit_bytes=(10 + 2 * nw * BINS * width * 6 // MIB) * MIB),
        cost_estimate=pl.CostEstimate(flops=10**8, bytes_accessed=8 * nnar * virts[0].size, transcendentals=0),
        name="sources",
    )(place, *virts)


def stack_kernel(nw, wins, start, size, group, count_ref, me_ref, *refs):
    nsrc = nw // wins
    recvs, src_ref, lag_ref = refs[:nsrc], refs[nsrc], refs[nsrc + 1]
    out_ref, wide, turned, cross, held, sems = refs[-6:]
    width = SLOTS * VIRTUAL_SOURCES
    depth = 2 * nw
    pack = src_ref.shape[1] // depth
    full = pack * depth
    pitch, bpitch = size + 8, BINS + 8

    lag = lag_ref[...].astype(BF)
    for m in range(nsrc):
        src = me_ref[0] ^ m
        for w in range(wins):
            for p in range(2):
                row = pl.multiple_of((p * nw + src * wins + w) * pitch, 8)
                at = (w * 2 + p) * size
                wide[pl.ds(row, size), :] = recvs[m][at : at + size].astype(F32)

    shape = (BINS, full)
    own = lax.broadcasted_iota(jnp.int32, shape, 0) % pack == lax.broadcasted_iota(jnp.int32, shape, 1) // depth

    def turn(i, carry):
        flat = wide[pl.ds(i, depth, stride=pitch), :]
        flat = jnp.concatenate([flat] * pack, 0).T
        if pack > 1:
            flat = jnp.where(own, flat, 0.0)
        for c in range(0, full, 128):
            part = flat[:, c : min(c + 128, full)]
            turned[c // 128, pl.ds(pl.multiple_of(i * bpitch, 8), BINS), 0 : part.shape[1]] = part
        return carry

    lax.fori_loop(0, size, turn, 0, unroll=16)
    slot = lax.broadcasted_iota(jnp.int32, (1, 2 * width), 1) % width // VIRTUAL_SOURCES
    scale = jnp.where(slot < count_ref[0], 1.0 / math.sqrt(nw), 0.0).astype(F32)

    def one(j, carry):
        rows = []
        for u in range(pack):
            at = pl.ds(j * pack + u, size, stride=bpitch)
            rows.append(jnp.concatenate([turned[c, at, :] for c in range(turned.shape[0])], 1))
        left = jnp.concatenate(rows, 0)[:, :full].astype(BF)
        value = dot(left, src_ref[j]) * scale
        for u in range(pack):
            at = pl.ds(pl.multiple_of((j * pack + u) * pitch, 8), size)
            for p in range(2):
                cross[p, at, :] = value[u * size : (u + 1) * size, p * width : (p + 1) * width]
        return carry

    lax.fori_loop(0, BINS // pack, one, 0, unroll=64 // pack)

    rows = 4
    copies = []
    for step in range(size // group):
        for q in range(0, group, rows):
            lefts = []
            for u in range(rows):
                at = step * group + q + u
                tiles = [cross[p, pl.ds(at, BINS, stride=pitch), :].astype(BF).T for p in range(2)]
                lefts.append(jnp.concatenate(tiles, 1))
            value = dot(jnp.concatenate(lefts, 0), lag).astype(BF)
            for u in range(rows):
                for k in range(SLOTS):
                    at = u * width + k * VIRTUAL_SOURCES
                    held[step, k, q + u] = value[at : at + VIRTUAL_SOURCES]
        target = out_ref.at[0, :, pl.ds(start + step * group, group)]
        copies.append(pltpu.make_async_copy(held.at[step], target, sems.at[step]))
        copies[-1].start()
    for copy in copies:
        copy.wait()


def stack(recvs, table, count, me, lag, before, start, size, wins, chans):
    nw = wins * len(recvs)
    group = 8
    pack = 2 if 4 * nw <= 128 else 1
    table = table.reshape(BINS // pack, pack * 2 * nw, table.shape[2])
    shape = (1, SLOTS, chans, VIRTUAL_SOURCES, LAG_COUNT)
    smem, vmem = pl.BlockSpec(memory_space=pltpu.SMEM), pl.BlockSpec(memory_space=pltpu.VMEM)
    operands = [count, me, *recvs, table, lag]
    in_specs = [smem, smem] + [vmem] * (len(operands) - 2)
    aliases = {}
    if before is not None:
        operands.append(before)
        in_specs.append(pl.BlockSpec(memory_space=pl.ANY))
        aliases = {len(operands) - 1: 0}
    steps = size // group
    return pl.pallas_call(
        lambda *refs: stack_kernel(nw, wins, start, size, group, *refs),
        in_specs=in_specs,
        out_specs=pl.BlockSpec(memory_space=pl.ANY),
        scratch_shapes=[
            pltpu.VMEM((2 * nw * (size + 8), BINS), F32),
            pltpu.VMEM((-(-2 * nw * pack // 128), size * (BINS + 8), 128), F32),
            pltpu.VMEM((2, BINS * (size + 8), SLOTS * VIRTUAL_SOURCES), F32),
            pltpu.VMEM((steps, SLOTS, group, VIRTUAL_SOURCES, LAG_COUNT), BF),
            pltpu.SemaphoreType.DMA((steps,)),
        ],
        out_shape=jax.ShapeDtypeStruct(shape, BF),
        input_output_aliases=aliases,
        compiler_params=pltpu.CompilerParams(vmem_limit_bytes=32 * MIB),
        cost_estimate=pl.CostEstimate(
            flops=size * 128 * 256 * 256 * 4, bytes_accessed=2 * (table.size + size * 32768), transcendentals=0
        ),
        name="stack",
    )(*operands)


def swap(value, axis, mask):
    return lax.ppermute(value, axis, [(i, i ^ mask) for i in range(lax.axis_size(axis))])


def after(value, others):
    return lax.optimization_barrier((value, others))[0] if others else value


def on_device(records, taps, pair_sources, pair_counts):
    nblk, chans, time = records.shape
    wins = time // WLEN
    nv = chans // VSTEP
    nwide, nnar = lax.axis_size("wide"), lax.axis_size("narrow")
    half = chans // 2
    me = lax.axis_index("wide").astype(jnp.int32)[None]
    place = lax.axis_index("narrow").astype(jnp.int32)[None]
    ahead = [(i, i + 1) for i in range(nwide - 1)]
    order = list(range(nwide - 1, 0, -1))
    rows, tip = extract(records)
    tip = lax.ppermute(tip, "wide", ahead)
    halo = lax.ppermute(after(records[:, :, time - HALF :], [tip]), "wide", ahead)
    picked, toeplitz, forward = virtual(rows, tip, taps[None], pair_sources, nblk)
    picked = lax.all_to_all(picked, "wide", split_axis=0, concat_axis=0, tiled=True)
    chunks = spectra(records, halo, toeplitz, forward, me, (half, half))
    picked, (near, far) = lax.optimization_barrier((picked, chunks))

    top = nnar // 2
    slots = {0: picked, **{n: swap(picked, "narrow", n) for n in (top, 1) if n}}
    for i, m in enumerate(order):
        waits = []
        if i == len(order) - 2:
            waits = [slots[n] for n in sorted(slots) if n]
        near[m] = swap(after(near[m], waits), "wide", m)
    bit = top
    while bit:
        for n in sorted(slots):
            if n ^ bit not in slots:
                slots[n ^ bit] = swap(after(slots[n], [near[m] for m in order[:3]]), "narrow", bit)
        bit //= 2
    for i, m in enumerate(order):
        waits = [near[order[min(i + 2, nwide - 2)]]] + ([slots[n] for n in sorted(slots) if n] if i >= 2 else [])
        far[m] = swap(after(far[m], waits), "wide", m)
    table = sources([slots[n] for n in range(nnar)], place, wins, nv)
    lag = jnp.asarray(lag_table())
    out = stack(near, table, pair_counts, me, lag, None, 0, half, wins, chans)
    return stack(far, table, pair_counts, me, lag, out, half, half, wins, chans)


def solution(mesh):
    return jax.shard_map(
        on_device,
        mesh=mesh,
        in_specs=(P(None, "narrow", "wide"), P(), P(), P("wide")),
        out_specs=P("wide", None, "narrow", None, None),
        check_vma=False,
    )
```
